32 devices in a mesh: rep: 4 (over x, core), shard: 8 (over z, y).
Axes of the slice: x: 2, y: 2, z: 4, core: 2. Of those that a mesh axis runs over, the one named last changes fastest.
Arguments:
- tokens: bfloat16 [16384, 2048], P(('rep', 'shard')), may hold values from -6 to 6
- cotangent: bfloat16 [16384, 2048], P(('rep', 'shard')), may hold values from -6 to 6
- lengths: int32 [64], replicated, may hold values from 128 to 384, as said below
- order: int32 [64], P(('rep', 'shard')), may hold values from 0 to 63, as said below
- mask: int32 [16384], P(('rep', 'shard')), may hold values from 0 to 1, as said below
- in_weight: float32 [2048, 8512], P('shard'), may hold values from -0.125 to 0.125
- out_weight: float32 [4096, 2048], P('shard'), may hold values from -0.09375 to 0.09375
- conv_weight: float32 [4, 4352], replicated, may hold values from -3 to 3
- conv_bias: float32 [4352], replicated, may hold values from -3 to 3
- dt_bias: float32 [64], replicated, may hold values from -7 to -2
- a_log: float32 [64], replicated, may hold values from -1 to 2.5
- skip_gain: float32 [64], replicated, may hold values from 0.5 to 2
- gain_outer: float32 [2048], replicated, may hold values from 0.5 to 1.5
- gain_inner: float32 [4096], replicated, may hold values from 0.5 to 1.5
Outputs:
- layer_out: bfloat16 [16384, 2048], P(('rep', 'shard'))
- grad_tokens: float32 [16384, 2048], P(('rep', 'shard'))
- grad_in_weight: float32 [2048, 8512], P('shard')
- grad_out_weight: float32 [4096, 2048], P('shard')
- grad_conv_weight: float32 [4, 4352], replicated
- grad_conv_bias: float32 [4352], replicated
- grad_dt_bias: float32 [64], replicated
- grad_a_log: float32 [64], replicated
- grad_skip_gain: float32 [64], replicated
- grad_gain_outer: float32 [2048], replicated
- grad_gain_inner: float32 [4096], replicated
The draws below stay inside these ranges and needn't reach their ends.
Inputs may be any that keep to these rules, and one draw needn't show every extreme that they name: Each block of 512 rows holds 2 sequences whose lengths sum to at most 512. `order`: A permutation of the sequences. `mask`: 1 exactly on the rows that a block's sequences fill, 0 on the rest of the block.
All inputs are finite; a program needn't handle non-finite values.
Results may differ from the reference program's by a relative error of at most 0.012.
Values may be sent and summed in bfloat16 or wider, within the bound.
No kernel may reach another device: no remote copies, remote signals or barrier semaphores. Data moves between devices by JAX's collectives and lax.ppermute only.
A program may use at most 384 MiB of HBM per device.

```python
import jax
import jax.numpy as jnp
from jax import lax

D = 2048
DIN = 4096
P_SIZE = 64
N = 128
KCONV = 4
Q = 256
SEQ_DEV = 2
TOK_DEV = 512
H = 64
CONVCH = 4352
NPROJ = 8512
TOKENS = 16384
NSEQ = 64


def layout(key):
    blocks = NSEQ // SEQ_DEV
    arrival = jax.random.permutation(jax.random.fold_in(key, 11), NSEQ).astype(jnp.int32)
    first_len = jax.random.randint(jax.random.fold_in(key, 12), (blocks,), TOK_DEV // 4, TOK_DEV // 2 + 1).astype(jnp.int32)
    padding = jax.random.randint(jax.random.fold_in(key, 13), (blocks,), 0, TOK_DEV // 8 + 1).astype(jnp.int32)
    fullest = jax.random.randint(jax.random.fold_in(key, 14), (), 0, blocks).astype(jnp.int32)
    block_index = jnp.arange(blocks, dtype=jnp.int32)
    first_len = jnp.where(block_index == fullest, TOK_DEV // 4, first_len).astype(jnp.int32)
    padding = jnp.where(block_index == fullest, 0, padding).astype(jnp.int32)
    used = TOK_DEV - padding
    slot_len = jnp.stack([first_len, used - first_len], axis=1).reshape(NSEQ)
    lengths = jnp.zeros((NSEQ,), jnp.int32).at[arrival].set(slot_len)
    return (arrival, lengths, used)


def draw_lengths(key, part):
    arrival, lengths, used = layout(key)
    return lengths


def draw_order(key, part):
    arrival, lengths, used = layout(key)
    return arrival


def draw_mask(key, part):
    arrival, lengths, used = layout(key)
    row_index = jnp.arange(TOK_DEV, dtype=jnp.int32)
    return (row_index[None, :] < used[:, None]).astype(jnp.int32).reshape(NSEQ // SEQ_DEV * TOK_DEV)


def steps_of(stream_key, extent, split, smallest, largest):
    loudness, own = 1.0, jax.random.fold_in(stream_key, 6)
    for position, blocks in split:
        steps = jnp.exp(jax.random.uniform(jax.random.fold_in(own, position), (blocks,), jnp.float32, smallest / len(split), largest / len(split)))
        loudness = loudness * jnp.repeat(steps, extent[position] // blocks).reshape([-1 if axis == position else 1 for axis in range(len(extent))])
    return loudness


def centred(key, extent, width, reach, shards=(), kind=jnp.bfloat16):
    array = width * jax.random.normal(key, extent, jnp.float32)
    if shards:
        array = array * steps_of(key, extent, shards, -0.22, 0.18)
    return jnp.clip(array, -reach, reach).astype(kind)


def setup_inputs(seed: int = 0) -> dict:
    keys = jax.random.split(jax.random.key(seed), 15)
    tokens = centred(keys[0], (TOKENS, D), 1.0, 6.0, ((0, 32),))
    cotangent = centred(keys[1], (TOKENS, D), 1.0, 6.0, ((0, 32),))
    lengths = draw_lengths(jax.random.fold_in(keys[14], 71), 0)
    order = draw_order(jax.random.fold_in(keys[14], 71), 0)
    mask = draw_mask(jax.random.fold_in(keys[14], 71), 0)
    in_weight = centred(keys[5], (D, NPROJ), D ** -0.5, 0.125, ((0, 8),), jnp.float32)
    out_weight = centred(keys[6], (DIN, D), DIN ** -0.5, 0.09375, ((0, 8),), jnp.float32)
    conv_weight = centred(keys[7], (KCONV, CONVCH), KCONV ** -0.5, 3.0, (), jnp.float32)
    conv_bias = centred(keys[8], (CONVCH,), 0.5, 3.0, (), jnp.float32)
    dt_bias = jnp.clip(jax.random.uniform(keys[9], (H,), jnp.float32, -7.0, -2.0), -7.0, -2.0)
    a_log = jnp.clip(jax.random.uniform(keys[10], (H,), jnp.float32, -1.0, 2.5), -1.0, 2.5)
    skip_gain = jnp.clip(jax.random.uniform(keys[11], (H,), jnp.float32, 0.5, 2.0), 0.5, 2.0)
    gain_outer = jnp.clip(1.0 + 0.1 * jax.random.normal(keys[12], (D,), jnp.float32), 0.5, 1.5)
    gain_inner = jnp.clip(1.0 + 0.1 * jax.random.normal(keys[13], (DIN,), jnp.float32), 0.5, 1.5)
    return {"tokens": tokens, "cotangent": cotangent, "lengths": lengths, "order": order, "mask": mask, "in_weight": in_weight, "out_weight": out_weight, "conv_weight": conv_weight, "conv_bias": conv_bias, "dt_bias": dt_bias, "a_log": a_log, "skip_gain": skip_gain, "gain_outer": gain_outer, "gain_inner": gain_inner}


EPSILON = 1e-05
HIGHEST = lax.Precision.HIGHEST

@jax.custom_vjp
def low(v):
    return lax.optimization_barrier(v.astype(jnp.bfloat16)).astype(jnp.float32)

@jax.custom_vjp
def low_back(v):
    return v

def low_keep(v):
    return (low(v), None)

def low_pass(kept, grad):
    return (grad,)

def back_keep(v):
    return (v, None)

def back_low(kept, grad):
    return (low(grad),)
low.defvjp(low_keep, low_pass)
low_back.defvjp(back_keep, back_low)

def segment_table(order_blocks, lengths, total_rows):
    catalog = jnp.arange(lengths.shape[0], dtype=jnp.int32)
    picked = lax.optimization_barrier(jnp.sum(jnp.where(order_blocks[:, :, None] == catalog[None, None, :], lengths[None, None, :], 0), axis=2))
    bounds = jnp.cumsum(picked, axis=1)
    row_index = jnp.arange(total_rows, dtype=jnp.int32)
    return lax.optimization_barrier(jnp.sum((row_index[None, :, None] >= bounds[:, None, :]).astype(jnp.int32), axis=2))

def convolve(channels, segment, conv_weight, conv_bias):
    total_rows = channels.shape[0]
    result = conv_bias[None, :] + conv_weight[KCONV - 1][None, :] * channels
    for back_step in range(1, KCONV):
        shifted = jnp.concatenate([jnp.zeros((back_step, channels.shape[1]), jnp.float32), channels[:total_rows - back_step]], 0)
        earlier = jnp.concatenate([jnp.full((back_step,), -1, jnp.int32), segment[:total_rows - back_step]])
        linked = (earlier == segment).astype(jnp.float32)
        result = result + conv_weight[KCONV - 1 - back_step][None, :] * shifted * linked[:, None]
    return jax.nn.silu(result)

def block_step(state, pieces):
    values, bmat, cmat, step_size, decay, segment, prev_segment = pieces
    cumul = jnp.cumsum(decay, axis=0)
    final = cumul[-1]
    size_q = segment.shape[0]
    row_index = jnp.arange(size_q, dtype=jnp.int32)
    allowed = (segment[:, None] == segment[None, :]) & (row_index[:, None] >= row_index[None, :])
    spread = cumul.T[:, :, None] - cumul.T[:, None, :]
    weights = jnp.exp(jnp.where(allowed[None], spread, -1e+30))
    scores = jnp.dot(cmat, bmat.T, precision=HIGHEST)
    mixing = weights * scores[None] * step_size.T[:, None, :]
    output = jnp.einsum('hij,jhp->ihp', mixing, values, precision=HIGHEST)
    entering = jnp.exp(cumul) * (segment == prev_segment).astype(jnp.float32)[:, None]
    output = output + jnp.einsum('in,hpn->ihp', cmat, state, precision=HIGHEST) * entering[:, :, None]
    tail_keep = (segment == segment[-1])[:, None]
    tail = jnp.exp(jnp.where(tail_keep, final[None, :] - cumul, -1e+30)) * step_size
    carried = jnp.exp(final) * (segment[-1] == prev_segment).astype(jnp.float32)
    state = state * carried[:, None, None] + jnp.einsum('jh,jhp,jn->hpn', tail, values, bmat, precision=HIGHEST)
    return (state, output)

def mixer(projected, segment, conv_weight, conv_bias, dt_bias, a_log, skip_gain, gain_inner):
    total_rows = projected.shape[0]
    gate_part = projected[:, :DIN]
    conv_out = convolve(projected[:, DIN:2 * DIN + 2 * N], segment, conv_weight, conv_bias)
    dt_raw = projected[:, 2 * DIN + 2 * N:]
    step_size = jax.nn.softplus(dt_raw + dt_bias[None, :])
    decay = -jnp.exp(a_log)[None, :] * step_size
    values = conv_out[:, :DIN].reshape(total_rows, H, P_SIZE)
    bmat = conv_out[:, DIN:DIN + N]
    cmat = conv_out[:, DIN + N:]
    blocks = total_rows // Q
    prev_segment = jnp.concatenate([jnp.full((1,), -1, jnp.int32), segment[Q - 1:total_rows - 1:Q]])
    pieces = (values.reshape(blocks, Q, H, P_SIZE), bmat.reshape(blocks, Q, N), cmat.reshape(blocks, Q, N), step_size.reshape(blocks, Q, H), decay.reshape(blocks, Q, H), segment.reshape(blocks, Q), prev_segment)
    _, outputs = lax.scan(jax.checkpoint(block_step), jnp.zeros((H, P_SIZE, N), jnp.float32), pieces)
    scanned = outputs.reshape(total_rows, H, P_SIZE) + skip_gain[None, :, None] * values
    gated = scanned.reshape(total_rows, DIN) * jax.nn.silu(gate_part)
    return gated * lax.rsqrt(lax.optimization_barrier(jnp.mean(gated * gated, axis=1, keepdims=True)) + EPSILON) * gain_inner[None, :]

def reference(tokens, cotangent, lengths, order, mask, in_weight, out_weight, conv_weight, conv_bias, dt_bias, a_log, skip_gain, gain_outer, gain_inner):
    blocks = tokens.shape[0] // TOK_DEV
    segments = segment_table(order.reshape(blocks, SEQ_DEV), lengths, TOK_DEV)
    inputs = tokens.astype(jnp.float32).reshape(blocks, TOK_DEV, D)
    keep = mask.astype(jnp.float32).reshape(blocks, TOK_DEV)

    def whole(params, activ):
        w_in, w_out, c_weight, c_bias, d_bias, decay_log, skip, g_outer, g_inner = params
        w_in16 = low(w_in)
        w_out16 = low(w_out)

        def one_block(items):
            rows, segment, keep_rows = items
            normed = low(rows * lax.rsqrt(lax.optimization_barrier(jnp.mean(rows * rows, axis=1, keepdims=True)) + EPSILON) * g_outer[None, :])
            projected = low_back(low(jnp.dot(normed, w_in16, precision=HIGHEST)))
            inner = low(mixer(projected, segment, c_weight, c_bias, d_bias, decay_log, skip, g_inner))
            branch = jnp.dot(inner, w_out16, precision=HIGHEST)
            return keep_rows[:, None] * (rows + branch)
        return lax.map(jax.checkpoint(one_block), (activ, segments, keep))
    params = (in_weight, out_weight, conv_weight, conv_bias, dt_bias, a_log, skip_gain, gain_outer, gain_inner)
    result, pullback = jax.vjp(whole, params, inputs)
    grad_params, grad_inputs = pullback(cotangent.astype(jnp.float32).reshape(blocks, TOK_DEV, D))
    g_in, g_out, g_cw, g_cb, g_db, g_al, g_sk, g_go, g_gi = grad_params
    return (result.reshape(tokens.shape[0], D).astype(jnp.bfloat16), grad_inputs.reshape(tokens.shape[0], D), g_in, g_out, g_cw, g_cb, g_db, g_al, g_sk, g_go, g_gi)
```

```python
import functools

import jax
import jax.numpy as jnp
from jax import lax
from jax.experimental import pallas as pl
from jax.experimental.pallas import tpu as pltpu
from jax.sharding import PartitionSpec as P

D = 2048
DIN = 4096
P_SIZE = 64
N = 128
Q = 256
H = 64
CONVCH = DIN + 2 * N
EPSILON = 1e-05
LOG2E = 1.4426950408889634
LANES = 128
TOK = 512
HIGHEST = lax.Precision.HIGHEST
BF = jnp.bfloat16
F32 = jnp.float32
NT = (((1,), (1,)), ((), ()))
TN = (((0,), (0,)), ((), ()))
VMEM_LIMIT = 48 * 1024 * 1024
RING = (0, 2, 4, 6, 7, 5, 3, 1)


def mm(a, b):
    return jnp.dot(a, b, preferred_element_type=F32)


def mm_nt(a, b):
    return lax.dot_general(a, b, NT, preferred_element_type=F32)


def iota(shape, dim):
    return lax.broadcasted_iota(jnp.int32, shape, dim)


def start_of(rows, b1, b2):
    return jnp.where(rows >= b2, b2, jnp.where(rows >= b1, b1, 0))


def sigmoid(v):
    return 0.5 * jnp.tanh(0.5 * v) + 0.5


def conv_pre(x, taps, bias, lk):
    pre = bias + taps[3] * x
    for k in range(1, 4):
        pre = pre + taps[3 - k] * (pltpu.roll(x, k, 0) * lk[k - 1])
    return pre


def taps_of(cw_ref, lanes):
    return [cw_ref[k : k + 1, lanes] for k in range(4)], cw_ref[4:5, lanes]


def prepare(b1, b2, bc_ref, dt_ref, cwb_ref, hp_ref, sel_ref, lk, score, bmat, cmat, btrans, ctrans,
            dts, sig, cum, cumt, ecol, tcol, transposed):
    rows = iota((TOK, LANES), 0)
    pos = rows - start_of(rows, b1, b2)
    for k in range(1, 4):
        lk[k - 1] = (pos >= k).astype(F32)
    links = [lk[0], lk[1], lk[2]]
    for half, keep in ((0, bmat), (1, cmat)):
        lanes = slice(half * LANES, (half + 1) * LANES)
        taps, bias = taps_of(cwb_ref, lanes)
        pre = conv_pre(bc_ref[:, lanes].astype(F32), taps, bias, links)
        act = pre * sigmoid(pre)
        keep[...] = act.astype(BF)
        if half == 0:
            btrans[...] = act[:Q].T.astype(BF)
        elif ctrans is not None:
            ctrans[...] = act[Q:].T.astype(BF)
    for c in range(2):
        part = slice(c * Q, (c + 1) * Q)
        if transposed:
            s = mm_nt(bmat[part, :], cmat[part, :])
        else:
            s = mm_nt(cmat[part, :], bmat[part, :])
        score[c] = jnp.where(allowed(c, b1, b2, transposed), s, 0.0)
    raw = mm(dt_ref[...], sel_ref[...]) + hp_ref[0:1, :]
    step = jnp.maximum(raw, 0.0) + jnp.log1p(jnp.exp(-jnp.abs(raw)))
    dts[...] = step
    if sig is not None:
        sig[...] = sigmoid(raw)
    decay = step * (hp_ref[1:2, :] * LOG2E)
    lower = (iota((Q, Q), 0) >= iota((Q, Q), 1)).astype(F32)
    for c in range(2):
        part = slice(c * Q, (c + 1) * Q)
        total = jnp.dot(lower, decay[part], precision=HIGHEST, preferred_element_type=F32)
        cum[part, :] = total
        cumt[:, part] = total.T
        if c == 0:
            last = start_of(Q - 1, b1, b2)
            tcol[...] = jnp.where(rows[:Q] >= last, jnp.exp2(total[Q - 1 : Q, :] - total), 0.0)
        else:
            linked = start_of(rows[Q:], b1, b2) <= Q - 1
            ecol[...] = jnp.where(linked, jnp.exp2(total), 0.0)


def allowed(c, b1, b2, transposed):
    late = iota((Q, Q), 1 if transposed else 0) + c * Q
    early = iota((Q, Q), 0 if transposed else 1) + c * Q
    return (early <= late) & (early >= start_of(late, b1, b2))


def pair(ref_value, first):
    return jnp.where(first, ref_value[:, 0:1], ref_value[:, 1:2])


def fwd_kernel(bnd, xs_ref, bc_ref, dt_ref, cwx_ref, cwb_ref, hp_ref, sel_ref, out_ref,
               lk, score, bmat, cmat, btrans, dts, cum, cumt, ecol, tcol):
    b, t = pl.program_id(0), pl.program_id(1)

    @pl.when(t == 0)
    def _():
        prepare(bnd[b, 0], bnd[b, 1], bc_ref, dt_ref, cwb_ref, hp_ref, sel_ref, lk, score, bmat, cmat,
                btrans, None, dts, None, cum, cumt, ecol, tcol, False)

    turn = lax.rem(LANES - 2 * t, LANES)
    taps, bias = taps_of(cwx_ref, slice(None))
    pre = conv_pre(xs_ref[...].astype(F32), taps, bias, [lk[0], lk[1], lk[2]])
    x = pre * sigmoid(pre)
    first = iota((TOK, LANES), 1) < P_SIZE
    xt = x * pair(pltpu.roll(dts[...], turn, 1), first)
    xt16 = xt.astype(BF)
    mine = [jnp.where(first, xt16, jnp.zeros_like(xt16)), jnp.where(first, jnp.zeros_like(xt16), xt16)]
    cumr = pltpu.roll(cum[...], turn, 1)
    half = Q // 2
    outs = []
    for c in range(2):
        o = c * Q
        top = bottom = None
        for h in range(2):
            row = cumt[pl.ds(2 * t + h, 1), o : o + Q]
            col = cumr[o : o + Q, h : h + 1]
            w = jnp.exp2(jnp.minimum(col[:half] - row[:, :half], 0.0)) * score[c, :half, :half]
            y = mm(w.astype(BF), mine[h][o : o + half])
            top = y if top is None else top + y
            w = jnp.exp2(jnp.minimum(col[half:] - row, 0.0)) * score[c, half:, :]
            y = mm(w.astype(BF), mine[h][o : o + Q])
            bottom = y if bottom is None else bottom + y
        outs.append(jnp.concatenate([top, bottom], 0))
    tx = pair(pltpu.roll(tcol[...], turn, 1), first[:Q])
    ex = pair(pltpu.roll(ecol[...], turn, 1), first[:Q])
    state = mm(btrans[...], (tx * xt[:Q]).astype(BF))
    outs[1] = outs[1] + mm(cmat[Q:, :], state.astype(BF)) * ex
    skip = cwx_ref[5:6, :]
    out_ref[...] = jnp.concatenate(outs, 0) + skip * x


def bwd_kernel(bnd, xs_ref, bc_ref, dt_ref, cwx_ref, cwb_ref, hp_ref, sel_ref, scan_ref, dscan_ref,
               out_ref, dcw_ref, dhp_ref,
               lk, score, bmat, cmat, btrans, ctrans, dts, sig, cum, cumt, ecol, tcol, dscore, rsum, rsum3, dball, dcall):
    b, t = pl.program_id(0), pl.program_id(1)
    tiles = pl.num_programs(1)
    b1, b2 = bnd[b, 0], bnd[b, 1]

    @pl.when(t == 0)
    def _():
        prepare(b1, b2, bc_ref, dt_ref, cwb_ref, hp_ref, sel_ref, lk, score, bmat, cmat,
                btrans, ctrans, dts, sig, cum, cumt, ecol, tcol, True)
        dscore[...] = jnp.zeros_like(dscore)
        rsum[...] = jnp.zeros_like(rsum)
        rsum3[...] = jnp.zeros_like(rsum3)
        dball[...] = jnp.zeros_like(dball)
        dcall[...] = jnp.zeros_like(dcall)

    @pl.when((t == 0) & (b == 0))
    def _():
        dcw_ref[...] = jnp.zeros_like(dcw_ref)
        dhp_ref[...] = jnp.zeros_like(dhp_ref)

    turn = lax.rem(LANES - 2 * t, LANES)
    taps, bias = taps_of(cwx_ref, slice(None))
    links = [lk[0], lk[1], lk[2]]
    xin = xs_ref[...].astype(F32)
    pre = conv_pre(xin, taps, bias, links)
    sg = sigmoid(pre)
    x = pre * sg
    first = iota((TOK, LANES), 1) < P_SIZE
    dtx = pair(pltpu.roll(dts[...], turn, 1), first)
    xt = x * dtx
    xt16 = xt.astype(BF)
    xtf = xt16.astype(F32)
    skip = cwx_ref[5:6, :]
    dy = dscan_ref[...]
    dy16 = dy.astype(BF)
    dyf = dy16.astype(F32)
    mine = [jnp.where(first, dy16, jnp.zeros_like(dy16)), jnp.where(first, jnp.zeros_like(dy16), dy16)]
    cumr = pltpu.roll(cum[...], turn, 1)
    half = Q // 2
    parts = []
    for c in range(2):
        o = c * Q
        top = bottom = None
        for h in range(2):
            row = cumt[pl.ds(2 * t + h, 1), o : o + Q]
            col = cumr[o : o + Q, h : h + 1]
            w = jnp.exp2(jnp.minimum(row - col[:half], 0.0))
            dscore[c, :half, :] += w * mm_nt(xt16[o : o + half], mine[h][o : o + Q])
            y = mm((w * score[c, :half, :]).astype(BF), mine[h][o : o + Q])
            top = y if top is None else top + y
            w = jnp.exp2(jnp.minimum(row[:, half:] - col[half:], 0.0))
            dscore[c, half:, half:] += w * mm_nt(xt16[o + half : o + Q], mine[h][o + half : o + Q])
            y = mm((w * score[c, half:, half:]).astype(BF), mine[h][o + half : o + Q])
            bottom = y if bottom is None else bottom + y
        parts.append(jnp.concatenate([top, bottom], 0))
    tx = pair(pltpu.roll(tcol[...], turn, 1), first[:Q])
    ex = pair(pltpu.roll(ecol[...], turn, 1), first[:Q])
    txt16 = (tx * xt[:Q]).astype(BF)
    state = mm(btrans[...], txt16).astype(BF)
    dye = (ex * dy[Q:]).astype(BF)
    dstate = mm(ctrans[...], dye).astype(BF)
    dcall[...] += mm_nt(dye, state)
    dball[...] += mm_nt(txt16, dstate)
    across = tx * mm(bmat[:Q, :], dstate)
    within = jnp.concatenate(parts, 0)
    dxt = jnp.concatenate([parts[0] + across, parts[1]], 0)
    r1 = dyf * (scan_ref[...] - skip * x) - xtf * within
    r2 = x * dxt
    r3 = xtf[:Q] * across

    def split(v):
        hi = v.astype(BF)
        return [hi, (v - hi.astype(F32)).astype(BF)]

    def to_heads(width, offset):
        lane, head = iota((LANES, width), 0), iota((LANES, width), 1)
        return (head == offset + 2 * t + jnp.where(lane >= P_SIZE, 1, 0)).astype(BF)

    e1, e2 = to_heads(2 * LANES, 0), to_heads(2 * LANES, LANES)
    rsum[...] += mm(jnp.concatenate(split(r1), 1), jnp.concatenate([e1, e1], 0)) + mm(
        jnp.concatenate(split(r2), 1), jnp.concatenate([e2, e2], 0)
    )
    e3 = to_heads(LANES, 0)
    rsum3[...] += mm(jnp.concatenate(split(r3), 1), jnp.concatenate([e3, e3], 0))

    def conv_back(dact, pre, sg, xin, taps):
        dpre = dact * (sg * (1.0 + pre * (1.0 - sg)))
        g = taps[3] * dpre
        sums = [None] * 5
        sums[3] = jnp.sum(dpre * xin, axis=0, keepdims=True)
        sums[4] = jnp.sum(dpre, axis=0, keepdims=True)
        for k in range(1, 4):
            q = links[k - 1] * dpre
            g = g + taps[3 - k] * pltpu.roll(q, TOK - k, 0)
            sums[3 - k] = jnp.sum(q * pltpu.roll(xin, k, 0), axis=0, keepdims=True)
        return g, sums

    g, sums = conv_back(dxt * dtx + skip * dy, pre, sg, xin, taps)
    sums.append(jnp.sum(dy * x, axis=0, keepdims=True))
    sums.append(jnp.zeros((2, LANES), F32))
    here = pl.ds(pl.multiple_of(t * LANES, LANES), LANES)
    out_ref[:, here] = g.astype(BF)
    dcw_ref[:, here] += jnp.concatenate(sums, 0)

    @pl.when(t == tiles - 1)
    def _():
        db, dc = [], []
        for c in range(2):
            part = slice(c * Q, (c + 1) * Q)
            ds = jnp.where(allowed(c, b1, b2, True), dscore[c], 0.0)
            db.append(mm(ds.astype(BF), cmat[part, :]))
            dc.append(mm(ds.T.astype(BF), bmat[part, :]))
        db[0] = db[0] + dball[...]
        dc[1] = dc[1] + dcall[...]
        base = tiles * LANES
        for i, dact in enumerate((jnp.concatenate(db, 0), jnp.concatenate(dc, 0))):
            lanes = slice(i * LANES, (i + 1) * LANES)
            taps_b, bias_b = taps_of(cwb_ref, lanes)
            xin_b = bc_ref[:, lanes].astype(F32)
            pre_b = conv_pre(xin_b, taps_b, bias_b, links)
            g, sums = conv_back(dact, pre_b, sigmoid(pre_b), xin_b, taps_b)
            sums.append(jnp.zeros((3, LANES), F32))
            at = pl.ds(pl.multiple_of(base + i * LANES, LANES), LANES)
            out_ref[:, at] = g.astype(BF)
            dcw_ref[:, at] += jnp.concatenate(sums, 0)
        upper = (iota((Q, Q), 0) <= iota((Q, Q), 1)).astype(F32)
        below = (iota((Q, Q), 0) > iota((Q, Q), 1)).astype(F32)
        high = functools.partial(jnp.dot, precision=HIGHEST, preferred_element_type=F32)
        rate = hp_ref[1:2, :]
        da = jnp.concatenate(
            [
                high(upper, rsum[:Q, :LANES]) + high(below, rsum3[...]),
                high(upper, rsum[Q:, :LANES]),
            ],
            0,
        )
        step = dts[...]
        draw = (rsum[:, LANES:] + da * rate) * sig[...]
        dhp_ref[0:1, :] += jnp.sum(draw, axis=0, keepdims=True)
        dhp_ref[1:2, :] += jnp.sum(da * (rate * step), axis=0, keepdims=True)
        at = pl.ds(pl.multiple_of(base + 2 * LANES, LANES), LANES)
        out_ref[:, at] = mm_nt(draw.astype(BF), sel_ref[...]).astype(BF)


def stat_kernel(place, scan_ref, gate_ref, gin_ref, gain_ref, out_ref, one, two):
    t = pl.program_id(1)

    @pl.when(t == 0)
    def _():
        one[...] = jnp.zeros_like(one)
        two[...] = jnp.zeros_like(two)

    gate = gate_ref[...].astype(F32)
    gated = scan_ref[...] * (gate * sigmoid(gate))
    one[...] += gated * gated
    two[...] += gated * (gin_ref[...] * gain_ref[...])

    @pl.when(t == pl.num_programs(1) - 1)
    def _():
        a = jnp.sum(one[...].T, axis=0, keepdims=True)
        c = jnp.sum(two[...].T, axis=0, keepdims=True)
        out_ref[0] = jnp.concatenate([a, c, jnp.zeros((6, TOK), F32)], 0)


def gate_kernel(place, sum_ref, scan_ref, gate_ref, gin_ref, gain_ref, inner_ref, dgate_ref, dscan_ref, dgain_ref, rinv, coef):
    b, t = pl.program_id(0), pl.program_id(1)

    @pl.when(t == 0)
    def _():
        r = lax.rsqrt(sum_ref[0, 0:1, :] * (1.0 / DIN) + EPSILON)
        c = r * r * sum_ref[0, 1:2, :] * (1.0 / DIN)
        rinv[...] = jnp.broadcast_to(r, (LANES, TOK)).T
        coef[...] = jnp.broadcast_to(c, (LANES, TOK)).T

    @pl.when((t == 0) & (b == 0))
    def _():
        dgain_ref[...] = jnp.zeros_like(dgain_ref)

    gate = gate_ref[...].astype(F32)
    sg = sigmoid(gate)
    act = gate * sg
    scan = scan_ref[...]
    gain = gain_ref[...]
    gated = scan * act
    scaled = gated * rinv[...]
    gin = gin_ref[...]
    inner_ref[...] = (scaled * gain).astype(BF)
    dgated = rinv[...] * (gin * gain - gated * coef[...])
    dscan_ref[...] = dgated * act
    dgate_ref[...] = (dgated * scan * (sg * (1.0 + gate * (1.0 - sg)))).astype(BF)
    here = pl.ds(pl.multiple_of(t * LANES, LANES), LANES)
    dgain_ref[0:1, here] += jnp.sum(gin * scaled, axis=0, keepdims=True)


def params(*semantics):
    return pltpu.CompilerParams(dimension_semantics=semantics, vmem_limit_bytes=VMEM_LIMIT)


def block_scratch(extra):
    base = [
        pltpu.VMEM((3, TOK, LANES), F32),
        pltpu.VMEM((2, Q, Q), F32),
        pltpu.VMEM((TOK, LANES), BF),
        pltpu.VMEM((TOK, LANES), BF),
        pltpu.VMEM((LANES, Q), BF),
    ]
    column = pltpu.VMEM((TOK, LANES), F32)
    rest = [
        column,
        pltpu.VMEM((LANES, TOK), F32),
        pltpu.VMEM((Q, LANES), F32),
        pltpu.VMEM((Q, LANES), F32),
    ]
    if not extra:
        return base + [column] + rest
    return base + [pltpu.VMEM((LANES, Q), BF), column, column] + rest + [
        pltpu.VMEM((2, Q, Q), F32),
        pltpu.VMEM((TOK, 2 * LANES), F32),
        pltpu.VMEM((Q, LANES), F32),
        pltpu.VMEM((Q, LANES), F32),
        pltpu.VMEM((Q, LANES), F32),
    ]


def mixer_specs(tiles):
    return [
        pl.BlockSpec((TOK, LANES), lambda b, t, *_: (b, t)),
        pl.BlockSpec((TOK, 2 * LANES), lambda b, t, *_: (b, tiles // 2)),
        pl.BlockSpec((TOK, LANES), lambda b, t, *_: (b, tiles + 2)),
        pl.BlockSpec((8, LANES), lambda b, t, *_: (0, t)),
        pl.BlockSpec((8, 2 * LANES), lambda b, t, *_: (0, tiles // 2)),
        pl.BlockSpec((8, LANES), lambda b, t, *_: (0, 0)),
        pl.BlockSpec((LANES, LANES), lambda b, t, *_: (0, 0)),
    ]


def scan_forward(bounds, proj, cw, hp, sel, tiles):
    blocks = proj.shape[0] // TOK
    return pl.pallas_call(
        fwd_kernel,
        out_shape=jax.ShapeDtypeStruct((blocks * TOK, tiles * LANES), F32),
        grid_spec=pltpu.PrefetchScalarGridSpec(
            num_scalar_prefetch=1,
            grid=(blocks, tiles),
            in_specs=mixer_specs(tiles),
            out_specs=pl.BlockSpec((TOK, LANES), lambda b, t, *_: (b, t)),
            scratch_shapes=block_scratch(False),
        ),
        compiler_params=params("arbitrary", "arbitrary"),
        cost_estimate=pl.CostEstimate(flops=blocks * 2_000_000_000, bytes_accessed=blocks * 4_000_000, transcendentals=0),
    )(bounds, proj, proj, proj, cw, cw, hp, sel)


def scan_backward(bounds, proj, cw, hp, sel, scan, dscan, tiles):
    blocks = proj.shape[0] // TOK
    width = (tiles + 3) * LANES
    tile = pl.BlockSpec((TOK, LANES), lambda b, t, *_: (b, t))
    return pl.pallas_call(
        bwd_kernel,
        out_shape=(
            jax.ShapeDtypeStruct((blocks * TOK, width), BF),
            jax.ShapeDtypeStruct((8, (tiles + 2) * LANES), F32),
            jax.ShapeDtypeStruct((8, LANES), F32),
        ),
        grid_spec=pltpu.PrefetchScalarGridSpec(
            num_scalar_prefetch=1,
            grid=(blocks, tiles),
            in_specs=mixer_specs(tiles) + [tile, tile],
            out_specs=(
                pl.BlockSpec((TOK, width), lambda b, t, *_: (b, 0)),
                pl.BlockSpec((8, (tiles + 2) * LANES), lambda b, t, *_: (0, 0)),
                pl.BlockSpec((8, LANES), lambda b, t, *_: (0, 0)),
            ),
            scratch_shapes=block_scratch(True),
        ),
        compiler_params=params("arbitrary", "arbitrary"),
        cost_estimate=pl.CostEstimate(flops=blocks * 8_000_000_000, bytes_accessed=blocks * 6_000_000, transcendentals=0),
    )(bounds, proj, proj, proj, cw, cw, hp, sel, scan, dscan)


def gate_stats(place, scan, gate, ginner, gain):
    blocks, tiles = scan.shape[0] // TOK, scan.shape[1] // LANES
    tile = pl.BlockSpec((TOK, LANES), lambda b, t, *_: (b, t))
    return pl.pallas_call(
        stat_kernel,
        out_shape=jax.ShapeDtypeStruct((blocks, 8, TOK), F32),
        grid_spec=pltpu.PrefetchScalarGridSpec(
            num_scalar_prefetch=1,
            grid=(blocks, tiles),
            in_specs=[
                tile,
                tile,
                pl.BlockSpec((TOK, LANES), lambda b, t, place: (b, place[t])),
                pl.BlockSpec((1, LANES), lambda b, t, *_: (0, t)),
            ],
            out_specs=pl.BlockSpec((1, 8, TOK), lambda b, t, *_: (b, 0, 0)),
            scratch_shapes=[pltpu.VMEM((TOK, LANES), F32)] * 2,
        ),
        compiler_params=params("arbitrary", "arbitrary"),
        cost_estimate=pl.CostEstimate(flops=0, bytes_accessed=blocks * 5_000_000, transcendentals=0),
    )(place, scan, gate, ginner, gain)


def gate_both(place, sums, scan, gate, ginner, gain):
    blocks, tiles = scan.shape[0] // TOK, scan.shape[1] // LANES
    tile = pl.BlockSpec((TOK, LANES), lambda b, t, *_: (b, t))
    moved = pl.BlockSpec((TOK, LANES), lambda b, t, place: (b, place[t]))
    rows = blocks * TOK
    return pl.pallas_call(
        gate_kernel,
        out_shape=(
            jax.ShapeDtypeStruct((rows, tiles * LANES), BF),
            jax.ShapeDtypeStruct((rows, tiles * LANES), BF),
            jax.ShapeDtypeStruct((rows, tiles * LANES), F32),
            jax.ShapeDtypeStruct((8, tiles * LANES), F32),
        ),
        grid_spec=pltpu.PrefetchScalarGridSpec(
            num_scalar_prefetch=1,
            grid=(blocks, tiles),
            in_specs=[
                pl.BlockSpec((1, 8, TOK), lambda b, t, *_: (b, 0, 0)),
                tile,
                tile,
                moved,
                pl.BlockSpec((1, LANES), lambda b, t, *_: (0, t)),
            ],
            out_specs=(moved, tile, tile, pl.BlockSpec((8, tiles * LANES), lambda b, t, *_: (0, 0))),
            scratch_shapes=[pltpu.VMEM((TOK, LANES), F32)] * 2,
        ),
        compiler_params=params("arbitrary", "arbitrary"),
        cost_estimate=pl.CostEstimate(flops=0, bytes_accessed=blocks * 9_000_000, transcendentals=0),
    )(place, sums, scan, gate, ginner, gain)


def pick_kernel(table, w_ref, out_ref, *, width):
    t = pl.program_id(0)
    lane = iota(w_ref.shape, 1) + table[t] * LANES
    out_ref[...] = jnp.where(lane < width, w_ref[...], 0.0).astype(BF)


def pick_columns(table, weight, tiles):
    rows = weight.shape[0]
    return pl.pallas_call(
        functools.partial(pick_kernel, width=weight.shape[1]),
        out_shape=jax.ShapeDtypeStruct((rows, tiles * LANES), BF),
        grid_spec=pltpu.PrefetchScalarGridSpec(
            num_scalar_prefetch=1,
            grid=(tiles,),
            in_specs=[pl.BlockSpec((rows, LANES), lambda t, table: (0, table[t]))],
            out_specs=pl.BlockSpec((rows, LANES), lambda t, table: (0, t)),
        ),
        compiler_params=params("arbitrary"),
        cost_estimate=pl.CostEstimate(flops=0, bytes_accessed=rows * tiles * 768, transcendentals=0),
    )(table, weight)


STEP = 128


def norm_kernel(perm, tok_ref, gain_ref, out_ref):
    x = tok_ref[...].astype(F32)
    inv = lax.rsqrt(jnp.mean(x * x, axis=1, keepdims=True) + EPSILON)
    wide = D // 8
    for k in range(8):
        here = pl.ds(pl.multiple_of(perm[k] * wide, wide), wide)
        out_ref[:, k * wide : (k + 1) * wide] = (
            tok_ref[:, here].astype(F32) * inv * gain_ref[:, here]
        ).astype(BF)


def norm_rows(perm, tokens, gain):
    rows = tokens.shape[0]
    row = pl.BlockSpec((STEP, D), lambda i, *_: (i, 0))
    return pl.pallas_call(
        norm_kernel,
        out_shape=jax.ShapeDtypeStruct((rows, D), BF),
        grid_spec=pltpu.PrefetchScalarGridSpec(
            num_scalar_prefetch=1,
            grid=(rows // STEP,),
            in_specs=[row, pl.BlockSpec((1, D), lambda i, *_: (0, 0))],
            out_specs=row,
        ),
        compiler_params=params("arbitrary"),
        cost_estimate=pl.CostEstimate(flops=0, bytes_accessed=rows * D * 4, transcendentals=0),
    )(perm, tokens, gain)


def last_kernel(perm, tok_ref, cot_ref, keep_ref, gain_ref, one_ref, two_ref, three_ref, out_ref, grad):
    wide = D // 8
    for k in range(8):
        here = pl.ds(pl.multiple_of(perm[k] * wide, wide), wide)
        at = slice(k * wide, (k + 1) * wide)
        grad[:, here] = (
            one_ref[:, at].astype(F32) + two_ref[:, at].astype(F32) + three_ref[:, at].astype(F32)
        ) * gain_ref[:, here]
    x = tok_ref[...].astype(F32)
    inv = lax.rsqrt(jnp.mean(x * x, axis=1, keepdims=True) + EPSILON)
    g = grad[...]
    dot = jnp.mean(g * x, axis=1, keepdims=True)
    out_ref[...] = inv * (g - x * (inv * inv * dot)) + keep_ref[...] * cot_ref[...].astype(F32)


def last_rows(perm, tokens, cotangent, keep, gain, parts):
    rows = tokens.shape[0]
    row = pl.BlockSpec((STEP, D), lambda i, *_: (i, 0))
    return pl.pallas_call(
        last_kernel,
        out_shape=jax.ShapeDtypeStruct((rows, D), F32),
        grid_spec=pltpu.PrefetchScalarGridSpec(
            num_scalar_prefetch=1,
            grid=(rows // STEP,),
            in_specs=[
                row,
                row,
                pl.BlockSpec((STEP, 1), lambda i, *_: (i, 0)),
                pl.BlockSpec((1, D), lambda i, *_: (0, 0)),
                row,
                row,
                row,
            ],
            out_specs=row,
            scratch_shapes=[pltpu.VMEM((STEP, D), F32)],
        ),
        compiler_params=params("arbitrary"),
        cost_estimate=pl.CostEstimate(flops=0, bytes_accessed=rows * D * 14, transcendentals=0),
    )(perm, tokens, cotangent, keep, gain, *parts)


def join_kernel(me, *refs, tiles):
    out_ref = refs[-1]
    gates, rests = refs[:4], refs[4:8]
    r = me[0]
    for k in range(4):
        for t in range(tiles):
            at = slice(t * LANES, (t + 1) * LANES)
            owner = jnp.bitwise_xor(r, k)
            here = pl.ds(pl.multiple_of((4 * t + owner) * LANES, LANES), LANES)
            out_ref[:, here] = gates[k][:, at].astype(F32)
            here = pl.ds(pl.multiple_of((4 * (t + tiles) + owner) * LANES, LANES), LANES)
            out_ref[:, here] = rests[k][:, at].astype(F32)
    shared = sum(rests[k][:, tiles * LANES :].astype(F32) for k in range(4))
    base = 8 * tiles * LANES
    out_ref[:, base:] = shared[:, : out_ref.shape[1] - base]


def join_columns(me, gates, rests, width):
    rows = gates[0].shape[0]
    step = min(rows, 64)
    tiles = gates[0].shape[1] // LANES
    spec = lambda a: pl.BlockSpec((step, a.shape[1]), lambda i, *_: (i, 0))
    return pl.pallas_call(
        functools.partial(join_kernel, tiles=tiles),
        out_shape=jax.ShapeDtypeStruct((rows, width), F32),
        grid_spec=pltpu.PrefetchScalarGridSpec(
            num_scalar_prefetch=1,
            grid=(rows // step,),
            in_specs=[spec(a) for a in gates + rests],
            out_specs=pl.BlockSpec((step, width), lambda i, *_: (i, 0)),
        ),
        compiler_params=params("arbitrary"),
        cost_estimate=pl.CostEstimate(flops=0, bytes_accessed=rows * width * 6, transcendentals=0),
    )(me, *gates, *rests)


def swap(x, d):
    return lax.ppermute(x, "rep", [(i, i ^ d) for i in range(4)])


def share_rep(x):
    core, chip = swap(x, 1), swap(x, 2)
    return [x, core, chip, swap(chip, 1)]


def scatter_rep(parts):
    far = swap(parts[3].astype(BF), 1)
    chip = swap((parts[2].astype(F32) + far.astype(F32)).astype(BF), 2)
    return [parts[0], swap(parts[1].astype(BF), 1), chip]


FORWARD = [(RING[i], RING[(i + 1) % 8]) for i in range(8)]
BACKWARD = [(b, a) for a, b in FORWARD]


def relative(s, n):
    if n != 8:
        return jnp.arange(8, dtype=jnp.int32), jnp.arange(8, dtype=jnp.int32)
    table, inverse = [], []
    for shard in range(8):
        p = RING.index(shard)
        row = [RING[(p + d) % 8] for d in (0, -1, 1, -2, 2, -3, 3, 4)]
        table.append(row)
        inverse.append([row.index(i) for i in range(8)])
    return jnp.asarray(table, jnp.int32)[s], jnp.asarray(inverse, jnp.int32)[s]


def ring_gather(x):
    fw = lambda v: lax.ppermute(v, "shard", FORWARD)
    bw = lambda v: lax.ppermute(v, "shard", BACKWARD)
    pieces, a, b = [x], x, x
    for _ in range(3):
        a, b = fw(a), bw(b)
        pieces += [a, b]
    half = x.shape[0] // 2
    return pieces + [fw(a[:half]), bw(b[half:])]


def ring_scatter(parts):
    fw = lambda v: lax.ppermute(v.astype(BF), "shard", FORWARD).astype(F32)
    bw = lambda v: lax.ppermute(v.astype(BF), "shard", BACKWARD).astype(F32)
    own, f1, b1, f2, b2, f3, b3, far = parts
    half = far.shape[0] // 2
    rf, rb = fw(far[:half]), bw(far[half:])
    sf = jnp.concatenate([b3[:half] + rf, b3[half:]], 0)
    sb = jnp.concatenate([f3[:half], f3[half:] + rb], 0)
    for forward, backward in ((b2, f2), (b1, f1)):
        rf, rb = fw(sf), bw(sb)
        sf, sb = forward + rf, backward + rb
    return own + fw(sf) + bw(sb)


def gather_rows(x, n):
    if n == 8:
        return jnp.concatenate(ring_gather(x), 0)
    return lax.all_gather(x, "shard", axis=0, tiled=True)


def scatter_rows(total, n):
    if n == 8:
        rows = total.shape[0] // 8
        return ring_scatter([total[k * rows : (k + 1) * rows] for k in range(8)])
    return lax.psum_scatter(total, "shard", scatter_dimension=0, tiled=True)


def shards(n, tokens, cotangent, lengths, order, mask, in_weight, out_weight, conv_weight, conv_bias, dt_bias,
           a_log, skip_gain, gain_outer, gain_inner):
    r, s = lax.axis_index("rep"), lax.axis_index("shard")
    tiles = DIN // LANES // 4
    perm, place = relative(s, n)
    keep = mask.astype(F32)[:, None]
    catalog = jnp.arange(lengths.shape[0], dtype=jnp.int32)
    picked = jnp.sum(jnp.where(order[:, None] == catalog[None, :], lengths[None, :], 0), axis=1)
    bounds = jnp.stack([picked[0], picked[0] + picked[1]])[None, :]
    bounds = jnp.concatenate([bounds, swap(bounds, 1), swap(bounds, 2), swap(bounds, 3)], 0)

    mine = jnp.arange(tiles, dtype=jnp.int32) * 4 + r
    shared = jnp.arange(3, dtype=jnp.int32) + 8 * tiles
    rest_table = jnp.concatenate([mine + 4 * tiles, shared])
    w_rest = gather_rows(pick_columns(rest_table, in_weight, tiles + 3), n)
    normed = norm_rows(perm, tokens, gain_outer[None, :])
    normed = jnp.concatenate(share_rep(normed), 0)
    w_gate = gather_rows(pick_columns(mine, in_weight, tiles), n)
    gout = (cotangent.astype(F32) * keep).astype(BF)
    gout = jnp.concatenate(share_rep(gout), 0)
    if n == 8:
        own_rows = lax.dynamic_slice_in_dim(out_weight, r * LANES, LANES, 0).astype(BF)
        w_out = gather_rows(own_rows, n)
    else:
        w_out = lax.all_gather(out_weight.astype(BF), "shard", axis=0, tiled=True)
        w_out = lax.dynamic_index_in_dim(w_out.reshape(tiles, 4, LANES, D), r, 1, False).reshape(tiles * LANES, D)

    def own_lanes(v, width):
        v = lax.dynamic_index_in_dim(v.reshape(v.shape[:-1] + (tiles, 4, width)), r, v.ndim, False)
        return v.reshape(v.shape[:-2] + (tiles * width,))

    heads = H // 4
    rows8 = jnp.concatenate(
        [conv_weight, conv_bias[None], jnp.pad(jnp.broadcast_to(skip_gain[:, None], (H, P_SIZE)).reshape(1, DIN), ((0, 0), (0, 2 * N))),
         jnp.zeros((2, CONVCH), F32)], 0)
    cw = jnp.concatenate([own_lanes(rows8[:, :DIN], LANES), rows8[:, DIN:]], 1)
    hp = jnp.stack([own_lanes(dt_bias, 2), own_lanes(-jnp.exp(a_log), 2)])
    hp = jnp.pad(hp, ((0, 6), (0, LANES - heads)))
    lane = jnp.arange(LANES, dtype=jnp.int32)
    head = 8 * (lane // 2) + 2 * r + lane % 2
    sel = ((lane[:, None] == head[None, :]) & (lane[None, :] < heads)).astype(BF)
    gain = own_lanes(gain_inner, LANES)[None, :]

    proj = mm(normed, w_rest).astype(BF)
    scan = scan_forward(bounds, proj, cw, hp, sel, tiles)
    gate = mm(normed, w_gate).astype(BF)
    ginner = mm_nt(gout, w_out)
    sums = gate_stats(place, scan, gate, ginner, gain)
    there = [swap(sums, d) for d in (1, 2, 3)]
    sums = jnp.stack([sums[k] + there[0][k ^ 1] + there[1][k ^ 2] + there[2][k ^ 3] for k in range(4)])
    inner, dgate, dscan, dgain = gate_both(place, sums, scan, gate, ginner, gain)
    branch = mm(inner, w_out)
    branch = scatter_rep([branch[k * TOK : (k + 1) * TOK] for k in range(4)])
    branch = sum(p.astype(F32) for p in branch)
    layer_out = (keep * (tokens.astype(F32) + branch)).astype(BF)

    share_out = lax.dot_general(inner, gout, TN, preferred_element_type=F32)
    if n == 8:
        share_out = scatter_rows(share_out, n)
        pieces = share_rep(share_out.astype(BF))
        ordered = jnp.stack(pieces)
        grad_out_weight = jnp.concatenate(
            [lax.dynamic_index_in_dim(ordered, jnp.bitwise_xor(r, q), 0, False) for q in range(4)], 0
        ).astype(F32)
    else:
        spread = share_out.reshape(tiles, 1, LANES, D) * (jnp.arange(4)[None, :, None, None] == r)
        share_out = lax.psum_scatter(spread.reshape(DIN, D), "shard", scatter_dimension=0, tiled=True)
        grad_out_weight = lax.psum(share_out, "rep")
    share_gate = scatter_rows(lax.dot_general(normed, dgate, TN, preferred_element_type=F32), n)
    gates = share_rep(share_gate.astype(BF))
    gproj, dcw, dhp = scan_backward(bounds, proj, cw, hp, sel, scan, dscan, tiles)
    share_rest = scatter_rows(lax.dot_general(normed, gproj, TN, preferred_element_type=F32), n)
    rests = share_rep(share_rest.astype(BF))
    grad_in_weight = join_columns(r[None], gates, rests, in_weight.shape[1])
    gnormed = mm_nt(gproj, w_rest) + mm_nt(dgate, w_gate)
    dgo = jnp.sum(gnormed * normed.astype(F32), axis=0).reshape(8, D // 8)[place].reshape(D) / gain_outer
    gnormed = gnormed.astype(BF)
    parts = scatter_rep([gnormed[k * TOK : (k + 1) * TOK] for k in range(4)])
    grad_tokens = last_rows(perm, tokens, cotangent, keep, gain_outer[None, :], parts)

    at_r = (jnp.arange(4) == r).astype(F32)

    def all_lanes(v, width):
        v = v.reshape(v.shape[:-1] + (tiles, 1, width)) * at_r[:, None]
        return v.reshape(v.shape[:-3] + (tiles * 4 * width,))

    wide = jnp.concatenate([all_lanes(dcw[:5, : tiles * LANES], LANES), dcw[:5, tiles * LANES :]], 1)
    dskip = jnp.sum(dcw[5, : tiles * LANES].reshape(heads, P_SIZE), axis=1)
    small = [
        wide[:4].reshape(-1),
        wide[4],
        all_lanes(dhp[0, :heads], 2),
        all_lanes(dhp[1, :heads], 2),
        all_lanes(dskip, 2),
        dgo,
        all_lanes(dgain[0], LANES),
    ]
    sizes = [v.shape[0] for v in small]
    small = lax.psum(jnp.concatenate(small), ("rep", "shard"))
    ends = [sum(sizes[: i + 1]) for i in range(len(sizes))]
    g_cw, g_cb, g_db, g_al, g_sk, g_go, g_gi = [small[e - z : e] for e, z in zip(ends, sizes)]
    return (
        layer_out,
        grad_tokens,
        grad_in_weight,
        grad_out_weight,
        g_cw.reshape(4, CONVCH),
        g_cb,
        g_db,
        g_al,
        g_sk,
        g_go,
        g_gi,
    )


def solution(mesh):
    rows = P(("rep", "shard"), None)
    vector = P(("rep", "shard"))
    owned = P("shard", None)
    return jax.shard_map(
        functools.partial(shards, mesh.shape["shard"]),
        mesh=mesh,
        in_specs=(rows, rows, P(), vector, vector, owned, owned) + (P(),) * 7,
        out_specs=(rows, rows, owned, owned) + (P(),) * 7,
        check_vma=False,
    )
```

```python
import functools

import jax
import jax.numpy as jnp
from jax import lax
from jax.experimental import pallas as pl
from jax.experimental.pallas import tpu as pltpu
from jax.sharding import PartitionSpec as P

D = 2048
DIN = 4096
P_SIZE = 64
N = 128
Q = 256
H = 64
CONVCH = DIN + 2 * N
EPSILON = 1e-05
LOG2E = 1.4426950408889634
LANES = 128
TOK = 512
TILES = DIN // 128 // 4
REST = TILES * 128 + 2 * N + H // 4
HIGHEST = lax.Precision.HIGHEST
BF = jnp.bfloat16
F32 = jnp.float32
NT = (((1,), (1,)), ((), ()))
TN = (((0,), (0,)), ((), ()))
VMEM_LIMIT = 48 * 1024 * 1024
RING = (0, 2, 4, 6, 7, 5, 3, 1)


def mm(a, b):
    return jnp.dot(a, b, preferred_element_type=F32)


def mm_nt(a, b):
    return lax.dot_general(a, b, NT, preferred_element_type=F32)


def iota(shape, dim):
    return lax.broadcasted_iota(jnp.int32, shape, dim)


def start_of(rows, b1, b2):
    return jnp.where(rows >= b2, b2, jnp.where(rows >= b1, b1, 0))


def sigmoid(v):
    return 0.5 * jnp.tanh(0.5 * v) + 0.5


def conv_pre(x, taps, bias, lk):
    pre = bias + taps[3] * x
    for k in range(1, 4):
        pre = pre + taps[3 - k] * (pltpu.roll(x, k, 0) * lk[k - 1])
    return pre


def taps_of(cw_ref, lanes):
    return [cw_ref[k : k + 1, lanes] for k in range(4)], cw_ref[4:5, lanes]


def prepare(b1, b2, bc_ref, dt_ref, cwb_ref, hp_ref, lk, score, bmat, cmat, btrans, ctrans,
            dts, sig, cum, cumt, ecol, tcol, transposed):
    rows = iota((TOK, LANES), 0)
    pos = rows - start_of(rows, b1, b2)
    for k in range(1, 4):
        lk[k - 1] = (pos >= k).astype(F32)
    links = [lk[0], lk[1], lk[2]]
    for half, keep in ((0, bmat), (1, cmat)):
        lanes = slice(half * LANES, (half + 1) * LANES)
        taps, bias = taps_of(cwb_ref, lanes)
        pre = conv_pre(bc_ref[:, lanes].astype(F32), taps, bias, links)
        act = pre * sigmoid(pre)
        keep[...] = act.astype(BF)
        if half == 0:
            btrans[...] = act[:Q].T.astype(BF)
        elif ctrans is not None:
            ctrans[...] = act[Q:].T.astype(BF)
    for c in range(2):
        part = slice(c * Q, (c + 1) * Q)
        if transposed:
            s = mm_nt(bmat[part, :], cmat[part, :])
        else:
            s = mm_nt(cmat[part, :], bmat[part, :])
        score[c] = jnp.where(allowed(c, b1, b2, transposed), s, 0.0)
    raw = jnp.where(iota((TOK, LANES), 1) < H // 4, dt_ref[...].astype(F32), 0.0) + hp_ref[0:1, :]
    step = jnp.maximum(raw, 0.0) + jnp.log1p(jnp.exp(-jnp.abs(raw)))
    dts[...] = step
    if sig is not None:
        sig[...] = sigmoid(raw)
    decay = step * (hp_ref[1:2, :] * LOG2E)
    lower = (iota((Q, Q), 0) >= iota((Q, Q), 1)).astype(F32)
    for c in range(2):
        part = slice(c * Q, (c + 1) * Q)
        total = jnp.dot(lower, decay[part], precision=HIGHEST, preferred_element_type=F32)
        cum[part, :] = total
        cumt[:, part] = total.T
        if c == 0:
            last = start_of(Q - 1, b1, b2)
            tcol[...] = jnp.where(rows[:Q] >= last, jnp.exp2(total[Q - 1 : Q, :] - total), 0.0)
        else:
            linked = start_of(rows[Q:], b1, b2) <= Q - 1
            ecol[...] = jnp.where(linked, jnp.exp2(total), 0.0)


def allowed(c, b1, b2, transposed):
    late = iota((Q, Q), 1 if transposed else 0) + c * Q
    early = iota((Q, Q), 0 if transposed else 1) + c * Q
    return (early <= late) & (early >= start_of(late, b1, b2))


def pair(ref_value, first):
    return jnp.where(first, ref_value[:, 0:1], ref_value[:, 1:2])


def fwd_kernel(bnd, xs_ref, bc_ref, dt_ref, cwx_ref, cwb_ref, hp_ref, out_ref,
               lk, score, bmat, cmat, btrans, dts, cum, cumt, ecol, tcol):
    b, t = pl.program_id(0), pl.program_id(1)

    @pl.when(t == 0)
    def _():
        prepare(bnd[b, 0], bnd[b, 1], bc_ref, dt_ref, cwb_ref, hp_ref, lk, score, bmat, cmat,
                btrans, None, dts, None, cum, cumt, ecol, tcol, False)

    turn = lax.rem(LANES - 2 * t, LANES)
    taps, bias = taps_of(cwx_ref, slice(None))
    pre = conv_pre(xs_ref[...].astype(F32), taps, bias, [lk[0], lk[1], lk[2]])
    x = pre * sigmoid(pre)
    first = iota((TOK, LANES), 1) < P_SIZE
    xt = x * pair(pltpu.roll(dts[...], turn, 1), first)
    xt16 = xt.astype(BF)
    mine = [jnp.where(first, xt16, jnp.zeros_like(xt16)), jnp.where(first, jnp.zeros_like(xt16), xt16)]
    cumr = pltpu.roll(cum[...], turn, 1)
    half = Q // 2
    outs = []
    for c in range(2):
        o = c * Q
        top = bottom = None
        for h in range(2):
            row = cumt[pl.ds(2 * t + h, 1), o : o + Q]
            col = cumr[o : o + Q, h : h + 1]
            w = jnp.exp2(jnp.minimum(col[:half] - row[:, :half], 0.0)) * score[c, :half, :half]
            y = mm(w.astype(BF), mine[h][o : o + half])
            top = y if top is None else top + y
            w = jnp.exp2(jnp.minimum(col[half:] - row, 0.0)) * score[c, half:, :]
            y = mm(w.astype(BF), mine[h][o : o + Q])
            bottom = y if bottom is None else bottom + y
        outs.append(jnp.concatenate([top, bottom], 0))
    tx = pair(pltpu.roll(tcol[...], turn, 1), first[:Q])
    ex = pair(pltpu.roll(ecol[...], turn, 1), first[:Q])
    state = mm(btrans[...], (tx * xt[:Q]).astype(BF))
    outs[1] = outs[1] + mm(cmat[Q:, :], state.astype(BF)) * ex
    skip = cwx_ref[5:6, :]
    out_ref[...] = jnp.concatenate(outs, 0) + skip * x


def bwd_kernel(bnd, xs_ref, bc_ref, dt_ref, cwx_ref, cwb_ref, hp_ref, scan_ref, dscan_ref,
               out_ref, dcw_ref, dhp_ref,
               lk, score, bmat, cmat, btrans, ctrans, dts, sig, cum, cumt, ecol, tcol, dscore, rsum, rsum3, dball, dcall):
    b, t = pl.program_id(0), pl.program_id(1)
    tiles = TILES
    b1, b2 = bnd[b, 0], bnd[b, 1]

    @pl.when(t == 0)
    def _():
        prepare(b1, b2, bc_ref, dt_ref, cwb_ref, hp_ref, lk, score, bmat, cmat,
                btrans, ctrans, dts, sig, cum, cumt, ecol, tcol, True)
        dscore[...] = jnp.zeros_like(dscore)
        rsum[...] = jnp.zeros_like(rsum)
        rsum3[...] = jnp.zeros_like(rsum3)
        dball[...] = jnp.zeros_like(dball)
        dcall[...] = jnp.zeros_like(dcall)

    @pl.when((t == 0) & (b == 0))
    def _():
        dcw_ref[...] = jnp.zeros_like(dcw_ref)
        dhp_ref[...] = jnp.zeros_like(dhp_ref)

    turn = lax.rem(LANES - 2 * t, LANES)
    taps, bias = taps_of(cwx_ref, slice(None))
    links = [lk[0], lk[1], lk[2]]
    xin = xs_ref[...].astype(F32)
    pre = conv_pre(xin, taps, bias, links)
    sg = sigmoid(pre)
    x = pre * sg
    first = iota((TOK, LANES), 1) < P_SIZE
    dtx = pair(pltpu.roll(dts[...], turn, 1), first)
    xt = x * dtx
    xt16 = xt.astype(BF)
    xtf = xt16.astype(F32)
    skip = cwx_ref[5:6, :]
    dy16 = dscan_ref[...]
    dy = dy16.astype(F32)
    dyf = dy
    mine = [jnp.where(first, dy16, jnp.zeros_like(dy16)), jnp.where(first, jnp.zeros_like(dy16), dy16)]
    cumr = pltpu.roll(cum[...], turn, 1)
    half = Q // 2
    parts = []
    for c in range(2):
        o = c * Q
        top = bottom = None
        for h in range(2):
            row = cumt[pl.ds(2 * t + h, 1), o : o + Q]
            col = cumr[o : o + Q, h : h + 1]
            w = jnp.exp2(jnp.minimum(row - col[:half], 0.0))
            dscore[c, :half, :] += w * mm_nt(xt16[o : o + half], mine[h][o : o + Q])
            y = mm((w * score[c, :half, :]).astype(BF), mine[h][o : o + Q])
            top = y if top is None else top + y
            w = jnp.exp2(jnp.minimum(row[:, half:] - col[half:], 0.0))
            dscore[c, half:, half:] += w * mm_nt(xt16[o + half : o + Q], mine[h][o + half : o + Q])
            y = mm((w * score[c, half:, half:]).astype(BF), mine[h][o + half : o + Q])
            bottom = y if bottom is None else bottom + y
        parts.append(jnp.concatenate([top, bottom], 0))
    tx = pair(pltpu.roll(tcol[...], turn, 1), first[:Q])
    ex = pair(pltpu.roll(ecol[...], turn, 1), first[:Q])
    txt16 = (tx * xt[:Q]).astype(BF)
    state = mm(btrans[...], txt16).astype(BF)
    dye = (ex * dy[Q:]).astype(BF)
    dstate = mm(ctrans[...], dye).astype(BF)
    dcall[...] += mm_nt(dye, state)
    dball[...] += mm_nt(txt16, dstate)
    across = tx * mm(bmat[:Q, :], dstate)
    within = jnp.concatenate(parts, 0)
    dxt = jnp.concatenate([parts[0] + across, parts[1]], 0)
    r1 = dyf * (scan_ref[...] - skip * x) - xtf * within
    r2 = x * dxt
    r3 = xtf[:Q] * across

    def split(v):
        hi = v.astype(BF)
        return [hi, (v - hi.astype(F32)).astype(BF)]

    def to_heads(width, offset):
        lane, head = iota((LANES, width), 0), iota((LANES, width), 1)
        return (head == offset + 2 * t + jnp.where(lane >= P_SIZE, 1, 0)).astype(BF)

    e1, e2 = to_heads(2 * LANES, 0), to_heads(2 * LANES, LANES)
    rsum[...] += mm(jnp.concatenate(split(r1), 1), jnp.concatenate([e1, e1], 0)) + mm(
        jnp.concatenate(split(r2), 1), jnp.concatenate([e2, e2], 0)
    )
    e3 = to_heads(LANES, 0)
    rsum3[...] += mm(jnp.concatenate(split(r3), 1), jnp.concatenate([e3, e3], 0))

    def conv_back(dact, pre, sg, xin, taps):
        dpre = dact * (sg * (1.0 + pre * (1.0 - sg)))
        g = taps[3] * dpre
        sums = [None] * 5
        sums[3] = jnp.sum(dpre * xin, axis=0, keepdims=True)
        sums[4] = jnp.sum(dpre, axis=0, keepdims=True)
        for k in range(1, 4):
            q = links[k - 1] * dpre
            g = g + taps[3 - k] * pltpu.roll(q, TOK - k, 0)
            sums[3 - k] = jnp.sum(q * pltpu.roll(xin, k, 0), axis=0, keepdims=True)
        return g, sums

    g, sums = conv_back(dxt * dtx + skip * dy, pre, sg, xin, taps)
    sums.append(jnp.sum(dy * x, axis=0, keepdims=True))
    sums.append(jnp.zeros((2, LANES), F32))
    here = pl.ds(pl.multiple_of(t * LANES, LANES), LANES)
    out_ref[:, here] = g.astype(BF)
    dcw_ref[:, here] += jnp.concatenate(sums, 0)

    @pl.when(t == tiles - 1)
    def _():
        db, dc = [], []
        for c in range(2):
            part = slice(c * Q, (c + 1) * Q)
            ds = jnp.where(allowed(c, b1, b2, True), dscore[c], 0.0)
            db.append(mm(ds.astype(BF), cmat[part, :]))
            dc.append(mm(ds.T.astype(BF), bmat[part, :]))
        db[0] = db[0] + dball[...]
        dc[1] = dc[1] + dcall[...]
        base = tiles * LANES
        for i, dact in enumerate((jnp.concatenate(db, 0), jnp.concatenate(dc, 0))):
            lanes = slice(i * LANES, (i + 1) * LANES)
            taps_b, bias_b = taps_of(cwb_ref, lanes)
            xin_b = bc_ref[:, lanes].astype(F32)
            pre_b = conv_pre(xin_b, taps_b, bias_b, links)
            g, sums = conv_back(dact, pre_b, sigmoid(pre_b), xin_b, taps_b)
            sums.append(jnp.zeros((3, LANES), F32))
            at = slice(base + i * LANES, base + (i + 1) * LANES)
            out_ref[:, at] = g.astype(BF)
            dcw_ref[:, at] += jnp.concatenate(sums, 0)
        upper = (iota((Q, Q), 0) <= iota((Q, Q), 1)).astype(F32)
        below = (iota((Q, Q), 0) > iota((Q, Q), 1)).astype(F32)
        high = functools.partial(jnp.dot, precision=HIGHEST, preferred_element_type=F32)
        rate = hp_ref[1:2, :]
        da = jnp.concatenate(
            [
                high(upper, rsum[:Q, :LANES]) + high(below, rsum3[...]),
                high(upper, rsum[Q:, :LANES]),
            ],
            0,
        )
        step = dts[...]
        draw = (rsum[:, LANES:] + da * rate) * sig[...]
        dhp_ref[0:1, :] += jnp.sum(draw, axis=0, keepdims=True)
        dhp_ref[1:2, :] += jnp.sum(da * (rate * step), axis=0, keepdims=True)
        out_ref[:, base + 2 * LANES :] = draw[:, : H // 4].astype(BF)


def params(*semantics):
    return pltpu.CompilerParams(dimension_semantics=semantics, vmem_limit_bytes=VMEM_LIMIT)


def cost(flops, moved):
    return pl.CostEstimate(flops=int(flops), bytes_accessed=int(moved), transcendentals=0)


def block_scratch(extra):
    column = pltpu.VMEM((TOK, LANES), F32)
    part = pltpu.VMEM((Q, LANES), F32)
    half = pltpu.VMEM((LANES, Q), BF)
    base = [
        pltpu.VMEM((3, TOK, LANES), F32),
        pltpu.VMEM((2, Q, Q), F32),
        pltpu.VMEM((TOK, LANES), BF),
        pltpu.VMEM((TOK, LANES), BF),
        half,
    ]
    rest = [column, pltpu.VMEM((LANES, TOK), F32), part, part]
    if not extra:
        return base + [column] + rest
    return base + [half, column, column] + rest + [
        pltpu.VMEM((2, Q, Q), F32),
        pltpu.VMEM((TOK, 2 * LANES), F32),
        part,
        part,
        part,
    ]


def mixer_specs(first):
    return [
        pl.BlockSpec((TOK, LANES), lambda b, t, *_: (b + first, t)),
        pl.BlockSpec((TOK, 2 * LANES), lambda b, t, *_: (b + first, TILES // 2)),
        pl.BlockSpec((TOK, LANES), lambda b, t, *_: (b + first, TILES + 2)),
        pl.BlockSpec((8, LANES), lambda b, t, *_: (0, t)),
        pl.BlockSpec((8, 2 * LANES), lambda b, t, *_: (0, TILES // 2)),
        pl.BlockSpec((8, LANES), lambda b, t, *_: (0, 0)),
    ]


ANY = pl.BlockSpec(memory_space=pl.ANY)


def fwd_into(bnd, *refs):
    fwd_kernel(bnd, *refs[:6], *refs[7:])


def scan_forward(bounds, proj, cw, hp, first, count, into=None):
    return pl.pallas_call(
        fwd_kernel if into is None else fwd_into,
        out_shape=jax.ShapeDtypeStruct((proj.shape[0], TILES * LANES), F32),
        grid_spec=pltpu.PrefetchScalarGridSpec(
            num_scalar_prefetch=1,
            grid=(count, TILES),
            in_specs=mixer_specs(first) + ([] if into is None else [ANY]),
            out_specs=pl.BlockSpec((TOK, LANES), lambda b, t, *_: (b + first, t)),
            scratch_shapes=block_scratch(False),
        ),
        input_output_aliases={} if into is None else {7: 0},
        compiler_params=params("arbitrary", "arbitrary"),
        cost_estimate=cost(count * 8e9, count * 4e6),
    )(bounds[first : first + count], proj, proj, proj, cw, cw, hp, *([] if into is None else [into]))


def bwd_into(bnd, *refs):
    bwd_kernel(bnd, *refs[:8], *refs[9:])


def scan_backward(bounds, proj, cw, hp, scan, dscan, first, count, into=None):
    tile = pl.BlockSpec((TOK, LANES), lambda b, t, *_: (b + first, t))
    return pl.pallas_call(
        bwd_kernel if into is None else bwd_into,
        out_shape=(
            jax.ShapeDtypeStruct((proj.shape[0], REST), BF),
            jax.ShapeDtypeStruct((8, (TILES + 2) * LANES), F32),
            jax.ShapeDtypeStruct((8, LANES), F32),
        ),
        grid_spec=pltpu.PrefetchScalarGridSpec(
            num_scalar_prefetch=1,
            grid=(count, TILES),
            in_specs=mixer_specs(first) + [tile, tile] + ([] if into is None else [ANY]),
            out_specs=(
                pl.BlockSpec((TOK, REST), lambda b, t, *_: (b + first, 0)),
                pl.BlockSpec((8, (TILES + 2) * LANES), lambda b, t, *_: (0, 0)),
                pl.BlockSpec((8, LANES), lambda b, t, *_: (0, 0)),
            ),
            scratch_shapes=block_scratch(True),
        ),
        input_output_aliases={} if into is None else {9: 0},
        compiler_params=params("arbitrary", "arbitrary"),
        cost_estimate=cost(count * 16e9, count * 6e6),
    )(bounds[first : first + count], proj, proj, proj, cw, cw, hp, scan, dscan, *([] if into is None else [into]))


def ginner_kernel(gout_ref, w_ref, out_ref, wide_ref):
    @pl.when(pl.program_id(0) == 0)
    def _():
        for k in range(8):
            for p in range(8):
                wide_ref[p * LANES : (p + 1) * LANES, k * 256 : (k + 1) * 256] = w_ref[
                    k * LANES : (k + 1) * LANES, p * 256 : (p + 1) * 256
                ]

    out_ref[...] = mm_nt(gout_ref[...], wide_ref[...]).astype(BF)


def inner_gradient(gout, w_two):
    rows, inner = gout.shape[0], TILES * LANES
    return pl.pallas_call(
        ginner_kernel,
        out_shape=(jax.ShapeDtypeStruct((rows, inner), BF), jax.ShapeDtypeStruct((inner, D), BF)),
        grid=(rows // TOK,),
        in_specs=[
            pl.BlockSpec((TOK, D), lambda i: (i, 0)),
            pl.BlockSpec((inner, D), lambda i: (1, 0)),
        ],
        out_specs=(pl.BlockSpec((TOK, inner), lambda i: (i, 0)), pl.BlockSpec((inner, D), lambda i: (0, 0))),
        compiler_params=params("arbitrary"),
        cost_estimate=cost(2 * rows * inner * D, 2 * (rows * D + rows * inner + 2 * inner * D)),
    )(gout, w_two)


def stat_kernel(place, norm_ref, w_ref, scan_ref, gin_ref, gain_ref, gate_ref, out_ref):
    gate_ref[...] = mm_nt(norm_ref[...], w_ref[...]).astype(BF)
    one = two = jnp.zeros((TOK, LANES), F32)
    for t in range(TILES):
        at = slice(t * LANES, (t + 1) * LANES)
        there = pl.ds(pl.multiple_of(place[t] * LANES, LANES), LANES)
        gate = gate_ref[:, at].astype(F32)
        gated = scan_ref[:, at] * (gate * sigmoid(gate))
        one = one + gated * gated
        two = two + gated * (gin_ref[:, there].astype(F32) * gain_ref[:, at])
    a = jnp.sum(one.T, axis=0, keepdims=True)
    c = jnp.sum(two.T, axis=0, keepdims=True)
    out_ref[0] = jnp.concatenate([a, c, jnp.zeros((6, TOK), F32)], 0)


def gate_stats(place, normed, w_two, scan, ginner, gain):
    rows, inner = scan.shape
    tile = pl.BlockSpec((TOK, inner), lambda b, *_: (b, 0))
    return pl.pallas_call(
        stat_kernel,
        out_shape=(jax.ShapeDtypeStruct((rows, inner), BF), jax.ShapeDtypeStruct((rows // TOK, 8, TOK), F32)),
        grid_spec=pltpu.PrefetchScalarGridSpec(
            num_scalar_prefetch=1,
            grid=(rows // TOK,),
            in_specs=[
                pl.BlockSpec((TOK, D), lambda b, *_: (b, 0)),
                pl.BlockSpec((inner, D), lambda b, *_: (0, 0)),
                tile,
                tile,
                pl.BlockSpec((1, inner), lambda b, *_: (0, 0)),
            ],
            out_specs=(tile, pl.BlockSpec((1, 8, TOK), lambda b, *_: (b, 0, 0))),
        ),
        compiler_params=params("arbitrary"),
        cost_estimate=cost(2 * rows * inner * D, rows * (D * 2 + inner * 8) + inner * D * 2),
    )(place, normed, w_two, scan, ginner, gain)


def gate_kernel(place, sum_ref, scan_ref, gate_ref, gin_ref, gain_ref, inner_ref, dgate_ref, dscan_ref, dgain_ref):
    rows = scan_ref.shape[0]

    @pl.when((pl.program_id(0) == 0) & (pl.program_id(1) == 0))
    def _():
        dgain_ref[...] = jnp.zeros_like(dgain_ref)

    r = lax.rsqrt(sum_ref[0, 0:1, :] * (1.0 / DIN) + EPSILON)
    c = r * r * sum_ref[0, 1:2, :] * (1.0 / DIN)
    rinv = jnp.broadcast_to(r, (LANES, rows)).T
    coef = jnp.broadcast_to(c, (LANES, rows)).T
    for t in range(TILES):
        at = slice(t * LANES, (t + 1) * LANES)
        there = pl.ds(pl.multiple_of(place[t] * LANES, LANES), LANES)
        gate = gate_ref[:, at].astype(F32)
        sg = sigmoid(gate)
        act = gate * sg
        scan = scan_ref[:, at]
        gain = gain_ref[:, at]
        gated = scan * act
        scaled = gated * rinv
        gin = gin_ref[:, there].astype(F32)
        inner_ref[:, there] = (scaled * gain).astype(BF)
        dgated = rinv * (gin * gain - gated * coef)
        dscan_ref[:, at] = (dgated * act).astype(BF)
        dgate_ref[:, at] = (dgated * scan * (sg + act * (1.0 - sg))).astype(BF)
        dgain_ref[0:1, at] += jnp.sum(gin * scaled, axis=0, keepdims=True)


def gate_both(place, sums, scan, gate, ginner, gain):
    rows, inner = scan.shape
    tile = pl.BlockSpec((Q, inner), lambda b, h, *_: (2 * b + h, 0))
    out = jax.ShapeDtypeStruct((rows, inner), BF)
    return pl.pallas_call(
        gate_kernel,
        out_shape=(out, out, out, jax.ShapeDtypeStruct((8, inner), F32)),
        grid_spec=pltpu.PrefetchScalarGridSpec(
            num_scalar_prefetch=1,
            grid=(rows // TOK, 2),
            in_specs=[
                pl.BlockSpec((1, 8, Q), lambda b, h, *_: (b, 0, h)),
                tile,
                tile,
                tile,
                pl.BlockSpec((1, inner), lambda b, h, *_: (0, 0)),
            ],
            out_specs=(tile, tile, tile, pl.BlockSpec((8, inner), lambda b, h, *_: (0, 0))),
        ),
        compiler_params=params("arbitrary", "arbitrary"),
        cost_estimate=cost(0, rows * inner * 14),
    )(place, sums, scan, gate, ginner, gain)


def back_kernel(a_ref, wa_ref, b_ref, wb_ref, norm_ref, out_ref, dgo_ref):
    @pl.when(pl.program_id(0) == 0)
    def _():
        dgo_ref[...] = jnp.zeros_like(dgo_ref)

    for c in range(4):
        at = slice(c * 512, (c + 1) * 512)
        res = mm(a_ref[...], wa_ref[:, at]) + mm(b_ref[...], wb_ref[:, at])
        out_ref[:, at] = res.astype(BF)
        dgo_ref[0:1, at] += jnp.sum(res * norm_ref[:, at].astype(F32), axis=0, keepdims=True)


def normed_gradient(gproj, w_rest, dgate, w_two, normed, first, count):
    rows, inner = dgate.shape
    row = lambda width: pl.BlockSpec((TOK, width), lambda b: (b + first, 0))
    return pl.pallas_call(
        back_kernel,
        out_shape=(jax.ShapeDtypeStruct((count * TOK, D), BF), jax.ShapeDtypeStruct((8, D), F32)),
        grid=(count,),
        in_specs=[
            row(REST),
            pl.BlockSpec((REST, D), lambda b: (0, 0)),
            row(inner),
            pl.BlockSpec((inner, D), lambda b: (0, 0)),
            row(D),
        ],
        out_specs=(pl.BlockSpec((TOK, D), lambda b: (b, 0)), pl.BlockSpec((8, D), lambda b: (0, 0))),
        compiler_params=params("arbitrary"),
        cost_estimate=cost(2 * count * TOK * D * (REST + inner), 2 * (REST + inner) * D),
    )(gproj, w_rest, dgate, w_two, normed)


def across_kernel(a_ref, b_ref, out_ref, turned):
    @pl.when(pl.program_id(0) == 0)
    def _():
        turned[...] = a_ref[...].T

    res = mm(turned[...], b_ref[...])
    if out_ref.shape[0] == res.shape[0]:
        out_ref[...] = res.astype(out_ref.dtype)
    else:
        for p in range(8):
            out_ref[:, p * 256 : (p + 1) * 256] = res[p * LANES : (p + 1) * LANES].astype(out_ref.dtype)


def across_rows(a, b, retile):
    rows, m = a.shape
    n = b.shape[1]
    if retile:
        spec = pl.BlockSpec((LANES, 8 * 256), lambda k: (k, 0))
    else:
        spec = pl.BlockSpec((m, 256), lambda k: (0, k))
    return pl.pallas_call(
        across_kernel,
        out_shape=jax.ShapeDtypeStruct((m, n), BF),
        grid=(n // 256,),
        in_specs=[pl.BlockSpec((rows, m), lambda k: (0, 0)), pl.BlockSpec((rows, 256), lambda k: (0, k))],
        out_specs=spec,
        scratch_shapes=[pltpu.VMEM((m, rows), BF)],
        compiler_params=params("arbitrary"),
        cost_estimate=cost(2 * rows * m * n, 2 * (rows * m + rows * n + m * n)),
    )(a, b)


STEP = 128


def norm_kernel(perm, tok_ref, gain_ref, out_ref):
    x = tok_ref[...].astype(F32)
    inv = lax.rsqrt(jnp.mean(x * x, axis=1, keepdims=True) + EPSILON)
    wide = D // 8
    for k in range(8):
        here = pl.ds(pl.multiple_of(perm[k] * wide, wide), wide)
        out_ref[:, k * wide : (k + 1) * wide] = (
            tok_ref[:, here].astype(F32) * inv * gain_ref[:, here]
        ).astype(BF)


def norm_rows(perm, tokens, gain):
    rows = tokens.shape[0]
    row = pl.BlockSpec((STEP, D), lambda i, *_: (i, 0))
    return pl.pallas_call(
        norm_kernel,
        out_shape=jax.ShapeDtypeStruct((rows, D), BF),
        grid_spec=pltpu.PrefetchScalarGridSpec(
            num_scalar_prefetch=1,
            grid=(rows // STEP,),
            in_specs=[row, pl.BlockSpec((1, D), lambda i, *_: (0, 0))],
            out_specs=row,
        ),
        compiler_params=params("arbitrary"),
        cost_estimate=pl.CostEstimate(flops=0, bytes_accessed=rows * D * 4, transcendentals=0),
    )(perm, tokens, gain)


def last_kernel(perm, tok_ref, cot_ref, keep_ref, gain_ref, one_ref, two_ref, three_ref, out_ref, grad):
    wide = D // 8
    for k in range(8):
        here = pl.ds(pl.multiple_of(perm[k] * wide, wide), wide)
        at = slice(k * wide, (k + 1) * wide)
        grad[:, here] = (
            one_ref[:, at].astype(F32) + two_ref[:, at].astype(F32) + three_ref[:, at].astype(F32)
        ) * gain_ref[:, here]
    x = tok_ref[...].astype(F32)
    inv = lax.rsqrt(jnp.mean(x * x, axis=1, keepdims=True) + EPSILON)
    g = grad[...]
    dot = jnp.mean(g * x, axis=1, keepdims=True)
    out_ref[...] = inv * (g - x * (inv * inv * dot)) + keep_ref[...] * cot_ref[...].astype(F32)


def last_rows(perm, tokens, cotangent, keep, gain, parts):
    rows = tokens.shape[0]
    row = pl.BlockSpec((STEP, D), lambda i, *_: (i, 0))
    return pl.pallas_call(
        last_kernel,
        out_shape=jax.ShapeDtypeStruct((rows, D), F32),
        grid_spec=pltpu.PrefetchScalarGridSpec(
            num_scalar_prefetch=1,
            grid=(rows // STEP,),
            in_specs=[
                row,
                row,
                pl.BlockSpec((STEP, 1), lambda i, *_: (i, 0)),
                pl.BlockSpec((1, D), lambda i, *_: (0, 0)),
                row,
                row,
                row,
            ],
            out_specs=row,
            scratch_shapes=[pltpu.VMEM((STEP, D), F32)],
        ),
        compiler_params=params("arbitrary"),
        cost_estimate=pl.CostEstimate(flops=0, bytes_accessed=rows * D * 14, transcendentals=0),
    )(perm, tokens, cotangent, keep, gain, *parts)


def first_join_kernel(me, one, two, three, four, out_ref, grad_ref, stage, sem):
    pieces = (one, two, three, four)
    inner = TILES * LANES
    copies = []
    for k in range(4):
        q = jnp.bitwise_xor(me[0], k)
        for t in range(TILES):
            rows = pl.ds(pl.multiple_of((4 * t + q) * LANES, LANES), LANES)
            stage[rows, :] = pieces[k][t * LANES : (t + 1) * LANES, :].astype(F32)
    copy = pltpu.make_async_copy(stage, out_ref.at[pl.ds(0, 4 * inner)], sem)
    copy.start()
    for k in range(4):
        q = jnp.bitwise_xor(me[0], k)
        rows = pl.ds(pl.multiple_of(q * LANES, LANES), LANES)
        for c in range(8 if one.shape[1] == 256 else 0):
            grad_ref[rows, c * 256 : (c + 1) * 256] = pieces[k][
                inner + c * LANES : inner + (c + 1) * LANES, :
            ].astype(F32)
    copy.wait()


def first_join(me, pieces, width):
    lanes = pieces[0].shape[1]
    whole = pl.BlockSpec(pieces[0].shape, lambda i, *_: (0, 0))
    return pl.pallas_call(
        first_join_kernel,
        out_shape=(
            jax.ShapeDtypeStruct((width, lanes), F32),
            jax.ShapeDtypeStruct((4 * LANES, D), F32),
        ),
        grid_spec=pltpu.PrefetchScalarGridSpec(
            num_scalar_prefetch=1,
            grid=(1,),
            in_specs=[whole] * 4,
            out_specs=(ANY, pl.BlockSpec((4 * LANES, D), lambda i, *_: (0, 0))),
            scratch_shapes=[pltpu.VMEM((4 * TILES * LANES, lanes), F32), pltpu.SemaphoreType.DMA],
        ),
        compiler_params=params("arbitrary"),
        cost_estimate=cost(0, 20e6),
    )(me, *pieces)


def last_join_kernel(me, one, two, three, four, into, out_ref, stage, sem):
    pieces = (one, two, three, four)
    inner = TILES * LANES
    few = H // 4
    for k in range(4):
        q = jnp.bitwise_xor(me[0], k)
        for t in range(TILES):
            rows = pl.ds(pl.multiple_of((4 * t + q) * LANES, LANES), LANES)
            stage[rows, :] = pieces[k][t * LANES : (t + 1) * LANES, :].astype(F32)
    stage[4 * inner : 4 * inner + 2 * N, :] = sum(p[inner : inner + 2 * N, :].astype(F32) for p in pieces)
    steps = None
    for k in range(4):
        q = jnp.bitwise_xor(me[0], k)
        head, mine = iota((H, few), 0), iota((H, few), 1)
        spread = (head == 8 * (mine // 2) + 2 * q + mine % 2).astype(BF)
        term = mm(spread, pieces[k][inner + 2 * N :, :])
        steps = term if steps is None else steps + term
    stage[4 * inner + 2 * N :, :] = steps
    copy = pltpu.make_async_copy(stage, out_ref.at[pl.ds(4 * inner, stage.shape[0])], sem)
    copy.start()
    copy.wait()


def last_join(me, pieces, into):
    lanes = pieces[0].shape[1]
    whole = pl.BlockSpec(pieces[0].shape, lambda i, *_: (0, 0))
    return pl.pallas_call(
        last_join_kernel,
        out_shape=jax.ShapeDtypeStruct(into.shape, F32),
        grid_spec=pltpu.PrefetchScalarGridSpec(
            num_scalar_prefetch=1,
            grid=(1,),
            in_specs=[whole] * 4 + [ANY],
            out_specs=ANY,
            scratch_shapes=[pltpu.VMEM((into.shape[0] - 4 * TILES * LANES, lanes), F32), pltpu.SemaphoreType.DMA],
        ),
        input_output_aliases={5: 0},
        compiler_params=params("arbitrary"),
        cost_estimate=cost(0, 8e6),
    )(me, *pieces, into)


def tie(*arrays):
    return lax.optimization_barrier(arrays)


def swap(x, d):
    return lax.ppermute(x, "rep", [(i, i ^ d) for i in range(4)])


def fw(x):
    return lax.ppermute(x, "shard", [(RING[i], RING[(i + 1) % 8]) for i in range(8)])


def bw(x):
    return lax.ppermute(x, "shard", [(RING[(i + 1) % 8], RING[i]) for i in range(8)])


def relative(s, n):
    if n != 8:
        return jnp.arange(8, dtype=jnp.int32), jnp.arange(8, dtype=jnp.int32)
    table, inverse = [], []
    for shard in range(8):
        p = RING.index(shard)
        row = [RING[(p + d) % 8] for d in (0, -1, 1, -2, 2, -3, 3, 4)]
        table.append(row)
        inverse.append([row.index(i) for i in range(8)])
    return jnp.asarray(table, jnp.int32)[s], jnp.asarray(inverse, jnp.int32)[s]


def cut(rows):
    return -(-rows // 32) * 16


def gather_ring(piece, work):
    half = cut(piece.shape[0])
    pieces, a, b = [piece], piece, piece
    done = []
    for k in range(4):
        if k < 3:
            a, b = fw(a), bw(b)
        else:
            a, b = fw(a[:half]), bw(b[half:])
        if k < len(work) and work[k] is not None:
            result = work[k](*done)
            a, b, *result = tie(a, b, *result)
            done = result
        else:
            a, b = tie(a, b)
        pieces += [a, b]
    far = jnp.concatenate(pieces[-2:], 0)
    return jnp.concatenate(pieces[:7] + [far], 1), done


def ring_sum(parts):
    own, f1, b1, f2, b2, f3, b3, far = parts
    half = cut(far.shape[0])
    add = lambda a, b: (a.astype(F32) + b.astype(F32)).astype(BF)
    rf, rb = yield fw(far[:half]), bw(far[half:])
    sf = jnp.concatenate([add(b3[:half], rf), b3[half:]], 0)
    sb = jnp.concatenate([f3[:half], add(f3[half:], rb)], 0)
    rf, rb = yield fw(sf), bw(sb)
    rf, rb = yield fw(add(b2, rf)), bw(add(f2, rb))
    rf, rb = yield fw(add(b1, rf)), bw(add(f1, rb))
    yield (own.astype(F32) + rf.astype(F32) + rb.astype(F32)).astype(BF)


def blocks_of(x):
    return [x[k * TOK : (k + 1) * TOK] for k in range(4)]


def sum_rep(parts):
    far = swap(parts[3], 1)
    chip = swap((parts[2].astype(F32) + far.astype(F32)).astype(BF), 2)
    return parts[0].astype(F32) + swap(parts[1], 1).astype(F32) + chip.astype(F32)


def shards(n, tokens, cotangent, lengths, order, mask, in_weight, out_weight, conv_weight, conv_bias, dt_bias,
           a_log, skip_gain, gain_outer, gain_inner):
    r, s = lax.axis_index("rep"), lax.axis_index("shard")
    ring = n == 8
    inner_width = TILES * LANES
    perm, place = relative(s, n)
    keep = mask.astype(F32)[:, None]
    catalog = jnp.arange(lengths.shape[0], dtype=jnp.int32)
    picked = jnp.sum(jnp.where(order[:, None] == catalog[None, :], lengths[None, :], 0), axis=1)
    bounds = jnp.stack([picked[0], picked[0] + picked[1]])[None, :]
    bounds = jnp.concatenate([bounds, swap(bounds, 1), swap(bounds, 2), swap(bounds, 3)], 0)

    turned = in_weight.T
    lanes = turned.shape[1]

    def own_rows(first, tile):
        part = turned[first : first + TILES * 4 * tile].reshape(TILES, 4, tile, lanes)
        return lax.dynamic_index_in_dim(part, r, 1, False).reshape(TILES * tile, lanes)

    rest = jnp.concatenate(
        [own_rows(DIN, LANES), turned[2 * DIN : 2 * DIN + 2 * N], own_rows(2 * DIN + 2 * N, 2)], 0
    ).astype(BF)
    gate_rows = own_rows(0, LANES).astype(BF)
    normed = norm_rows(perm, tokens, gain_outer[None, :])
    gout = (cotangent.astype(F32) * keep).astype(BF)

    def own_lanes(v, width):
        v = lax.dynamic_index_in_dim(v.reshape(v.shape[:-1] + (TILES, 4, width)), r, v.ndim, False)
        return v.reshape(v.shape[:-2] + (TILES * width,))

    heads = H // 4
    skip = jnp.broadcast_to(skip_gain[:, None], (H, P_SIZE)).reshape(1, DIN)
    rows8 = jnp.concatenate(
        [conv_weight, conv_bias[None], jnp.pad(skip, ((0, 0), (0, 2 * N))), jnp.zeros((2, CONVCH), F32)], 0
    )
    cw = jnp.concatenate([own_lanes(rows8[:, :DIN], LANES), rows8[:, DIN:]], 1)
    hp = jnp.stack([own_lanes(dt_bias, 2), own_lanes(-jnp.exp(a_log), 2)])
    hp = jnp.pad(hp, ((0, 6), (0, LANES - heads)))
    gain = own_lanes(gain_inner, LANES)[None, :]

    core, chip = swap(normed, 1), swap(normed, 2)
    if ring:
        w_rest, _ = gather_ring(rest, [])
    else:
        w_rest = lax.all_gather(rest, "shard", axis=1, tiled=True)
    w_rest, core, chip = tie(w_rest, core, chip)
    (all_normed,) = tie(jnp.concatenate([normed, core, chip, swap(chip, 1)], 0))

    if ring:
        out_rows = lax.dynamic_slice_in_dim(out_weight, r * LANES, LANES, 0).astype(BF)
        out_rows = out_rows.reshape(LANES, 8, 256).swapaxes(0, 1).reshape(inner_width, 256)
        two, _, gout = tie(jnp.concatenate([gate_rows, out_rows], 0), w_rest, gout)
        gcore, gchip = swap(gout, 1), swap(gout, 2)

        def project():
            return [mm_nt(all_normed, w_rest).astype(BF)]

        def scan_first(proj):
            return [proj, scan_forward(bounds, proj, cw, hp, 0, 2)]

        def scan_last(proj, scan):
            return [proj, scan_forward(bounds, proj, cw, hp, 2, 2, scan)]

        w_two, (proj, scan) = gather_ring(two, [project, scan_first, scan_last])
    else:
        gcore, gchip = swap(gout, 1), swap(gout, 2)
        proj = mm_nt(all_normed, w_rest).astype(BF)
        scan = scan_forward(bounds, proj, cw, hp, 0, 4)
        w_gate = lax.all_gather(gate_rows, "shard", axis=1, tiled=True)
        w_out = lax.all_gather(out_weight.astype(BF), "shard", axis=0, tiled=True)
        w_out = lax.dynamic_index_in_dim(w_out.reshape(TILES, 4, LANES, D), r, 1, False)
        w_out = w_out.reshape(8, LANES, 8, 256).transpose(2, 1, 0, 3).reshape(inner_width, D)
        w_two = jnp.concatenate([w_gate, w_out], 0)
    (all_gout,) = tie(jnp.concatenate([gout, gcore, gchip, swap(gchip, 1)], 0))

    ginner, w_out = inner_gradient(all_gout, w_two)
    gate, sums = gate_stats(place, all_normed, w_two, scan, ginner, gain)
    there = [swap(sums, d) for d in (1, 2, 3)]
    sums = jnp.stack([sums[k] + there[0][k ^ 1] + there[1][k ^ 2] + there[2][k ^ 3] for k in range(4)])
    inner, dgate, dscan, dgain = gate_both(place, sums, scan, gate, ginner, gain)
    grad_gate = across_rows(dgate, all_normed, False)
    grad_out = across_rows(inner, all_gout, True)

    def split(x):
        return [x[:, k * 256 : (k + 1) * 256] for k in range(8)]

    at_r = (jnp.arange(4) == r).astype(F32)
    sizes = [4 * CONVCH, CONVCH, H, H, H, D, DIN]

    def all_lanes(v, width):
        v = v.reshape(v.shape[:-1] + (TILES, 1, width)) * at_r[:, None]
        return v.reshape(v.shape[:-3] + (TILES * 4 * width,))

    def small_vector(dcw, dhp, dgo, dgain):
        wide = jnp.concatenate([all_lanes(dcw[:5, :inner_width], LANES), dcw[:5, inner_width:]], 1)
        dskip = jnp.sum(dcw[5, :inner_width].reshape(heads, P_SIZE), axis=1)
        dgo = dgo[0].reshape(8, D // 8)[place].reshape(D) / gain_outer
        parts = [
            wide.reshape(-1),
            all_lanes(dhp[0, :heads], 2),
            all_lanes(dhp[1, :heads], 2),
            all_lanes(dskip, 2),
            dgo,
            all_lanes(dgain[0], LANES),
        ]
        flat = jnp.concatenate(parts)
        return jnp.pad(flat, (0, -flat.shape[0] % 1024)).reshape(-1, LANES)

    width = in_weight.shape[1]
    back = functools.partial(scan_backward, bounds, proj, cw, hp, scan, dscan)
    final = functools.partial(normed_gradient, w_rest=w_rest, dgate=dgate, w_two=w_two, normed=all_normed)
    if ring:
        steps = ring_sum([jnp.concatenate(p, 0) for p in zip(split(grad_gate), split(grad_out))])
        sent = next(steps)
        branch = mm(inner, w_out).astype(BF)
        *sent, branch = tie(*sent, branch)
        b0, b1, b2, b3 = blocks_of(branch)
        sent = steps.send(sent)
        far = swap(b3, 1)
        gproj, dcw, dhp = back(0, 1)
        *sent, far, gproj = tie(*sent, far, gproj)
        sent = steps.send(sent)
        core, chip = swap(b1, 1), swap((b2.astype(F32) + far.astype(F32)).astype(BF), 2)
        gproj, d, e = back(1, 1, gproj)
        dcw, dhp = dcw + d, dhp + e
        gproj, d, e = back(2, 1, gproj)
        dcw, dhp = dcw + d, dhp + e
        *sent, gproj = tie(*sent, gproj)
        sent = steps.send(sent)
        gproj, d, e = back(3, 1, gproj)
        dcw, dhp = dcw + d, dhp + e
        *sent, gproj, core, chip = tie(*sent, gproj, core, chip)
        share = steps.send(sent)
        layer_out = (keep * (tokens.astype(F32) + b0.astype(F32) + core.astype(F32) + chip.astype(F32))).astype(BF)

        gates = [share, swap(share, 1), swap(share, 2)]
        grad_rest = lax.dot_general(gproj, all_normed, TN, preferred_element_type=F32).astype(BF)
        steps = ring_sum(split(grad_rest))
        sent = next(steps)
        grad3, dgo = final(gproj, first=3, count=1)
        *sent, grad3 = tie(*sent, grad3)
        sent = steps.send(sent)
        far = swap(grad3, 1)
        grad2, d = final(gproj, first=2, count=1)
        dgo = dgo + d
        far, grad2, gates[2], layer_out = tie(far, grad2, gates[2], layer_out)
        chip = swap((grad2.astype(F32) + far.astype(F32)).astype(BF), 2)
        grad1, d = final(gproj, first=1, count=1)
        dgo = dgo + d
        *sent, grad1 = tie(*sent, grad1)
        sent = steps.send(sent)
        core = swap(grad1, 1)
        gates.append(swap(gates[2], 1))
        grad0, d = final(gproj, first=0, count=1)
        dgo = dgo + d
        *sent, core, gates[3], grad0 = tie(*sent, core, gates[3], grad0)
        sent = steps.send(sent)
        grad_in, grad_out_weight = first_join(r[None], gates, width)
        small = small_vector(dcw, dhp, dgo, dgain)
        small = small + swap(small, 1)
        *sent, grad_in, small = tie(*sent, grad_in, small)
        share = steps.send(sent)
        rests = [share, swap(share, 1), swap(share, 2)]
        d = 1
        while d < n:
            small = small + lax.ppermute(small, "shard", [(i, i ^ d) for i in range(n)])
            d *= 2
        chip, small = tie(chip, small)
        small = small + swap(small, 2)
        rests.append(swap(rests[2], 1))
        parts = [grad0, core, chip]
        grad_tokens = last_rows(perm, tokens, cotangent, keep, gain_outer[None, :], parts)
    else:
        everyone = lambda x: [x, swap(x, 1), swap(x, 2), swap(x, 3)]
        rows_sum = lambda x: lax.psum_scatter(x.astype(F32), "shard", scatter_dimension=1, tiled=True).astype(BF)
        branch = mm(inner, w_out).astype(BF)
        gproj, dcw, dhp = back(0, 4)
        layer_out = (keep * (tokens.astype(F32) + sum_rep(blocks_of(branch)))).astype(BF)
        grad_rest = lax.dot_general(gproj, all_normed, TN, preferred_element_type=F32).astype(BF)
        gnormed, dgo = final(gproj, first=0, count=4)
        total = sum_rep(blocks_of(gnormed)).astype(BF)
        grad_tokens = last_rows(
            perm, tokens, cotangent, keep, gain_outer[None, :], [total, jnp.zeros_like(total), jnp.zeros_like(total)]
        )
        spread = grad_out.reshape(8, LANES, 8, 256).transpose(2, 1, 0, 3).reshape(TILES, 1, LANES, D).astype(F32)
        spread = spread * (jnp.arange(4)[None, :, None, None] == r)
        spread = lax.psum_scatter(spread.reshape(DIN, D), "shard", scatter_dimension=0, tiled=True)
        grad_out_weight = lax.psum(spread, "rep")
        gates = everyone(jnp.pad(rows_sum(grad_gate), ((0, inner_width), (0, 0))))
        rests = everyone(rows_sum(grad_rest))
        grad_in, _ = first_join(r[None], gates, width)
        small = lax.psum(small_vector(dcw, dhp, dgo, dgain), ("rep", "shard"))
    grad_in_weight = last_join(r[None], rests, grad_in).T

    small = small.reshape(-1)
    ends = [sum(sizes[: i + 1]) for i in range(len(sizes))]
    g_cw, g_cb, g_db, g_al, g_sk, g_go, g_gi = [small[e - z : e] for e, z in zip(ends, sizes)]
    return (
        layer_out,
        grad_tokens,
        grad_in_weight,
        grad_out_weight,
        g_cw.reshape(4, CONVCH),
        g_cb,
        g_db,
        g_al,
        g_sk,
        g_go,
        g_gi,
    )


def solution(mesh):
    rows = P(("rep", "shard"), None)
    vector = P(("rep", "shard"))
    owned = P("shard", None)
    return jax.shard_map(
        functools.partial(shards, mesh.shape["shard"]),
        mesh=mesh,
        in_specs=(rows, rows, P(), vector, vector, owned, owned) + (P(),) * 7,
        out_specs=(rows, rows, owned, owned) + (P(),) * 7,
        check_vma=False,
    )
```

```python
import functools

import jax
import jax.numpy as jnp
from jax import lax
from jax.experimental import pallas as pl
from jax.experimental.pallas import tpu as pltpu
from jax.sharding import PartitionSpec as P

D = 2048
DIN = 4096
P_SIZE = 64
N = 128
Q = 256
H = 64
CONVCH = DIN + 2 * N
EPSILON = 1e-05
LOG2E = 1.4426950408889634
LANES = 128
TOK = 512
TILES = DIN // 128 // 4
HEADS = H // 4
REST = TILES * 128 + 2 * N + H // 4
HIGHEST = lax.Precision.HIGHEST
BF = jnp.bfloat16
F32 = jnp.float32
NT = (((1,), (1,)), ((), ()))
TN = (((0,), (0,)), ((), ()))
RING = (0, 2, 4, 6, 7, 5, 3, 1)


def mm(a, b):
    return jnp.dot(a, b, preferred_element_type=F32)


def mm_nt(a, b):
    return lax.dot_general(a, b, NT, preferred_element_type=F32)


def iota(shape, dim):
    return lax.broadcasted_iota(jnp.int32, shape, dim)


def start_of(rows, b1, b2):
    return jnp.where(rows >= b2, b2, jnp.where(rows >= b1, b1, 0))


def sigmoid(v):
    return 0.5 * jnp.tanh(0.5 * v) + 0.5


def conv_pre(x, taps, bias, lk):
    pre = bias + taps[3] * x
    for k in range(1, 4):
        pre = pre + taps[3 - k] * (pltpu.roll(x, k, 0) * lk[k - 1])
    return pre


def taps_of(cw_ref, lanes):
    return [cw_ref[k : k + 1, lanes] for k in range(4)], cw_ref[4:5, lanes]


def terms(v, count):
    out = []
    for _ in range(count):
        out.append(v.astype(BF).astype(F32))
        v = v - out[-1]
    return out


def side_by_side(parts):
    return sum(pltpu.roll(p, HEADS * i, 1) if i else p for i, p in enumerate(parts))


def prepare(b1, b2, bc_ref, dt_ref, cwb_ref, hp_ref, lk, score, bmat, cmat, btrans, ctrans,
            dts, sig, late, early, expand, transposed):
    rows = iota((TOK, LANES), 0)
    lane = iota((TOK, LANES), 1)
    pos = rows - start_of(rows, b1, b2)
    for k in range(1, 4):
        lk[k - 1] = (pos >= k).astype(F32)
    links = [lk[0], lk[1], lk[2]]
    for half, keep in ((0, bmat), (1, cmat)):
        lanes = slice(half * LANES, (half + 1) * LANES)
        taps, bias = taps_of(cwb_ref, lanes)
        pre = conv_pre(bc_ref[:, lanes].astype(F32), taps, bias, links)
        act = pre * sigmoid(pre)
        keep[...] = act.astype(BF)
        if half == 0:
            btrans[...] = act[:Q].T.astype(BF)
        elif ctrans is not None:
            ctrans[...] = act[Q:].T.astype(BF)
    for c in range(2):
        part = slice(c * Q, (c + 1) * Q)
        if transposed:
            s = mm_nt(bmat[part, :], cmat[part, :])
        else:
            s = mm_nt(cmat[part, :], bmat[part, :])
        score[c] = jnp.where(allowed(c, b1, b2, transposed), s, 0.0)
    real = lane < HEADS
    raw = jnp.where(real, dt_ref[...].astype(F32), 0.0) + hp_ref[0:1, :]
    step = jnp.where(real, jnp.maximum(raw, 0.0) + jnp.log1p(jnp.exp(-jnp.abs(raw))), 0.0)
    if dts is not None:
        dts[...] = step
        sig[...] = sigmoid(raw)
    decay = step * (hp_ref[1:2, :] * LOG2E)
    lower = (iota((Q, Q), 0) >= iota((Q, Q), 1)).astype(F32)
    sums = [
        jnp.dot(lower, decay[c * Q : (c + 1) * Q], precision=HIGHEST, preferred_element_type=F32) for c in range(2)
    ]
    last = start_of(Q - 1, b1, b2)
    out = jnp.where(rows[:Q] >= last, jnp.exp2(sums[0][Q - 1 : Q, :] - sums[0]), 0.0)
    into = jnp.where(start_of(rows[Q:], b1, b2) <= Q - 1, jnp.exp2(sums[1]), 0.0)
    middle = jnp.where(real, jnp.concatenate([out, into], 0), 0.0)
    expand[...] = side_by_side(terms(step, 2) + terms(middle, 2)).astype(BF)
    split = side_by_side(terms(jnp.concatenate(sums, 0), 3))
    used = lane % 64 < 3 * HEADS
    late[...] = jnp.where(used & (lane >= 64), 1.0, split).astype(BF)
    early[...] = jnp.where(used & (lane < 64), 1.0, pltpu.roll(-split, 64, 1)).astype(BF)


def both_heads(v, t):
    lane = iota(v.shape, 1) % HEADS
    zero = jnp.zeros_like(v)
    return jnp.concatenate([jnp.where(lane == 2 * t, v, zero), jnp.where(lane == 2 * t + 1, v, zero)], 0)


def spread_over(expand, t):
    row, col = iota((LANES, 2 * LANES), 0), iota((LANES, 2 * LANES), 1)
    head = 2 * t + (col % LANES) // P_SIZE
    pick = (row % HEADS == head) & (row // (2 * HEADS) == col // LANES)
    both = mm(expand[...], pick.astype(BF))
    return both[:, :LANES], both[:, LANES:]


def allowed(c, b1, b2, transposed):
    late = iota((Q, Q), 1 if transposed else 0) + c * Q
    early = iota((Q, Q), 0 if transposed else 1) + c * Q
    return (early <= late) & (early >= start_of(late, b1, b2))


def fwd_kernel(bnd, xs_ref, bc_ref, dt_ref, cwx_ref, cwb_ref, hp_ref, out_ref,
               lk, score, bmat, cmat, btrans, late, early, expand):
    b = pl.program_id(0)
    prepare(bnd[b, 0], bnd[b, 1], bc_ref, dt_ref, cwb_ref, hp_ref, lk, score, bmat, cmat,
            btrans, None, None, None, late, early, expand, False)
    for t in range(TILES):
        fwd_tile(t, slice(t * LANES, (t + 1) * LANES), xs_ref, cwx_ref, out_ref,
                 lk, score, cmat, btrans, late, early, expand)


def fwd_tile(t, at, xs_ref, cwx_ref, out_ref, lk, score, cmat, btrans, late, early, expand):
    taps, bias = taps_of(cwx_ref, at)
    pre = conv_pre(xs_ref[:, at].astype(F32), taps, bias, [lk[0], lk[1], lk[2]])
    x = pre * sigmoid(pre)
    first = iota((TOK, LANES), 1) < P_SIZE
    dtx, middle = spread_over(expand, t)
    xt = x * dtx
    xt16 = xt.astype(BF)
    half = Q // 2
    outs = []
    for c in range(2):
        o = c * Q
        for rows, width in ((slice(o, o + half), half), (slice(o + half, o + Q), Q)):
            last = rows.stop - o
            w = mm_nt(both_heads(late[rows, :], t), early[o : o + width, :])
            s = score[c, last - half : last, :width]
            w = jnp.exp2(jnp.minimum(w, 0.0)) * jnp.concatenate([s, s], 0)
            y = mm(w.astype(BF), xt16[o : o + width])
            outs.append(jnp.where(first[:half], y[:half], y[half:]))
    outs = [jnp.concatenate(outs[:2], 0), jnp.concatenate(outs[2:], 0)]
    state = mm(btrans[...], (middle[:Q] * xt[:Q]).astype(BF))
    outs[1] = outs[1] + mm(cmat[Q:, :], state.astype(BF)) * middle[Q:]
    skip = cwx_ref[5:6, at]
    out_ref[:, at] = jnp.concatenate(outs, 0) + skip * x


def conv_back(dact, pre, sg, xin, taps, links):
    dpre = dact * (sg * (1.0 + pre * (1.0 - sg)))
    g = taps[3] * dpre
    sums = [None] * 5
    sums[3] = jnp.sum(dpre * xin, axis=0, keepdims=True)
    sums[4] = jnp.sum(dpre, axis=0, keepdims=True)
    for k in range(1, 4):
        q = links[k - 1] * dpre
        g = g + taps[3 - k] * pltpu.roll(q, TOK - k, 0)
        sums[3 - k] = jnp.sum(q * pltpu.roll(xin, k, 0), axis=0, keepdims=True)
    return g, sums


def bwd_tile(t, at, xs_ref, cwx_ref, scan_ref, dscan_ref, out_ref, dcw_ref,
             lk, score, bmat, btrans, ctrans, late, early, expand, dscore, rsum, rsum3, dball, dcall):
    taps, bias = taps_of(cwx_ref, at)
    links = [lk[0], lk[1], lk[2]]
    xin = xs_ref[:, at].astype(F32)
    pre = conv_pre(xin, taps, bias, links)
    sg = sigmoid(pre)
    x = pre * sg
    first = iota((TOK, LANES), 1) < P_SIZE
    dtx, middle = spread_over(expand, t)
    xt = x * dtx
    xt16 = xt.astype(BF)
    xtf = xt16.astype(F32)
    skip = cwx_ref[5:6, at]
    dy16 = dscan_ref[:, at]
    dy = dy16.astype(F32)
    dyf = dy
    zero = jnp.zeros((Q // 2, LANES), BF)
    half = Q // 2
    parts = []
    for c in range(2):
        o = c * Q
        for rows, begin in ((slice(o, o + half), 0), (slice(o + half, o + Q), half)):
            at_row = slice(begin, begin + half)
            later = slice(o + begin, o + Q)
            w = jnp.exp2(jnp.minimum(mm_nt(both_heads(early[rows, :], t), late[later, :]), 0.0))
            xr = xt16[rows]
            xr = jnp.concatenate([jnp.where(first[:half], xr, zero), jnp.where(first[:half], zero, xr)], 0)
            wp = w * mm_nt(xr, dy16[later])
            dscore[c, at_row, begin:] += wp[:half] + wp[half:]
            s = score[c, at_row, begin:]
            y = mm((w * jnp.concatenate([s, s], 0)).astype(BF), dy16[later])
            parts.append(jnp.where(first[:half], y[:half], y[half:]))
    parts = [jnp.concatenate(parts[:2], 0), jnp.concatenate(parts[2:], 0)]
    tx, ex = middle[:Q], middle[Q:]
    txt16 = (tx * xt[:Q]).astype(BF)
    state = mm(btrans[...], txt16).astype(BF)
    dye = (ex * dy[Q:]).astype(BF)
    dstate = mm(ctrans[...], dye).astype(BF)
    dcall[...] += mm_nt(dye, state)
    dball[...] += mm_nt(txt16, dstate)
    across = tx * mm(bmat[:Q, :], dstate)
    within = jnp.concatenate(parts, 0)
    dxt = jnp.concatenate([parts[0] + across, parts[1]], 0)
    r1 = dyf * (scan_ref[:, at] - skip * x) - xtf * within
    r2 = x * dxt
    r3 = xtf[:Q] * across

    hi = r1.astype(BF)
    row, col = iota((2 * LANES, LANES), 0), iota((2 * LANES, LANES), 1)
    pick = (col == 2 * t + (row % LANES) // P_SIZE).astype(BF)
    rsum[...] += mm(jnp.concatenate([hi, (r1 - hi.astype(F32)).astype(BF)], 1), pick)
    row, col = iota((2 * LANES, 2 * LANES), 0), iota((2 * LANES, 2 * LANES), 1)
    pick = ((col % LANES == 2 * t + (row % LANES) // P_SIZE) & (row // LANES == col // LANES)).astype(BF)
    r3 = jnp.concatenate([r3, jnp.zeros_like(r3)], 0)
    rsum3[...] += mm(jnp.concatenate([r2.astype(BF), r3.astype(BF)], 1), pick)
    g, sums = conv_back(dxt * dtx + skip * dy, pre, sg, xin, taps, links)
    sums.append(jnp.sum(dy * x, axis=0, keepdims=True))
    sums.append(jnp.zeros((2, LANES), F32))
    out_ref[:, at] = g.astype(BF)
    dcw_ref[:, at] += jnp.concatenate(sums, 0)


def bwd_kernel(bnd, xs_ref, bc_ref, dt_ref, cwx_ref, cwb_ref, hp_ref, scan_ref, dscan_ref,
               out_ref, dcw_ref, dhp_ref,
               lk, score, bmat, cmat, btrans, late, early, expand, ctrans, dts, sig, dscore, rsum, rsum3, dball, dcall):
    b = pl.program_id(0)
    b1, b2 = bnd[b, 0], bnd[b, 1]

    @pl.when(b == 0)
    def _():
        dcw_ref[...] = jnp.zeros_like(dcw_ref)
        dhp_ref[...] = jnp.zeros_like(dhp_ref)

    prepare(b1, b2, bc_ref, dt_ref, cwb_ref, hp_ref, lk, score, bmat, cmat,
            btrans, ctrans, dts, sig, late, early, expand, True)
    for v in (dscore, rsum, rsum3, dball, dcall):
        v[...] = jnp.zeros_like(v)
    for t in range(TILES):
        bwd_tile(t, slice(t * LANES, (t + 1) * LANES), xs_ref, cwx_ref, scan_ref, dscan_ref, out_ref, dcw_ref,
                 lk, score, bmat, btrans, ctrans, late, early, expand, dscore, rsum, rsum3, dball, dcall)
    links = [lk[0], lk[1], lk[2]]

    db, dc = [], []
    for c in range(2):
        part = slice(c * Q, (c + 1) * Q)
        ds = jnp.where(allowed(c, b1, b2, True), dscore[c], 0.0)
        db.append(mm(ds.astype(BF), cmat[part, :]))
        dc.append(mm(ds.T.astype(BF), bmat[part, :]))
    db[0] = db[0] + dball[...]
    dc[1] = dc[1] + dcall[...]
    base = TILES * LANES
    for i, dact in enumerate((jnp.concatenate(db, 0), jnp.concatenate(dc, 0))):
        lanes = slice(i * LANES, (i + 1) * LANES)
        taps_b, bias_b = taps_of(cwb_ref, lanes)
        xin_b = bc_ref[:, lanes].astype(F32)
        pre_b = conv_pre(xin_b, taps_b, bias_b, links)
        g, sums = conv_back(dact, pre_b, sigmoid(pre_b), xin_b, taps_b, links)
        sums.append(jnp.zeros((3, LANES), F32))
        at = slice(base + i * LANES, base + (i + 1) * LANES)
        out_ref[:, at] = g.astype(BF)
        dcw_ref[:, at] += jnp.concatenate(sums, 0)
    upper = (iota((Q, Q), 0) <= iota((Q, Q), 1)).astype(F32)
    below = (iota((Q, Q), 0) > iota((Q, Q), 1)).astype(F32)
    high = functools.partial(jnp.dot, precision=HIGHEST, preferred_element_type=F32)
    rate = hp_ref[1:2, :]
    da = jnp.concatenate(
        [
            high(upper, rsum[:Q, :]) + high(below, rsum3[:Q, LANES:]),
            high(upper, rsum[Q:, :]),
        ],
        0,
    )
    step = dts[...]
    draw = (rsum3[:, :LANES] + da * rate) * sig[...]
    dhp_ref[0:1, :] += jnp.sum(draw, axis=0, keepdims=True)
    dhp_ref[1:2, :] += jnp.sum(da * (rate * step), axis=0, keepdims=True)
    out_ref[:, base + 2 * LANES :] = draw[:, :HEADS].astype(BF)


def params(*semantics, mib=48):
    return pltpu.CompilerParams(dimension_semantics=semantics, vmem_limit_bytes=mib * 1024 * 1024)


def cost(flops, moved):
    return pl.CostEstimate(flops=int(flops / 16), bytes_accessed=int(moved / 16), transcendentals=0)


def block_scratch(extra):
    column = pltpu.VMEM((TOK, LANES), F32)
    packed = pltpu.VMEM((TOK, LANES), BF)
    part = pltpu.VMEM((Q, LANES), F32)
    half = pltpu.VMEM((LANES, Q), BF)
    square = pltpu.VMEM((2, Q, Q), F32)
    base = [pltpu.VMEM((3, TOK, LANES), F32), square, packed, packed, half, packed, packed, packed]
    if not extra:
        return base
    return base + [half, column, column, square, column, pltpu.VMEM((TOK, 2 * LANES), F32), part, part]


def mixer_specs(first):
    return [
        pl.BlockSpec((TOK, TILES * LANES), lambda b, *_: (b + first, 0)),
        pl.BlockSpec((TOK, 2 * LANES), lambda b, *_: (b + first, TILES // 2)),
        pl.BlockSpec((TOK, LANES), lambda b, *_: (b + first, TILES + 2)),
        pl.BlockSpec((8, TILES * LANES), lambda b, *_: (0, 0)),
        pl.BlockSpec((8, 2 * LANES), lambda b, *_: (0, TILES // 2)),
        pl.BlockSpec((8, LANES), lambda b, *_: (0, 0)),
    ]


ANY = pl.BlockSpec(memory_space=pl.ANY)


def fwd_into(bnd, *refs):
    fwd_kernel(bnd, *refs[:6], *refs[7:])


def scan_forward(bounds, proj, cw, hp, first, count, into=None):
    return pl.pallas_call(
        fwd_kernel if into is None else fwd_into,
        out_shape=jax.ShapeDtypeStruct((proj.shape[0], TILES * LANES), F32),
        grid_spec=pltpu.PrefetchScalarGridSpec(
            num_scalar_prefetch=1,
            grid=(count,),
            in_specs=mixer_specs(first) + ([] if into is None else [ANY]),
            out_specs=pl.BlockSpec((TOK, TILES * LANES), lambda b, *_: (b + first, 0)),
            scratch_shapes=block_scratch(False),
        ),
        input_output_aliases={} if into is None else {7: 0},
        compiler_params=params("arbitrary"),
        cost_estimate=cost(count * 8e9, count * 4e6),
    )(bounds[first : first + count], proj, proj, proj, cw, cw, hp, *([] if into is None else [into]))


def bwd_into(bnd, *refs):
    bwd_kernel(bnd, *refs[:8], *refs[9:])


def scan_backward(bounds, proj, cw, hp, scan, dscan, first, count, into=None):
    tile = pl.BlockSpec((TOK, TILES * LANES), lambda b, *_: (b + first, 0))
    return pl.pallas_call(
        bwd_kernel if into is None else bwd_into,
        out_shape=(
            jax.ShapeDtypeStruct((proj.shape[0], REST), BF),
            jax.ShapeDtypeStruct((8, (TILES + 2) * LANES), F32),
            jax.ShapeDtypeStruct((8, LANES), F32),
        ),
        grid_spec=pltpu.PrefetchScalarGridSpec(
            num_scalar_prefetch=1,
            grid=(count,),
            in_specs=mixer_specs(first) + [tile, tile] + ([] if into is None else [ANY]),
            out_specs=(
                pl.BlockSpec((TOK, REST), lambda b, *_: (b + first, 0)),
                pl.BlockSpec((8, (TILES + 2) * LANES), lambda b, *_: (0, 0)),
                pl.BlockSpec((8, LANES), lambda b, *_: (0, 0)),
            ),
            scratch_shapes=block_scratch(True),
        ),
        input_output_aliases={} if into is None else {9: 0},
        compiler_params=params("arbitrary"),
        cost_estimate=cost(count * 16e9, count * 6e6),
    )(
        bounds[first : first + count],
        proj, proj, proj,
        cw,
        cw,
        hp,
        scan, dscan,
        *([] if into is None else [into]),
    )


def whole_once(a):
    return pl.BlockSpec(a.shape, lambda i, *_: (0, 0), pipeline_mode=pl.Buffered(1))


def ginner_kernel(perm, gout_ref, *refs):
    pieces, (out_ref, wide_ref, gate_ref) = refs[:-3], refs[-3:]
    inner = TILES * LANES

    @pl.when(pl.program_id(0) == 0)
    def _():
        for p, piece in enumerate(pieces):
            rows = pl.ds(pl.multiple_of(perm[p] * LANES, LANES), LANES)
            for k in range(8):
                wide_ref[rows, k * 256 : (k + 1) * 256] = piece[inner + k * LANES : inner + (k + 1) * LANES, :]
            gate_ref[:, p * 256 : (p + 1) * 256] = piece[:inner, :]

    out_ref[...] = mm_nt(gout_ref[...], wide_ref[...]).astype(BF)


def inner_gradient(perm, gout, pieces):
    rows, inner = gout.shape[0], TILES * LANES
    whole = pl.BlockSpec((inner, D), lambda i, *_: (0, 0))
    return pl.pallas_call(
        ginner_kernel,
        out_shape=(jax.ShapeDtypeStruct((rows, inner), BF), jax.ShapeDtypeStruct((inner, D), BF), jax.ShapeDtypeStruct((inner, D), BF)),
        grid_spec=pltpu.PrefetchScalarGridSpec(
            num_scalar_prefetch=1,
            grid=(rows // TOK,),
            in_specs=[pl.BlockSpec((TOK, D), lambda i, *_: (i, 0))] + [whole_once(a) for a in pieces],
            out_specs=(pl.BlockSpec((TOK, inner), lambda i, *_: (i, 0)), whole, whole),
        ),
        compiler_params=params("arbitrary"),
        cost_estimate=cost(2 * rows * inner * D, 2 * (rows * D + rows * inner + 4 * inner * D)),
    )(perm, gout, *pieces)


def out_kernel(perm, inner_ref, gout_ref, out_ref, turned, result):
    @pl.when(pl.program_id(0) == 0)
    def _():
        turned[...] = inner_ref[...].T

    result[...] = mm(turned[...], gout_ref[...])
    for p in range(8):
        rows = pl.ds(pl.multiple_of(perm[p] * LANES, LANES), LANES)
        out_ref[:, p * 256 : (p + 1) * 256] = result[rows, :].astype(BF)


def out_terms(perm, inner, gout):
    rows, wide = inner.shape
    return pl.pallas_call(
        out_kernel,
        out_shape=jax.ShapeDtypeStruct((wide, D), BF),
        grid_spec=pltpu.PrefetchScalarGridSpec(
            num_scalar_prefetch=1,
            grid=(8,),
            in_specs=[
                pl.BlockSpec((rows, wide), lambda k, *_: (0, 0)),
                pl.BlockSpec((rows, 256), lambda k, *_: (0, k)),
            ],
            out_specs=pl.BlockSpec((LANES, D), lambda k, *_: (k, 0)),
            scratch_shapes=[pltpu.VMEM((wide, rows), BF), pltpu.VMEM((wide, 256), F32)],
        ),
        compiler_params=params("arbitrary", mib=48),
        cost_estimate=cost(2 * rows * wide * D, 2 * (rows * wide + rows * D + wide * D)),
    )(perm, inner, gout)


def stat_kernel(norm_ref, w_ref, scan_ref, gin_ref, gain_ref, gate_ref, out_ref):
    gate_ref[...] = mm_nt(norm_ref[...], w_ref[...]).astype(BF)
    one = two = jnp.zeros((TOK, LANES), F32)
    for t in range(TILES):
        at = slice(t * LANES, (t + 1) * LANES)
        gate = gate_ref[:, at].astype(F32)
        gated = scan_ref[:, at] * (gate * sigmoid(gate))
        one = one + gated * gated
        two = two + gated * (gin_ref[:, at].astype(F32) * gain_ref[:, at])
    a = jnp.sum(one.T, axis=0, keepdims=True)
    c = jnp.sum(two.T, axis=0, keepdims=True)
    out_ref[0] = jnp.concatenate([a, c, jnp.zeros((6, TOK), F32)], 0)


def gate_stats(normed, w_gate, scan, ginner, gain):
    rows, inner = scan.shape
    tile = pl.BlockSpec((TOK, inner), lambda b: (b, 0))
    return pl.pallas_call(
        stat_kernel,
        out_shape=(jax.ShapeDtypeStruct((rows, inner), BF), jax.ShapeDtypeStruct((rows // TOK, 8, TOK), F32)),
        grid=(rows // TOK,),
        in_specs=[
            pl.BlockSpec((TOK, D), lambda b: (b, 0)),
            pl.BlockSpec((inner, D), lambda b: (0, 0)),
            tile,
            tile,
            pl.BlockSpec((1, inner), lambda b: (0, 0)),
        ],
        out_specs=(tile, pl.BlockSpec((1, 8, TOK), lambda b: (b, 0, 0))),
        compiler_params=params("arbitrary", mib=48),
        cost_estimate=cost(2 * rows * inner * D, rows * (D * 2 + inner * 8) + inner * D * 2),
    )(normed, w_gate, scan, ginner, gain)


def gate_kernel(sum_ref, scan_ref, gate_ref, gin_ref, gain_ref, inner_ref, dgate_ref, dscan_ref, dgain_ref):
    rows = scan_ref.shape[0]

    @pl.when((pl.program_id(0) == 0) & (pl.program_id(1) == 0))
    def _():
        dgain_ref[...] = jnp.zeros_like(dgain_ref)

    r = lax.rsqrt(sum_ref[0, 0:1, :] * (1.0 / DIN) + EPSILON)
    c = r * r * sum_ref[0, 1:2, :] * (1.0 / DIN)
    rinv = jnp.broadcast_to(r, (LANES, rows)).T
    coef = jnp.broadcast_to(c, (LANES, rows)).T
    for t in range(TILES):
        at = slice(t * LANES, (t + 1) * LANES)
        gate = gate_ref[:, at].astype(F32)
        sg = sigmoid(gate)
        act = gate * sg
        scan = scan_ref[:, at]
        gain = gain_ref[:, at]
        gated = scan * act
        scaled = gated * rinv
        gin = gin_ref[:, at].astype(F32)
        inner_ref[:, at] = (scaled * gain).astype(BF)
        dgated = rinv * (gin * gain - gated * coef)
        dscan_ref[:, at] = (dgated * act).astype(BF)
        dgate_ref[:, at] = (dgated * scan * (sg + act * (1.0 - sg))).astype(BF)
        dgain_ref[0:1, at] += jnp.sum(gin * scaled, axis=0, keepdims=True)


def gate_both(sums, scan, gate, ginner, gain):
    rows, inner = scan.shape
    tile = pl.BlockSpec((Q, inner), lambda b, h: (2 * b + h, 0))
    whole = jax.ShapeDtypeStruct((rows, inner), BF)
    return pl.pallas_call(
        gate_kernel,
        out_shape=(whole, whole, whole, jax.ShapeDtypeStruct((8, inner), F32)),
        grid=(rows // TOK, 2),
        in_specs=[
            pl.BlockSpec((1, 8, Q), lambda b, h: (b, 0, h)),
            tile,
            tile,
            tile,
            pl.BlockSpec((1, inner), lambda b, h: (0, 0)),
        ],
        out_specs=(tile, tile, tile, pl.BlockSpec((8, inner), lambda b, h: (0, 0))),
        compiler_params=params("arbitrary", "arbitrary", mib=48),
        cost_estimate=cost(0, rows * inner * 14),
    )(sums, scan, gate, ginner, gain)


def back_kernel(a_ref, wa_ref, b_ref, wb_ref, norm_ref, out_ref, dgo_ref):
    @pl.when(pl.program_id(0) == 0)
    def _():
        dgo_ref[...] = jnp.zeros_like(dgo_ref)

    for c in range(4):
        at = slice(c * 512, (c + 1) * 512)
        res = mm(a_ref[...], wa_ref[:, at]) + mm(b_ref[...], wb_ref[:, at])
        out_ref[:, at] = res.astype(BF)
        dgo_ref[0:1, at] += jnp.sum(res * norm_ref[:, at].astype(F32), axis=0, keepdims=True)


def normed_gradient(gproj, w_rest, dgate, w_two, normed, first, count):
    rows, inner = dgate.shape
    row = lambda width: pl.BlockSpec((TOK, width), lambda b: (b + first, 0))
    return pl.pallas_call(
        back_kernel,
        out_shape=(jax.ShapeDtypeStruct((count * TOK, D), BF), jax.ShapeDtypeStruct((8, D), F32)),
        grid=(count,),
        in_specs=[
            row(REST),
            pl.BlockSpec((REST, D), lambda b: (0, 0)),
            row(inner),
            pl.BlockSpec((inner, D), lambda b: (0, 0)),
            row(D),
        ],
        out_specs=(pl.BlockSpec((TOK, D), lambda b: (b, 0)), pl.BlockSpec((8, D), lambda b: (0, 0))),
        compiler_params=params("arbitrary", mib=48),
        cost_estimate=cost(2 * count * TOK * D * (REST + inner), 2 * (REST + inner) * D),
    )(gproj, w_rest, dgate, w_two, normed)


def across_kernel(a_ref, b_ref, out_ref, *turned):
    if len(turned) == 2:
        (kept, turned) = turned

        @pl.when(pl.program_id(0) == 0)
        def _():
            turned[...] = a_ref[...].T
            kept[...] = turned[...]
    else:
        turned = a_ref
    out_ref[...] = mm(turned[...], b_ref[...]).astype(out_ref.dtype)


def across_rows(a, b, first, count, turn):
    rows, n = b.shape
    m = a.shape[1] if turn else a.shape[0]
    whole = pl.BlockSpec(a.shape, lambda k: (0, 0))
    part = jax.ShapeDtypeStruct((m, count * 256), BF)
    spec = pl.BlockSpec((m, 256), lambda k: (0, k))
    return pl.pallas_call(
        across_kernel,
        out_shape=(part, jax.ShapeDtypeStruct((m, rows), BF)) if turn else part,
        grid=(count,),
        in_specs=[whole, pl.BlockSpec((rows, 256), lambda k: (0, k + first))],
        out_specs=(spec, pl.BlockSpec((m, rows), lambda k: (0, 0))) if turn else spec,
        scratch_shapes=[pltpu.VMEM((m, rows), BF)] if turn else [],
        compiler_params=params("arbitrary", mib=48),
        cost_estimate=cost(2 * rows * m * 256 * count, 2 * (rows * m + rows * 256 * count + m * 256 * count)),
    )(a, b)


def pick_rest_kernel(me, *refs):
    tiles, (shared, steps, out_ref) = refs[:TILES], refs[TILES:]
    for t, ref in enumerate(tiles):
        out_ref[t * LANES : (t + 1) * LANES, :] = ref[...].astype(BF)
    wide = TILES * LANES
    out_ref[wide : wide + 2 * N, :] = shared[...].astype(BF)
    mine, head = iota((HEADS, H), 0), iota((HEADS, H), 1)
    pick = (head == 8 * (mine // 2) + 2 * me[0] + mine % 2).astype(BF)
    out_ref[wide + 2 * N :, :] = mm(pick, steps[...].astype(BF)).astype(BF)


def tile_spec(lanes, t):
    return pl.BlockSpec((LANES, lanes), lambda i, me: (4 * t + me[0], 0))


def pick_rest(me, turned):
    lanes = turned.shape[1]
    fixed = lambda rows, at: pl.BlockSpec((rows, lanes), lambda i, me: (at // rows, 0))
    return pl.pallas_call(
        pick_rest_kernel,
        out_shape=jax.ShapeDtypeStruct((REST, lanes), BF),
        grid_spec=pltpu.PrefetchScalarGridSpec(
            num_scalar_prefetch=1,
            grid=(1,),
            in_specs=[tile_spec(lanes, TILES + t) for t in range(TILES)] + [fixed(2 * N, 2 * DIN), fixed(H, 2 * DIN + 2 * N)],
            out_specs=pl.BlockSpec((REST, lanes), lambda i, me: (0, 0)),
        ),
        compiler_params=params("arbitrary"),
        cost_estimate=cost(0, 6 * REST * lanes),
    )(me, *[turned] * (TILES + 2))


def pick_two_kernel(me, *refs):
    tiles, (rows, out_ref) = refs[:TILES], refs[TILES:]
    for t, ref in enumerate(tiles):
        out_ref[t * LANES : (t + 1) * LANES, :] = ref[...].astype(BF)
    wide = TILES * LANES
    for k in range(8):
        out_ref[wide + k * LANES : wide + (k + 1) * LANES, :] = rows[:, k * 256 : (k + 1) * 256].astype(BF)


def pick_two(me, turned, out_weight):
    lanes = turned.shape[1]
    return pl.pallas_call(
        pick_two_kernel,
        out_shape=jax.ShapeDtypeStruct((2 * TILES * LANES, lanes), BF),
        grid_spec=pltpu.PrefetchScalarGridSpec(
            num_scalar_prefetch=1,
            grid=(1,),
            in_specs=[tile_spec(lanes, t) for t in range(TILES)] + [pl.BlockSpec((LANES, D), lambda i, me: (me[0], 0))],
            out_specs=pl.BlockSpec((2 * TILES * LANES, lanes), lambda i, me: (0, 0)),
        ),
        compiler_params=params("arbitrary"),
        cost_estimate=cost(0, 12 * TILES * LANES * lanes),
    )(me, *[turned] * TILES, out_weight)


def pick_gate_kernel(me, *refs):
    for t, ref in enumerate(refs[:-1]):
        refs[-1][t * LANES : (t + 1) * LANES, :] = ref[...].astype(BF)


def pick_gate(me, turned):
    lanes = turned.shape[1]
    return pl.pallas_call(
        pick_gate_kernel,
        out_shape=jax.ShapeDtypeStruct((TILES * LANES, lanes), BF),
        grid_spec=pltpu.PrefetchScalarGridSpec(
            num_scalar_prefetch=1,
            grid=(1,),
            in_specs=[tile_spec(lanes, t) for t in range(TILES)],
            out_specs=pl.BlockSpec((TILES * LANES, lanes), lambda i, me: (0, 0)),
        ),
        compiler_params=params("arbitrary"),
        cost_estimate=cost(0, 6 * TILES * LANES * lanes),
    )(me, *[turned] * TILES)


STEP = 128


def norm_kernel(perm, tok_ref, gain_ref, out_ref):
    x = tok_ref[...].astype(F32)
    inv = lax.rsqrt(jnp.mean(x * x, axis=1, keepdims=True) + EPSILON)
    wide = D // 8
    for k in range(8):
        here = pl.ds(pl.multiple_of(perm[k] * wide, wide), wide)
        out_ref[:, k * wide : (k + 1) * wide] = (
            tok_ref[:, here].astype(F32) * inv * gain_ref[:, here]
        ).astype(BF)


def norm_rows(perm, tokens, gain):
    rows = tokens.shape[0]
    row = pl.BlockSpec((STEP, D), lambda i, *_: (i, 0))
    return pl.pallas_call(
        norm_kernel,
        out_shape=jax.ShapeDtypeStruct((rows, D), BF),
        grid_spec=pltpu.PrefetchScalarGridSpec(
            num_scalar_prefetch=1,
            grid=(rows // STEP,),
            in_specs=[row, pl.BlockSpec((1, D), lambda i, *_: (0, 0))],
            out_specs=row,
        ),
        compiler_params=params("arbitrary"),
        cost_estimate=pl.CostEstimate(flops=0, bytes_accessed=rows * D * 4, transcendentals=0),
    )(perm, tokens, gain)


def last_kernel(perm, tok_ref, cot_ref, keep_ref, gain_ref, one_ref, two_ref, three_ref, out_ref, grad):
    wide = D // 8
    for k in range(8):
        here = pl.ds(pl.multiple_of(perm[k] * wide, wide), wide)
        at = slice(k * wide, (k + 1) * wide)
        grad[:, here] = (
            one_ref[:, at].astype(F32) + two_ref[:, at].astype(F32) + three_ref[:, at].astype(F32)
        ) * gain_ref[:, here]
    x = tok_ref[...].astype(F32)
    inv = lax.rsqrt(jnp.mean(x * x, axis=1, keepdims=True) + EPSILON)
    g = grad[...]
    dot = jnp.mean(g * x, axis=1, keepdims=True)
    out_ref[...] = inv * (g - x * (inv * inv * dot)) + keep_ref[...] * cot_ref[...].astype(F32)


def last_rows(perm, tokens, cotangent, keep, gain, parts):
    rows = tokens.shape[0]
    row = pl.BlockSpec((STEP, D), lambda i, *_: (i, 0))
    return pl.pallas_call(
        last_kernel,
        out_shape=jax.ShapeDtypeStruct((rows, D), F32),
        grid_spec=pltpu.PrefetchScalarGridSpec(
            num_scalar_prefetch=1,
            grid=(rows // STEP,),
            in_specs=[
                row,
                row,
                pl.BlockSpec((STEP, 1), lambda i, *_: (i, 0)),
                pl.BlockSpec((1, D), lambda i, *_: (0, 0)),
                row,
                row,
                row,
            ],
            out_specs=row,
            scratch_shapes=[pltpu.VMEM((STEP, D), F32)],
        ),
        compiler_params=params("arbitrary"),
        cost_estimate=pl.CostEstimate(flops=0, bytes_accessed=rows * D * 14, transcendentals=0),
    )(perm, tokens, cotangent, keep, gain, *parts)


def first_join_kernel(me, *refs):
    pieces, (out_ref, grad_ref, stage, sem) = refs[:4], refs[4:]
    inner = TILES * LANES
    for k in range(4):
        q = jnp.bitwise_xor(me[0], k)
        for t in range(TILES):
            rows = pl.ds(pl.multiple_of((4 * t + q) * LANES, LANES), LANES)
            stage[rows, :] = pieces[k][t * LANES : (t + 1) * LANES, :].astype(F32)
    copy = pltpu.make_async_copy(stage, out_ref.at[pl.ds(0, 4 * inner)], sem)
    copy.start()
    for k in range(4):
        q = jnp.bitwise_xor(me[0], k)
        rows = pl.ds(pl.multiple_of(q * LANES, LANES), LANES)
        for c in range((pieces[k].shape[0] - inner) // LANES):
            grad_ref[rows, c * 256 : (c + 1) * 256] = pieces[k][
                inner + c * LANES : inner + (c + 1) * LANES, :
            ].astype(F32)
    copy.wait()


def first_join(me, pieces, width):
    lanes = pieces[0].shape[1]
    whole = pl.BlockSpec(pieces[0].shape, lambda i, *_: (0, 0))
    return pl.pallas_call(
        first_join_kernel,
        out_shape=(
            jax.ShapeDtypeStruct((width, lanes), F32),
            jax.ShapeDtypeStruct((4 * LANES, D), F32),
        ),
        grid_spec=pltpu.PrefetchScalarGridSpec(
            num_scalar_prefetch=1,
            grid=(1,),
            in_specs=[whole] * 4,
            out_specs=(ANY, pl.BlockSpec((4 * LANES, D), lambda i, *_: (0, 0))),
            scratch_shapes=[pltpu.VMEM((4 * TILES * LANES, lanes), F32), pltpu.SemaphoreType.DMA],
        ),
        compiler_params=params("arbitrary", mib=48),
        cost_estimate=cost(0, 20e6),
    )(me, *pieces)


def last_join_kernel(me, one, two, three, four, into, out_ref, stage, sem):
    pieces = (one, two, three, four)
    inner = TILES * LANES
    few = H // 4
    for k in range(4):
        q = jnp.bitwise_xor(me[0], k)
        for t in range(TILES):
            rows = pl.ds(pl.multiple_of((4 * t + q) * LANES, LANES), LANES)
            stage[rows, :] = pieces[k][t * LANES : (t + 1) * LANES, :].astype(F32)
    stage[4 * inner : 4 * inner + 2 * N, :] = sum(p[inner : inner + 2 * N, :].astype(F32) for p in pieces)
    steps = None
    for k in range(4):
        q = jnp.bitwise_xor(me[0], k)
        head, mine = iota((H, few), 0), iota((H, few), 1)
        spread = (head == 8 * (mine // 2) + 2 * q + mine % 2).astype(BF)
        term = mm(spread, pieces[k][inner + 2 * N :, :])
        steps = term if steps is None else steps + term
    stage[4 * inner + 2 * N :, :] = steps
    copy = pltpu.make_async_copy(stage, out_ref.at[pl.ds(4 * inner, stage.shape[0])], sem)
    copy.start()
    copy.wait()


def last_join(me, pieces, into):
    lanes = pieces[0].shape[1]
    whole = pl.BlockSpec(pieces[0].shape, lambda i, *_: (0, 0))
    return pl.pallas_call(
        last_join_kernel,
        out_shape=jax.ShapeDtypeStruct(into.shape, F32),
        grid_spec=pltpu.PrefetchScalarGridSpec(
            num_scalar_prefetch=1,
            grid=(1,),
            in_specs=[whole] * 4 + [ANY],
            out_specs=ANY,
            scratch_shapes=[pltpu.VMEM((into.shape[0] - 4 * TILES * LANES, lanes), F32), pltpu.SemaphoreType.DMA],
        ),
        input_output_aliases={5: 0},
        compiler_params=params("arbitrary"),
        cost_estimate=cost(0, 8e6),
    )(me, *pieces, into)


def tie(*arrays):
    return lax.optimization_barrier(arrays)


def swap(x, d):
    return lax.ppermute(x, "rep", [(i, i ^ d) for i in range(4)])


def fw(x):
    return lax.ppermute(x, "shard", [(RING[i], RING[(i + 1) % 8]) for i in range(8)])


def bw(x):
    return lax.ppermute(x, "shard", [(RING[(i + 1) % 8], RING[i]) for i in range(8)])


def relative(s, n):
    if n != 8:
        return jnp.arange(8, dtype=jnp.int32), jnp.arange(8, dtype=jnp.int32)
    table, inverse = [], []
    for shard in range(8):
        p = RING.index(shard)
        row = [RING[(p + d) % 8] for d in (0, -1, 1, -2, 2, -3, 3, 4)]
        table.append(row)
        inverse.append([row.index(i) for i in range(8)])
    return jnp.asarray(table, jnp.int32)[s], jnp.asarray(inverse, jnp.int32)[s]


def cut(rows):
    return -(-rows // 32) * 16


def ring_pieces(piece, pieces):
    half = cut(piece.shape[0])
    a = b = piece
    pieces.append(piece)
    for _ in range(3):
        a, b = yield fw(a), bw(b)
        pieces += [a, b]
    a, b = yield fw(a[:half]), bw(b[half:])
    pieces.append(jnp.concatenate([a, b], 0))
    yield


def add16(a, b):
    return (a.astype(F32) + b.astype(F32)).astype(BF)


def ring_sum():
    far = yield
    half = cut(far.shape[0])
    rf, rb, (own, f1, b1, f2, b2, f3, b3) = yield far[:half], far[half:]
    sf = jnp.concatenate([add16(b3[:half], rf), b3[half:]], 0)
    sb = jnp.concatenate([f3[:half], add16(f3[half:], rb)], 0)
    rf, rb = yield sf, sb
    rf, rb = yield add16(b2, rf), add16(f2, rb)
    rf, rb = yield add16(b1, rf), add16(f1, rb)
    yield (own.astype(F32) + rf.astype(F32) + rb.astype(F32)).astype(BF)


def launch(steps, arrived, *others):
    forward, backward, *others = tie(*steps.send(arrived), *others)
    return [fw(forward), bw(backward)], *others


def blocks_of(x):
    return [x[k * TOK : (k + 1) * TOK] for k in range(4)]


def sum_rep(parts):
    far = swap(parts[3], 1)
    chip = swap((parts[2].astype(F32) + far.astype(F32)).astype(BF), 2)
    return parts[0].astype(F32) + swap(parts[1], 1).astype(F32) + chip.astype(F32)


def shards(n, tokens, cotangent, lengths, order, mask, in_weight, out_weight, conv_weight, conv_bias, dt_bias,
           a_log, skip_gain, gain_outer, gain_inner):
    r, s = lax.axis_index("rep"), lax.axis_index("shard")
    ring = n == 8
    inner_width = TILES * LANES
    perm, place = relative(s, n)
    keep = mask.astype(F32)[:, None]
    catalog = jnp.arange(lengths.shape[0], dtype=jnp.int32)
    picked = jnp.sum(jnp.where(order[:, None] == catalog[None, :], lengths[None, :], 0), axis=1)
    bounds = jnp.stack([picked[0], picked[0] + picked[1]])[None, :]
    bounds = jnp.concatenate([bounds, swap(bounds, 1), swap(bounds, 2), swap(bounds, 3)], 0)

    turned = in_weight.T
    me = r[None]
    rest = pick_rest(me, turned)
    normed = norm_rows(perm, tokens, gain_outer[None, :])
    gout = (cotangent.astype(F32) * keep).astype(BF)

    def own_lanes(v, width):
        v = lax.dynamic_index_in_dim(v.reshape(v.shape[:-1] + (TILES, 4, width)), r, v.ndim, False)
        return v.reshape(v.shape[:-2] + (TILES * width,))

    heads = H // 4
    skip = jnp.broadcast_to(skip_gain[:, None], (H, P_SIZE)).reshape(1, DIN)
    rows8 = jnp.concatenate(
        [conv_weight, conv_bias[None], jnp.pad(skip, ((0, 0), (0, 2 * N))), jnp.zeros((2, CONVCH), F32)], 0
    )
    cw = jnp.concatenate([own_lanes(rows8[:, :DIN], LANES), rows8[:, DIN:]], 1)
    hp = jnp.stack([own_lanes(dt_bias, 2), own_lanes(-jnp.exp(a_log), 2)])
    hp = jnp.pad(hp, ((0, 6), (0, LANES - heads)))
    gain = own_lanes(gain_inner, LANES)[None, :]

    if ring:
        pieces = []
        steps = ring_pieces(rest, pieces)
        sent = next(steps)
        core, chip = swap(normed, 1), swap(normed, 2)
        two = pick_two(me, turned, out_weight)
        *sent, core, two = tie(*sent, core, two)
        sent = steps.send(sent)
        *sent, gout = tie(*sent, gout)
        sent = steps.send(sent)
        sent = steps.send(tie(*sent))
        *sent, chip, two = tie(*sent, chip, two)
        steps.send(sent)
        rest_pieces = pieces

        pieces = []
        steps = ring_pieces(two, pieces)
        sent = next(steps)
        far, gchip, gcore = swap(chip, 1), swap(gout, 2), swap(gout, 1)
        w_rest = jnp.concatenate(rest_pieces, 1)
        all_normed = jnp.concatenate([normed, core, chip, far], 0)
        all_normed, w_rest = tie(all_normed, w_rest)
        proj = mm_nt(all_normed, w_rest).astype(BF)
        *sent, proj = tie(*sent, proj)
        sent = steps.send(sent)
        scan = scan_forward(bounds, proj, cw, hp, 0, 2)
        *sent, scan, gchip, gcore = tie(*sent, scan, gchip, gcore)
        sent = steps.send(sent)
        gfar = swap(gchip, 1)
        scan = scan_forward(bounds, proj, cw, hp, 2, 2, scan)
        *sent, scan, gfar = tie(*sent, scan, gfar)
        sent = steps.send(sent)
        all_gout = jnp.concatenate([gout, gcore, gchip, gfar], 0)
        *sent, all_gout = tie(*sent, all_gout)
        steps.send(sent)
        ginner, w_out, w_two = inner_gradient(perm, all_gout, pieces)
    else:
        everyone = lambda x: [x, swap(x, 1), swap(x, 2), swap(x, 3)]
        w_rest = lax.all_gather(rest, "shard", axis=1, tiled=True)
        w_two = lax.all_gather(pick_gate(me, turned), "shard", axis=1, tiled=True)
        w_out = lax.all_gather(out_weight.astype(BF), "shard", axis=0, tiled=True)
        w_out = lax.dynamic_index_in_dim(w_out.reshape(TILES, 4, LANES, D), r, 1, False).reshape(inner_width, D)
        all_normed = jnp.concatenate(everyone(normed), 0)
        all_gout = jnp.concatenate(everyone(gout), 0)
        proj = mm_nt(all_normed, w_rest).astype(BF)
        scan = scan_forward(bounds, proj, cw, hp, 0, 4)
        ginner = mm_nt(all_gout, w_out).astype(BF)

    gate, sums = gate_stats(all_normed, w_two, scan, ginner, gain)
    there = [swap(sums, d) for d in (1, 2, 3)]
    sums = jnp.stack([sums[k] + there[0][k ^ 1] + there[1][k ^ 2] + there[2][k ^ 3] for k in range(4)])
    inner, dgate, dscan, dgain = gate_both(sums, scan, gate, ginner, gain)

    def columns_of(x):
        return [x[:, k * 256 : (k + 1) * 256] for k in range(x.shape[1] // 256)]

    at_r = (jnp.arange(4) == r).astype(F32)
    sizes = [4 * CONVCH, CONVCH, H, H, H, D, DIN]

    def all_lanes(v, width):
        v = v.reshape(v.shape[:-1] + (TILES, 1, width)) * at_r[:, None]
        return v.reshape(v.shape[:-3] + (TILES * 4 * width,))

    def small_vector(dcw, dhp, dgo, dgain):
        wide = jnp.concatenate([all_lanes(dcw[:5, :inner_width], LANES), dcw[:5, inner_width:]], 1)
        dskip = jnp.sum(dcw[5, :inner_width].reshape(heads, P_SIZE), axis=1)
        dgo = dgo[0].reshape(8, D // 8)[place].reshape(D) / gain_outer
        parts = [
            wide.reshape(-1),
            all_lanes(dhp[0, :heads], 2),
            all_lanes(dhp[1, :heads], 2),
            all_lanes(dskip, 2),
            dgo,
            all_lanes(dgain[0], LANES),
        ]
        flat = jnp.concatenate(parts)
        return jnp.pad(flat, (0, -flat.shape[0] % 1024)).reshape(-1, LANES)

    width = in_weight.shape[1]
    final = functools.partial(normed_gradient, w_rest=w_rest, dgate=dgate, w_two=w_two, normed=all_normed)
    if ring:
        outs = columns_of(out_terms(perm, inner, all_gout))
        (dgate, _) = tie(dgate, outs[7])
        terms8 = columns_of(across_rows(dgate, all_normed, 0, 8, True)[0])
        terms8 = [jnp.concatenate(p, 0) for p in zip(terms8, outs)]
        steps = ring_sum()
        next(steps)
        sent, inner, dscan = launch(steps, terms8[7], inner, dscan)
        back = functools.partial(scan_backward, bounds, proj, cw, hp, scan)
        branch = mm(inner, w_out).astype(BF)
        *sent, branch = tie(*sent, branch)
        b0, b1, b2, b3 = blocks_of(branch)
        sent, dscan, b3 = launch(steps, (*sent, terms8[:7]), dscan, b3)
        far = swap(b3, 1)
        gproj, dcw, dhp = back(dscan, 2, 2)
        *sent, gproj, far = tie(*sent, gproj, far)
        sent, gproj, chip = launch(steps, sent, gproj, add16(b2, far))
        core, chip = swap(b1, 1), swap(chip, 2)
        grad3, dgo = final(gproj, first=3, count=1)
        (gproj, grad3) = tie(gproj, grad3)
        far = swap(grad3, 1)
        gproj, d, e = back(dscan, 0, 1, gproj)
        dcw, dhp = dcw + d, dhp + e
        *sent, gproj, core, far = tie(*sent, gproj, core, far)
        sent, gproj = launch(steps, sent, gproj)
        grad2, d = final(gproj, first=2, count=1)
        dgo = dgo + d
        (gproj, total) = tie(gproj, add16(grad2, far))
        gproj, d, e = back(dscan, 1, 1, gproj)
        dcw, dhp = dcw + d, dhp + e
        *sent, gproj, chip = tie(*sent, gproj, chip)
        share, gproj = tie(steps.send(sent), gproj)
        branch = (b0, core, chip)
        upper = swap(total[: TOK // 2], 2)

        far, turned_proj = across_rows(gproj, all_normed, 7, 1, True)
        steps = ring_sum()
        next(steps)
        sent, turned_proj = launch(steps, far, turned_proj)
        gates = [share, swap(share, 1)]
        seven = across_rows(turned_proj, all_normed, 0, 7, False)
        *sent, seven, gproj, upper, lower, share = tie(*sent, seven, gproj, upper, total[TOK // 2 :], share)
        sent, gproj, lower = launch(steps, (*sent, columns_of(seven)), gproj, lower)
        lower = swap(lower, 2)
        early, d = final(gproj, first=0, count=2)
        dgo = dgo + d
        *sent, early, lower, share = tie(*sent, early, lower, share)
        sent, early, share, dgo = launch(steps, sent, early, share, dgo)
        gates.append(swap(share, 2))
        core = swap(early[TOK:], 1)
        small = small_vector(dcw, dhp, dgo, dgain)
        bits = [1 << k for k in range(n.bit_length() - 1)]
        flip = lambda v, d: v + lax.ppermute(v, "shard", [(i, i ^ d) for i in range(n)])
        small = small + swap(small, 1)
        small = flip(small, bits[0])
        layer_out = (keep * (tokens.astype(F32) + sum(b.astype(F32) for b in branch))).astype(BF)
        *sent, core, layer_out, small = tie(*sent, core, layer_out, small)
        sent, core, small = launch(steps, sent, core, small)
        small = flip(small, bits[1])
        parts = [early[:TOK], core, jnp.concatenate([upper, lower], 0)]
        grad_tokens = last_rows(perm, tokens, cotangent, keep, gain_outer[None, :], parts)
        *sent, gates[2], grad_tokens, small = tie(*sent, gates[2], grad_tokens, small)
        share, small, gates[2] = tie(steps.send(sent), small, gates[2])
        rests = [share, swap(share, 1), swap(share, 2)]
        gates.append(swap(gates[2], 1))
        grad_in, grad_out_weight = first_join(me, gates, width)
        for d in bits[2:]:
            small = flip(small, d)
        small = small + swap(small, 2)
        rests.append(swap(rests[2], 1))
    else:
        rows_sum = lambda x, axis: lax.psum_scatter(
            x.astype(F32), "shard", scatter_dimension=axis, tiled=True
        ).astype(BF)
        branch = sum_rep(blocks_of(mm(inner, w_out).astype(BF)))
        gproj, dcw, dhp = scan_backward(bounds, proj, cw, hp, scan, dscan, 0, 4)
        layer_out = (keep * (tokens.astype(F32) + branch.astype(F32))).astype(BF)
        gnormed, dgo = final(gproj, first=0, count=4)
        total = sum_rep(blocks_of(gnormed)).astype(BF)
        grad_tokens = last_rows(
            perm, tokens, cotangent, keep, gain_outer[None, :], [total, jnp.zeros_like(total), jnp.zeros_like(total)]
        )
        grad_out = lax.dot_general(inner, all_gout, TN, preferred_element_type=F32)
        spread = grad_out.reshape(TILES, 1, LANES, D).astype(F32) * (jnp.arange(4)[None, :, None, None] == r)
        spread = lax.psum_scatter(spread.reshape(DIN, D), "shard", scatter_dimension=0, tiled=True)
        grad_out_weight = lax.psum(spread, "rep")
        gates = everyone(rows_sum(across_rows(dgate, all_normed, 0, 8, True)[0], 1))
        rests = everyone(rows_sum(across_rows(gproj, all_normed, 0, 8, True)[0], 1))
        grad_in, _ = first_join(me, gates, width)
        small = lax.psum(small_vector(dcw, dhp, dgo, dgain), ("rep", "shard"))
    grad_in_weight = last_join(me, rests, grad_in).T

    small = small.reshape(-1)
    ends = [sum(sizes[: i + 1]) for i in range(len(sizes))]
    g_cw, g_cb, g_db, g_al, g_sk, g_go, g_gi = [small[e - z : e] for e, z in zip(ends, sizes)]
    return (
        layer_out,
        grad_tokens,
        grad_in_weight,
        grad_out_weight,
        g_cw.reshape(4, CONVCH),
        g_cb,
        g_db,
        g_al,
        g_sk,
        g_go,
        g_gi,
    )


def solution(mesh):
    rows = P(("rep", "shard"), None)
    vector = P(("rep", "shard"))
    owned = P("shard", None)
    return jax.shard_map(
        functools.partial(shards, mesh.shape["shard"]),
        mesh=mesh,
        in_specs=(rows, rows, P(), vector, vector, owned, owned) + (P(),) * 7,
        out_specs=(rows, rows, owned, owned) + (P(),) * 7,
        check_vma=False,
    )
```

```python
import functools

import jax
import jax.numpy as jnp
from jax import lax
from jax.experimental import pallas as pl
from jax.experimental.pallas import tpu as pltpu
from jax.sharding import PartitionSpec as P

D = 2048
DIN = 4096
P_SIZE = 64
N = 128
Q = 256
H = 64
CONVCH = DIN + 2 * N
EPSILON = 1e-05
LOG2E = 1.4426950408889634
LANES = 128
TOK = 512
TILES = DIN // 128 // 4
HEADS = H // 4
REST = TILES * 128 + 2 * N + H // 4
HIGHEST = lax.Precision.HIGHEST
BF = jnp.bfloat16
F32 = jnp.float32
NT = (((1,), (1,)), ((), ()))
TN = (((0,), (0,)), ((), ()))
RING = (0, 2, 4, 6, 7, 5, 3, 1)


def mm(a, b):
    return jnp.dot(a, b, preferred_element_type=F32)


def mm_nt(a, b):
    return lax.dot_general(a, b, NT, preferred_element_type=F32)


def iota(shape, dim):
    return lax.broadcasted_iota(jnp.int32, shape, dim)


def start_of(rows, b1, b2):
    return jnp.where(rows >= b2, b2, jnp.where(rows >= b1, b1, 0))


def sigmoid(v):
    return 0.5 * jnp.tanh(0.5 * v) + 0.5


def conv_pre(x, taps, bias, lk):
    pre = bias + taps[3] * x
    for k in range(1, 4):
        pre = pre + taps[3 - k] * (pltpu.roll(x, k, 0) * lk[k - 1])
    return pre


def taps_of(cw_ref, lanes):
    return [cw_ref[k : k + 1, lanes] for k in range(4)], cw_ref[4:5, lanes]


def terms(v, count):
    out = []
    for _ in range(count):
        out.append(v.astype(BF).astype(F32))
        v = v - out[-1]
    return out


def side_by_side(parts):
    return sum(pltpu.roll(p, HEADS * i, 1) if i else p for i, p in enumerate(parts))


def prepare(b1, b2, bc_ref, dt_ref, cwb_ref, hp_ref, lk, score, bmat, cmat, btrans, ctrans,
            dts, sig, late, early, expand, transposed):
    rows = iota((TOK, LANES), 0)
    lane = iota((TOK, LANES), 1)
    pos = rows - start_of(rows, b1, b2)
    for k in range(1, 4):
        lk[k - 1] = (pos >= k).astype(F32)
    links = [lk[0], lk[1], lk[2]]
    for half, keep in ((0, bmat), (1, cmat)):
        lanes = slice(half * LANES, (half + 1) * LANES)
        taps, bias = taps_of(cwb_ref, lanes)
        pre = conv_pre(bc_ref[:, lanes].astype(F32), taps, bias, links)
        act = pre * sigmoid(pre)
        keep[...] = act.astype(BF)
        if half == 0:
            btrans[...] = act[:Q].T.astype(BF)
        elif ctrans is not None:
            ctrans[...] = act[Q:].T.astype(BF)
    for c in range(2):
        part = slice(c * Q, (c + 1) * Q)
        if transposed:
            s = mm_nt(bmat[part, :], cmat[part, :])
        else:
            s = mm_nt(cmat[part, :], bmat[part, :])
        score[c] = jnp.where(allowed(c, b1, b2, transposed), s, 0.0)
    real = lane < HEADS
    raw = jnp.where(real, dt_ref[...].astype(F32), 0.0) + hp_ref[0:1, :]
    step = jnp.where(real, jnp.maximum(raw, 0.0) + jnp.log1p(jnp.exp(-jnp.abs(raw))), 0.0)
    if dts is not None:
        dts[...] = step
        sig[...] = sigmoid(raw)
    decay = step * (hp_ref[1:2, :] * LOG2E)
    lower = (iota((Q, Q), 0) >= iota((Q, Q), 1)).astype(F32)
    sums = [
        jnp.dot(lower, decay[c * Q : (c + 1) * Q], precision=HIGHEST, preferred_element_type=F32) for c in range(2)
    ]
    last = start_of(Q - 1, b1, b2)
    out = jnp.where(rows[:Q] >= last, jnp.exp2(sums[0][Q - 1 : Q, :] - sums[0]), 0.0)
    into = jnp.where(start_of(rows[Q:], b1, b2) <= Q - 1, jnp.exp2(sums[1]), 0.0)
    middle = jnp.where(real, jnp.concatenate([out, into], 0), 0.0)
    expand[...] = side_by_side(terms(step, 2) + terms(middle, 2)).astype(BF)
    split = side_by_side(terms(jnp.concatenate(sums, 0), 3))
    used = lane % 64 < 3 * HEADS
    late[...] = jnp.where(used & (lane >= 64), 1.0, split).astype(BF)
    early[...] = jnp.where(used & (lane < 64), 1.0, pltpu.roll(-split, 64, 1)).astype(BF)


def both_heads(v, t):
    lane = iota(v.shape, 1) % HEADS
    zero = jnp.zeros_like(v)
    return jnp.concatenate([jnp.where(lane == 2 * t, v, zero), jnp.where(lane == 2 * t + 1, v, zero)], 0)


def spread_over(expand, t):
    row, col = iota((LANES, 2 * LANES), 0), iota((LANES, 2 * LANES), 1)
    head = 2 * t + (col % LANES) // P_SIZE
    pick = (row % HEADS == head) & (row // (2 * HEADS) == col // LANES)
    both = mm(expand[...], pick.astype(BF))
    return both[:, :LANES], both[:, LANES:]


def allowed(c, b1, b2, transposed):
    late = iota((Q, Q), 1 if transposed else 0) + c * Q
    early = iota((Q, Q), 0 if transposed else 1) + c * Q
    return (early <= late) & (early >= start_of(late, b1, b2))


def fwd_kernel(bnd, xs_ref, bc_ref, dt_ref, cwx_ref, cwb_ref, hp_ref, out_ref,
               lk, score, bmat, cmat, btrans, late, early, expand):
    b = pl.program_id(0)
    prepare(bnd[b, 0], bnd[b, 1], bc_ref, dt_ref, cwb_ref, hp_ref, lk, score, bmat, cmat,
            btrans, None, None, None, late, early, expand, False)
    for t in range(TILES):
        fwd_tile(t, slice(t * LANES, (t + 1) * LANES), xs_ref, cwx_ref, out_ref,
                 lk, score, cmat, btrans, late, early, expand)


def fwd_tile(t, at, xs_ref, cwx_ref, out_ref, lk, score, cmat, btrans, late, early, expand):
    taps, bias = taps_of(cwx_ref, at)
    pre = conv_pre(xs_ref[:, at].astype(F32), taps, bias, [lk[0], lk[1], lk[2]])
    x = pre * sigmoid(pre)
    first = iota((TOK, LANES), 1) < P_SIZE
    dtx, middle = spread_over(expand, t)
    xt = x * dtx
    xt16 = xt.astype(BF)
    half = Q // 2
    outs = []
    for c in range(2):
        o = c * Q
        for rows, width in ((slice(o, o + half), half), (slice(o + half, o + Q), Q)):
            last = rows.stop - o
            w = mm_nt(both_heads(late[rows, :], t), early[o : o + width, :])
            s = score[c, last - half : last, :width]
            w = jnp.exp2(jnp.minimum(w, 0.0)) * jnp.concatenate([s, s], 0)
            y = mm(w.astype(BF), xt16[o : o + width])
            outs.append(jnp.where(first[:half], y[:half], y[half:]))
    outs = [jnp.concatenate(outs[:2], 0), jnp.concatenate(outs[2:], 0)]
    state = mm(btrans[...], (middle[:Q] * xt[:Q]).astype(BF))
    outs[1] = outs[1] + mm(cmat[Q:, :], state.astype(BF)) * middle[Q:]
    skip = cwx_ref[5:6, at]
    out_ref[:, at] = jnp.concatenate(outs, 0) + skip * x


def conv_back(dact, pre, sg, xin, taps, links):
    dpre = dact * (sg * (1.0 + pre * (1.0 - sg)))
    g = taps[3] * dpre
    sums = [None] * 5
    sums[3] = jnp.sum(dpre * xin, axis=0, keepdims=True)
    sums[4] = jnp.sum(dpre, axis=0, keepdims=True)
    for k in range(1, 4):
        q = links[k - 1] * dpre
        g = g + taps[3 - k] * pltpu.roll(q, TOK - k, 0)
        sums[3 - k] = jnp.sum(q * pltpu.roll(xin, k, 0), axis=0, keepdims=True)
    return g, sums


def bwd_tile(t, at, xs_ref, cwx_ref, scan_ref, dscan_ref, out_ref, dcw_ref,
             lk, score, bmat, btrans, ctrans, late, early, expand, dscore, rsum, rsum3, dball, dcall):
    taps, bias = taps_of(cwx_ref, at)
    links = [lk[0], lk[1], lk[2]]
    xin = xs_ref[:, at].astype(F32)
    pre = conv_pre(xin, taps, bias, links)
    sg = sigmoid(pre)
    x = pre * sg
    first = iota((TOK, LANES), 1) < P_SIZE
    dtx, middle = spread_over(expand, t)
    xt = x * dtx
    xt16 = xt.astype(BF)
    xtf = xt16.astype(F32)
    skip = cwx_ref[5:6, at]
    dy16 = dscan_ref[:, at]
    dy = dy16.astype(F32)
    dyf = dy
    zero = jnp.zeros((Q // 2, LANES), BF)
    half = Q // 2
    parts = []
    for c in range(2):
        o = c * Q
        for rows, begin in ((slice(o, o + half), 0), (slice(o + half, o + Q), half)):
            at_row = slice(begin, begin + half)
            later = slice(o + begin, o + Q)
            w = jnp.exp2(jnp.minimum(mm_nt(both_heads(early[rows, :], t), late[later, :]), 0.0))
            xr = xt16[rows]
            xr = jnp.concatenate([jnp.where(first[:half], xr, zero), jnp.where(first[:half], zero, xr)], 0)
            wp = w * mm_nt(xr, dy16[later])
            dscore[c, at_row, begin:] += wp[:half] + wp[half:]
            s = score[c, at_row, begin:]
            y = mm((w * jnp.concatenate([s, s], 0)).astype(BF), dy16[later])
            parts.append(jnp.where(first[:half], y[:half], y[half:]))
    parts = [jnp.concatenate(parts[:2], 0), jnp.concatenate(parts[2:], 0)]
    tx, ex = middle[:Q], middle[Q:]
    txt16 = (tx * xt[:Q]).astype(BF)
    state = mm(btrans[...], txt16).astype(BF)
    dye = (ex * dy[Q:]).astype(BF)
    dstate = mm(ctrans[...], dye).astype(BF)
    dcall[...] += mm_nt(dye, state)
    dball[...] += mm_nt(txt16, dstate)
    across = tx * mm(bmat[:Q, :], dstate)
    within = jnp.concatenate(parts, 0)
    dxt = jnp.concatenate([parts[0] + across, parts[1]], 0)
    r1 = dyf * (scan_ref[:, at] - skip * x) - xtf * within
    r2 = x * dxt
    r3 = xtf[:Q] * across

    hi = r1.astype(BF)
    row, col = iota((2 * LANES, LANES), 0), iota((2 * LANES, LANES), 1)
    pick = (col == 2 * t + (row % LANES) // P_SIZE).astype(BF)
    rsum[...] += mm(jnp.concatenate([hi, (r1 - hi.astype(F32)).astype(BF)], 1), pick)
    row, col = iota((2 * LANES, 2 * LANES), 0), iota((2 * LANES, 2 * LANES), 1)
    pick = ((col % LANES == 2 * t + (row % LANES) // P_SIZE) & (row // LANES == col // LANES)).astype(BF)
    r3 = jnp.concatenate([r3, jnp.zeros_like(r3)], 0)
    rsum3[...] += mm(jnp.concatenate([r2.astype(BF), r3.astype(BF)], 1), pick)
    g, sums = conv_back(dxt * dtx + skip * dy, pre, sg, xin, taps, links)
    sums.append(jnp.sum(dy * x, axis=0, keepdims=True))
    sums.append(jnp.zeros((2, LANES), F32))
    out_ref[:, at] = g.astype(BF)
    dcw_ref[:, at] += jnp.concatenate(sums, 0)


def bwd_kernel(bnd, xs_ref, bc_ref, dt_ref, cwx_ref, cwb_ref, hp_ref, scan_ref, dscan_ref,
               out_ref, dcw_ref, dhp_ref,
               lk, score, bmat, cmat, btrans, late, early, expand, ctrans, dts, sig, dscore, rsum, rsum3, dball, dcall):
    b = pl.program_id(0)
    b1, b2 = bnd[b, 0], bnd[b, 1]

    @pl.when(b == 0)
    def _():
        dcw_ref[...] = jnp.zeros_like(dcw_ref)
        dhp_ref[...] = jnp.zeros_like(dhp_ref)

    prepare(b1, b2, bc_ref, dt_ref, cwb_ref, hp_ref, lk, score, bmat, cmat,
            btrans, ctrans, dts, sig, late, early, expand, True)
    for v in (dscore, rsum, rsum3, dball, dcall):
        v[...] = jnp.zeros_like(v)
    for t in range(TILES):
        bwd_tile(t, slice(t * LANES, (t + 1) * LANES), xs_ref, cwx_ref, scan_ref, dscan_ref, out_ref, dcw_ref,
                 lk, score, bmat, btrans, ctrans, late, early, expand, dscore, rsum, rsum3, dball, dcall)
    links = [lk[0], lk[1], lk[2]]

    db, dc = [], []
    for c in range(2):
        part = slice(c * Q, (c + 1) * Q)
        ds = jnp.where(allowed(c, b1, b2, True), dscore[c], 0.0)
        db.append(mm(ds.astype(BF), cmat[part, :]))
        dc.append(mm(ds.T.astype(BF), bmat[part, :]))
    db[0] = db[0] + dball[...]
    dc[1] = dc[1] + dcall[...]
    base = TILES * LANES
    for i, dact in enumerate((jnp.concatenate(db, 0), jnp.concatenate(dc, 0))):
        lanes = slice(i * LANES, (i + 1) * LANES)
        taps_b, bias_b = taps_of(cwb_ref, lanes)
        xin_b = bc_ref[:, lanes].astype(F32)
        pre_b = conv_pre(xin_b, taps_b, bias_b, links)
        g, sums = conv_back(dact, pre_b, sigmoid(pre_b), xin_b, taps_b, links)
        sums.append(jnp.zeros((3, LANES), F32))
        at = slice(base + i * LANES, base + (i + 1) * LANES)
        out_ref[:, at] = g.astype(BF)
        dcw_ref[:, at] += jnp.concatenate(sums, 0)
    upper = (iota((Q, Q), 0) <= iota((Q, Q), 1)).astype(F32)
    below = (iota((Q, Q), 0) > iota((Q, Q), 1)).astype(F32)
    high = functools.partial(jnp.dot, precision=HIGHEST, preferred_element_type=F32)
    rate = hp_ref[1:2, :]
    da = jnp.concatenate(
        [
            high(upper, rsum[:Q, :]) + high(below, rsum3[:Q, LANES:]),
            high(upper, rsum[Q:, :]),
        ],
        0,
    )
    step = dts[...]
    draw = (rsum3[:, :LANES] + da * rate) * sig[...]
    dhp_ref[0:1, :] += jnp.sum(draw, axis=0, keepdims=True)
    dhp_ref[1:2, :] += jnp.sum(da * (rate * step), axis=0, keepdims=True)
    out_ref[:, base + 2 * LANES :] = draw[:, :HEADS].astype(BF)


def params(*semantics, mib=48):
    return pltpu.CompilerParams(dimension_semantics=semantics, vmem_limit_bytes=mib * 1024 * 1024)


def cost(flops, moved):
    return pl.CostEstimate(flops=int(flops / 16), bytes_accessed=int(moved / 16), transcendentals=0)


def block_scratch(extra):
    column = pltpu.VMEM((TOK, LANES), F32)
    packed = pltpu.VMEM((TOK, LANES), BF)
    part = pltpu.VMEM((Q, LANES), F32)
    half = pltpu.VMEM((LANES, Q), BF)
    square = pltpu.VMEM((2, Q, Q), F32)
    base = [pltpu.VMEM((3, TOK, LANES), F32), square, packed, packed, half, packed, packed, packed]
    if not extra:
        return base
    return base + [half, column, column, square, column, pltpu.VMEM((TOK, 2 * LANES), F32), part, part]


def mixer_specs(first):
    return [
        pl.BlockSpec((TOK, TILES * LANES), lambda b, *_: (b + first, 0)),
        pl.BlockSpec((TOK, 2 * LANES), lambda b, *_: (b + first, TILES // 2)),
        pl.BlockSpec((TOK, LANES), lambda b, *_: (b + first, TILES + 2)),
        pl.BlockSpec((8, TILES * LANES), lambda b, *_: (0, 0)),
        pl.BlockSpec((8, 2 * LANES), lambda b, *_: (0, TILES // 2)),
        pl.BlockSpec((8, LANES), lambda b, *_: (0, 0)),
    ]


ANY = pl.BlockSpec(memory_space=pl.ANY)


def fwd_into(bnd, *refs):
    fwd_kernel(bnd, *refs[:6], *refs[7:])


def scan_forward(bounds, proj, cw, hp, first, count, into=None):
    return pl.pallas_call(
        fwd_kernel if into is None else fwd_into,
        out_shape=jax.ShapeDtypeStruct((proj.shape[0], TILES * LANES), F32),
        grid_spec=pltpu.PrefetchScalarGridSpec(
            num_scalar_prefetch=1,
            grid=(count,),
            in_specs=mixer_specs(first) + ([] if into is None else [ANY]),
            out_specs=pl.BlockSpec((TOK, TILES * LANES), lambda b, *_: (b + first, 0)),
            scratch_shapes=block_scratch(False),
        ),
        input_output_aliases={} if into is None else {7: 0},
        compiler_params=params("arbitrary"),
        cost_estimate=cost(count * 8e9, count * 4e6),
    )(bounds[first : first + count], proj, proj, proj, cw, cw, hp, *([] if into is None else [into]))


def bwd_into(bnd, *refs):
    bwd_kernel(bnd, *refs[:8], *refs[9:])


def scan_backward(bounds, proj, cw, hp, scan, dscan, first, count, into=None):
    tile = pl.BlockSpec((TOK, TILES * LANES), lambda b, *_: (b + first, 0))
    return pl.pallas_call(
        bwd_kernel if into is None else bwd_into,
        out_shape=(
            jax.ShapeDtypeStruct((proj.shape[0], REST), BF),
            jax.ShapeDtypeStruct((8, (TILES + 2) * LANES), F32),
            jax.ShapeDtypeStruct((8, LANES), F32),
        ),
        grid_spec=pltpu.PrefetchScalarGridSpec(
            num_scalar_prefetch=1,
            grid=(count,),
            in_specs=mixer_specs(first) + [tile, tile] + ([] if into is None else [ANY]),
            out_specs=(
                pl.BlockSpec((TOK, REST), lambda b, *_: (b + first, 0)),
                pl.BlockSpec((8, (TILES + 2) * LANES), lambda b, *_: (0, 0)),
                pl.BlockSpec((8, LANES), lambda b, *_: (0, 0)),
            ),
            scratch_shapes=block_scratch(True),
        ),
        input_output_aliases={} if into is None else {9: 0},
        compiler_params=params("arbitrary"),
        cost_estimate=cost(count * 16e9, count * 6e6),
    )(
        bounds[first : first + count],
        proj, proj, proj,
        cw,
        cw,
        hp,
        scan, dscan,
        *([] if into is None else [into]),
    )


def whole_once(a):
    return pl.BlockSpec(a.shape, lambda i, *_: (0, 0), pipeline_mode=pl.Buffered(1))


def ginner_kernel(perm, gout_ref, *refs):
    pieces, (out_ref, wide_ref, gate_ref) = refs[:-3], refs[-3:]
    inner = TILES * LANES

    @pl.when(pl.program_id(0) == 0)
    def _():
        for p, piece in enumerate(pieces):
            rows = pl.ds(pl.multiple_of(perm[p] * LANES, LANES), LANES)
            for k in range(8):
                wide_ref[rows, k * 256 : (k + 1) * 256] = piece[inner + k * LANES : inner + (k + 1) * LANES, :]
            gate_ref[:, p * 256 : (p + 1) * 256] = piece[:inner, :]

    out_ref[...] = mm_nt(gout_ref[...], wide_ref[...]).astype(BF)


def inner_gradient(perm, gout, pieces):
    rows, inner = gout.shape[0], TILES * LANES
    whole = pl.BlockSpec((inner, D), lambda i, *_: (0, 0))
    return pl.pallas_call(
        ginner_kernel,
        out_shape=(jax.ShapeDtypeStruct((rows, inner), BF), jax.ShapeDtypeStruct((inner, D), BF), jax.ShapeDtypeStruct((inner, D), BF)),
        grid_spec=pltpu.PrefetchScalarGridSpec(
            num_scalar_prefetch=1,
            grid=(rows // TOK,),
            in_specs=[pl.BlockSpec((TOK, D), lambda i, *_: (i, 0))] + [whole_once(a) for a in pieces],
            out_specs=(pl.BlockSpec((TOK, inner), lambda i, *_: (i, 0)), whole, whole),
        ),
        compiler_params=params("arbitrary"),
        cost_estimate=cost(2 * rows * inner * D, 2 * (rows * D + rows * inner + 4 * inner * D)),
    )(perm, gout, *pieces)


def out_kernel(perm, inner_ref, gout_ref, out_ref, turned, result):
    @pl.when(pl.program_id(0) == 0)
    def _():
        turned[...] = inner_ref[...].T

    result[...] = mm(turned[...], gout_ref[...])
    for p in range(8):
        rows = pl.ds(pl.multiple_of(perm[p] * LANES, LANES), LANES)
        out_ref[:, p * 256 : (p + 1) * 256] = result[rows, :].astype(BF)


def out_terms(perm, inner, gout):
    rows, wide = inner.shape
    return pl.pallas_call(
        out_kernel,
        out_shape=jax.ShapeDtypeStruct((wide, D), BF),
        grid_spec=pltpu.PrefetchScalarGridSpec(
            num_scalar_prefetch=1,
            grid=(8,),
            in_specs=[
                pl.BlockSpec((rows, wide), lambda k, *_: (0, 0)),
                pl.BlockSpec((rows, 256), lambda k, *_: (0, k)),
            ],
            out_specs=pl.BlockSpec((LANES, D), lambda k, *_: (k, 0)),
            scratch_shapes=[pltpu.VMEM((wide, rows), BF), pltpu.VMEM((wide, 256), F32)],
        ),
        compiler_params=params("arbitrary", mib=48),
        cost_estimate=cost(2 * rows * wide * D, 2 * (rows * wide + rows * D + wide * D)),
    )(perm, inner, gout)


def stat_kernel(norm_ref, w_ref, scan_ref, gin_ref, gain_ref, gate_ref, out_ref):
    gate_ref[...] = mm_nt(norm_ref[...], w_ref[...]).astype(BF)
    one = two = jnp.zeros((TOK, LANES), F32)
    for t in range(TILES):
        at = slice(t * LANES, (t + 1) * LANES)
        gate = gate_ref[:, at].astype(F32)
        gated = scan_ref[:, at] * (gate * sigmoid(gate))
        one = one + gated * gated
        two = two + gated * (gin_ref[:, at].astype(F32) * gain_ref[:, at])
    a = jnp.sum(one.T, axis=0, keepdims=True)
    c = jnp.sum(two.T, axis=0, keepdims=True)
    out_ref[0] = jnp.concatenate([a, c, jnp.zeros((6, TOK), F32)], 0)


def gate_stats(normed, w_gate, scan, ginner, gain):
    rows, inner = scan.shape
    tile = pl.BlockSpec((TOK, inner), lambda b: (b, 0))
    return pl.pallas_call(
        stat_kernel,
        out_shape=(jax.ShapeDtypeStruct((rows, inner), BF), jax.ShapeDtypeStruct((rows // TOK, 8, TOK), F32)),
        grid=(rows // TOK,),
        in_specs=[
            pl.BlockSpec((TOK, D), lambda b: (b, 0)),
            pl.BlockSpec((inner, D), lambda b: (0, 0)),
            tile,
            tile,
            pl.BlockSpec((1, inner), lambda b: (0, 0)),
        ],
        out_specs=(tile, pl.BlockSpec((1, 8, TOK), lambda b: (b, 0, 0))),
        compiler_params=params("arbitrary", mib=48),
        cost_estimate=cost(2 * rows * inner * D, rows * (D * 2 + inner * 8) + inner * D * 2),
    )(normed, w_gate, scan, ginner, gain)


def gate_kernel(sum_ref, scan_ref, gate_ref, gin_ref, gain_ref, inner_ref, dgate_ref, dscan_ref, dgain_ref):
    rows = scan_ref.shape[0]

    @pl.when((pl.program_id(0) == 0) & (pl.program_id(1) == 0))
    def _():
        dgain_ref[...] = jnp.zeros_like(dgain_ref)

    r = lax.rsqrt(sum_ref[0, 0:1, :] * (1.0 / DIN) + EPSILON)
    c = r * r * sum_ref[0, 1:2, :] * (1.0 / DIN)
    rinv = jnp.broadcast_to(r, (LANES, rows)).T
    coef = jnp.broadcast_to(c, (LANES, rows)).T
    for t in range(TILES):
        at = slice(t * LANES, (t + 1) * LANES)
        gate = gate_ref[:, at].astype(F32)
        sg = sigmoid(gate)
        act = gate * sg
        scan = scan_ref[:, at]
        gain = gain_ref[:, at]
        gated = scan * act
        scaled = gated * rinv
        gin = gin_ref[:, at].astype(F32)
        inner_ref[:, at] = (scaled * gain).astype(BF)
        dgated = rinv * (gin * gain - gated * coef)
        dscan_ref[:, at] = (dgated * act).astype(BF)
        dgate_ref[:, at] = (dgated * scan * (sg + act * (1.0 - sg))).astype(BF)
        dgain_ref[0:1, at] += jnp.sum(gin * scaled, axis=0, keepdims=True)


def gate_both(sums, scan, gate, ginner, gain):
    rows, inner = scan.shape
    tile = pl.BlockSpec((Q, inner), lambda b, h: (2 * b + h, 0))
    whole = jax.ShapeDtypeStruct((rows, inner), BF)
    return pl.pallas_call(
        gate_kernel,
        out_shape=(whole, whole, whole, jax.ShapeDtypeStruct((8, inner), F32)),
        grid=(rows // TOK, 2),
        in_specs=[
            pl.BlockSpec((1, 8, Q), lambda b, h: (b, 0, h)),
            tile,
            tile,
            tile,
            pl.BlockSpec((1, inner), lambda b, h: (0, 0)),
        ],
        out_specs=(tile, tile, tile, pl.BlockSpec((8, inner), lambda b, h: (0, 0))),
        compiler_params=params("arbitrary", "arbitrary", mib=48),
        cost_estimate=cost(0, rows * inner * 14),
    )(sums, scan, gate, ginner, gain)


def back_kernel(a_ref, wa_ref, b_ref, wb_ref, norm_ref, out_ref, dgo_ref):
    @pl.when(pl.program_id(0) == 0)
    def _():
        dgo_ref[...] = jnp.zeros_like(dgo_ref)

    for c in range(4):
        at = slice(c * 512, (c + 1) * 512)
        res = mm(a_ref[...], wa_ref[:, at]) + mm(b_ref[...], wb_ref[:, at])
        out_ref[:, at] = res.astype(BF)
        dgo_ref[0:1, at] += jnp.sum(res * norm_ref[:, at].astype(F32), axis=0, keepdims=True)


def normed_gradient(gproj, w_rest, dgate, w_two, normed, first, count):
    rows, inner = dgate.shape
    row = lambda width: pl.BlockSpec((TOK, width), lambda b: (b + first, 0))
    return pl.pallas_call(
        back_kernel,
        out_shape=(jax.ShapeDtypeStruct((count * TOK, D), BF), jax.ShapeDtypeStruct((8, D), F32)),
        grid=(count,),
        in_specs=[
            row(REST),
            pl.BlockSpec((REST, D), lambda b: (0, 0)),
            row(inner),
            pl.BlockSpec((inner, D), lambda b: (0, 0)),
            row(D),
        ],
        out_specs=(pl.BlockSpec((TOK, D), lambda b: (b, 0)), pl.BlockSpec((8, D), lambda b: (0, 0))),
        compiler_params=params("arbitrary", mib=48),
        cost_estimate=cost(2 * count * TOK * D * (REST + inner), 2 * (REST + inner) * D),
    )(gproj, w_rest, dgate, w_two, normed)


def across_kernel(a_ref, b_ref, out_ref, *turned):
    if len(turned) == 2:
        (kept, turned) = turned

        @pl.when(pl.program_id(0) == 0)
        def _():
            turned[...] = a_ref[...].T
            kept[...] = turned[...]
    else:
        turned = a_ref
    out_ref[0] = mm(turned[...], b_ref[...]).astype(out_ref.dtype)


def across_rows(a, b, first, count, turn):
    rows, n = b.shape
    m = a.shape[1] if turn else a.shape[0]
    whole = pl.BlockSpec(a.shape, lambda k: (0, 0))
    part = jax.ShapeDtypeStruct((count, m, 256), BF)
    spec = pl.BlockSpec((1, m, 256), lambda k: (k, 0, 0))
    return pl.pallas_call(
        across_kernel,
        out_shape=(part, jax.ShapeDtypeStruct((m, rows), BF)) if turn else part,
        grid=(count,),
        in_specs=[whole, pl.BlockSpec((rows, 256), lambda k: (0, k + first))],
        out_specs=(spec, pl.BlockSpec((m, rows), lambda k: (0, 0))) if turn else spec,
        scratch_shapes=[pltpu.VMEM((m, rows), BF)] if turn else [],
        compiler_params=params("arbitrary", mib=48),
        cost_estimate=cost(2 * rows * m * 256 * count, 2 * (rows * m + rows * 256 * count + m * 256 * count)),
    )(a, b)


def pick_rest_kernel(me, *refs):
    tiles, (shared, steps, out_ref) = refs[:TILES], refs[TILES:]
    for t, ref in enumerate(tiles):
        out_ref[t * LANES : (t + 1) * LANES, :] = ref[...].astype(BF)
    wide = TILES * LANES
    out_ref[wide : wide + 2 * N, :] = shared[...].astype(BF)
    mine, head = iota((HEADS, H), 0), iota((HEADS, H), 1)
    pick = (head == 8 * (mine // 2) + 2 * me[0] + mine % 2).astype(BF)
    out_ref[wide + 2 * N :, :] = mm(pick, steps[...].astype(BF)).astype(BF)


def tile_spec(lanes, t):
    return pl.BlockSpec((LANES, lanes), lambda i, me: (4 * t + me[0], 0))


def pick_rest(me, turned):
    lanes = turned.shape[1]
    fixed = lambda rows, at: pl.BlockSpec((rows, lanes), lambda i, me: (at // rows, 0))
    return pl.pallas_call(
        pick_rest_kernel,
        out_shape=jax.ShapeDtypeStruct((REST, lanes), BF),
        grid_spec=pltpu.PrefetchScalarGridSpec(
            num_scalar_prefetch=1,
            grid=(1,),
            in_specs=[tile_spec(lanes, TILES + t) for t in range(TILES)] + [fixed(2 * N, 2 * DIN), fixed(H, 2 * DIN + 2 * N)],
            out_specs=pl.BlockSpec((REST, lanes), lambda i, me: (0, 0)),
        ),
        compiler_params=params("arbitrary"),
        cost_estimate=cost(0, 6 * REST * lanes),
    )(me, *[turned] * (TILES + 2))


def pick_two_kernel(me, *refs):
    tiles, (rows, out_ref) = refs[:TILES], refs[TILES:]
    for t, ref in enumerate(tiles):
        out_ref[t * LANES : (t + 1) * LANES, :] = ref[...].astype(BF)
    wide = TILES * LANES
    for k in range(8):
        out_ref[wide + k * LANES : wide + (k + 1) * LANES, :] = rows[:, k * 256 : (k + 1) * 256].astype(BF)


def pick_two(me, turned, out_weight):
    lanes = turned.shape[1]
    return pl.pallas_call(
        pick_two_kernel,
        out_shape=jax.ShapeDtypeStruct((2 * TILES * LANES, lanes), BF),
        grid_spec=pltpu.PrefetchScalarGridSpec(
            num_scalar_prefetch=1,
            grid=(1,),
            in_specs=[tile_spec(lanes, t) for t in range(TILES)] + [pl.BlockSpec((LANES, D), lambda i, me: (me[0], 0))],
            out_specs=pl.BlockSpec((2 * TILES * LANES, lanes), lambda i, me: (0, 0)),
        ),
        compiler_params=params("arbitrary"),
        cost_estimate=cost(0, 12 * TILES * LANES * lanes),
    )(me, *[turned] * TILES, out_weight)


def pick_gate_kernel(me, *refs):
    for t, ref in enumerate(refs[:-1]):
        refs[-1][t * LANES : (t + 1) * LANES, :] = ref[...].astype(BF)


def pick_gate(me, turned):
    lanes = turned.shape[1]
    return pl.pallas_call(
        pick_gate_kernel,
        out_shape=jax.ShapeDtypeStruct((TILES * LANES, lanes), BF),
        grid_spec=pltpu.PrefetchScalarGridSpec(
            num_scalar_prefetch=1,
            grid=(1,),
            in_specs=[tile_spec(lanes, t) for t in range(TILES)],
            out_specs=pl.BlockSpec((TILES * LANES, lanes), lambda i, me: (0, 0)),
        ),
        compiler_params=params("arbitrary"),
        cost_estimate=cost(0, 6 * TILES * LANES * lanes),
    )(me, *[turned] * TILES)


STEP = 128


def norm_kernel(perm, tok_ref, gain_ref, out_ref):
    x = tok_ref[...].astype(F32)
    inv = lax.rsqrt(jnp.mean(x * x, axis=1, keepdims=True) + EPSILON)
    wide = D // 8
    for k in range(8):
        here = pl.ds(pl.multiple_of(perm[k] * wide, wide), wide)
        out_ref[:, k * wide : (k + 1) * wide] = (
            tok_ref[:, here].astype(F32) * inv * gain_ref[:, here]
        ).astype(BF)


def norm_rows(perm, tokens, gain):
    rows = tokens.shape[0]
    row = pl.BlockSpec((STEP, D), lambda i, *_: (i, 0))
    return pl.pallas_call(
        norm_kernel,
        out_shape=jax.ShapeDtypeStruct((rows, D), BF),
        grid_spec=pltpu.PrefetchScalarGridSpec(
            num_scalar_prefetch=1,
            grid=(rows // STEP,),
            in_specs=[row, pl.BlockSpec((1, D), lambda i, *_: (0, 0))],
            out_specs=row,
        ),
        compiler_params=params("arbitrary"),
        cost_estimate=pl.CostEstimate(flops=0, bytes_accessed=rows * D * 4, transcendentals=0),
    )(perm, tokens, gain)


def last_kernel(perm, tok_ref, cot_ref, keep_ref, gain_ref, one_ref, two_ref, three_ref, out_ref, grad):
    wide = D // 8
    for k in range(8):
        here = pl.ds(pl.multiple_of(perm[k] * wide, wide), wide)
        at = slice(k * wide, (k + 1) * wide)
        grad[:, here] = (
            one_ref[:, at].astype(F32) + two_ref[:, at].astype(F32) + three_ref[:, at].astype(F32)
        ) * gain_ref[:, here]
    x = tok_ref[...].astype(F32)
    inv = lax.rsqrt(jnp.mean(x * x, axis=1, keepdims=True) + EPSILON)
    g = grad[...]
    dot = jnp.mean(g * x, axis=1, keepdims=True)
    out_ref[...] = inv * (g - x * (inv * inv * dot)) + keep_ref[...] * cot_ref[...].astype(F32)


def last_rows(perm, tokens, cotangent, keep, gain, parts):
    rows = tokens.shape[0]
    row = pl.BlockSpec((STEP, D), lambda i, *_: (i, 0))
    return pl.pallas_call(
        last_kernel,
        out_shape=jax.ShapeDtypeStruct((rows, D), F32),
        grid_spec=pltpu.PrefetchScalarGridSpec(
            num_scalar_prefetch=1,
            grid=(rows // STEP,),
            in_specs=[
                row,
                row,
                pl.BlockSpec((STEP, 1), lambda i, *_: (i, 0)),
                pl.BlockSpec((1, D), lambda i, *_: (0, 0)),
                row,
                row,
                row,
            ],
            out_specs=row,
            scratch_shapes=[pltpu.VMEM((STEP, D), F32)],
        ),
        compiler_params=params("arbitrary"),
        cost_estimate=pl.CostEstimate(flops=0, bytes_accessed=rows * D * 14, transcendentals=0),
    )(perm, tokens, cotangent, keep, gain, *parts)


def first_join_kernel(me, *refs):
    pieces, (out_ref, grad_ref, stage, sem) = refs[:4], refs[4:]
    inner = TILES * LANES
    for k in range(4):
        q = jnp.bitwise_xor(me[0], k)
        for t in range(TILES):
            rows = pl.ds(pl.multiple_of((4 * t + q) * LANES, LANES), LANES)
            stage[rows, :] = pieces[k][t * LANES : (t + 1) * LANES, :].astype(F32)
    copy = pltpu.make_async_copy(stage, out_ref.at[pl.ds(0, 4 * inner)], sem)
    copy.start()
    for k in range(4):
        q = jnp.bitwise_xor(me[0], k)
        rows = pl.ds(pl.multiple_of(q * LANES, LANES), LANES)
        for c in range((pieces[k].shape[0] - inner) // LANES):
            grad_ref[rows, c * 256 : (c + 1) * 256] = pieces[k][
                inner + c * LANES : inner + (c + 1) * LANES, :
            ].astype(F32)
    copy.wait()


def first_join(me, pieces, width):
    lanes = pieces[0].shape[1]
    whole = pl.BlockSpec(pieces[0].shape, lambda i, *_: (0, 0))
    return pl.pallas_call(
        first_join_kernel,
        out_shape=(
            jax.ShapeDtypeStruct((width, lanes), F32),
            jax.ShapeDtypeStruct((4 * LANES, D), F32),
        ),
        grid_spec=pltpu.PrefetchScalarGridSpec(
            num_scalar_prefetch=1,
            grid=(1,),
            in_specs=[whole] * 4,
            out_specs=(ANY, pl.BlockSpec((4 * LANES, D), lambda i, *_: (0, 0))),
            scratch_shapes=[pltpu.VMEM((4 * TILES * LANES, lanes), F32), pltpu.SemaphoreType.DMA],
        ),
        compiler_params=params("arbitrary", mib=48),
        cost_estimate=cost(0, 320e6),
    )(me, *pieces)


def last_join_kernel(me, one, two, three, four, into, out_ref, stage, sem):
    pieces = (one, two, three, four)
    inner = TILES * LANES
    few = H // 4
    for k in range(4):
        q = jnp.bitwise_xor(me[0], k)
        for t in range(TILES):
            rows = pl.ds(pl.multiple_of((4 * t + q) * LANES, LANES), LANES)
            stage[rows, :] = pieces[k][t * LANES : (t + 1) * LANES, :].astype(F32)
    stage[4 * inner : 4 * inner + 2 * N, :] = sum(p[inner : inner + 2 * N, :].astype(F32) for p in pieces)
    steps = None
    for k in range(4):
        q = jnp.bitwise_xor(me[0], k)
        head, mine = iota((H, few), 0), iota((H, few), 1)
        spread = (head == 8 * (mine // 2) + 2 * q + mine % 2).astype(BF)
        term = mm(spread, pieces[k][inner + 2 * N :, :])
        steps = term if steps is None else steps + term
    stage[4 * inner + 2 * N :, :] = steps
    copy = pltpu.make_async_copy(stage, out_ref.at[pl.ds(4 * inner, stage.shape[0])], sem)
    copy.start()
    copy.wait()


def last_join(me, pieces, into):
    lanes = pieces[0].shape[1]
    whole = pl.BlockSpec(pieces[0].shape, lambda i, *_: (0, 0))
    return pl.pallas_call(
        last_join_kernel,
        out_shape=jax.ShapeDtypeStruct(into.shape, F32),
        grid_spec=pltpu.PrefetchScalarGridSpec(
            num_scalar_prefetch=1,
            grid=(1,),
            in_specs=[whole] * 4 + [ANY],
            out_specs=ANY,
            scratch_shapes=[pltpu.VMEM((into.shape[0] - 4 * TILES * LANES, lanes), F32), pltpu.SemaphoreType.DMA],
        ),
        input_output_aliases={5: 0},
        compiler_params=params("arbitrary"),
        cost_estimate=cost(0, 8e6),
    )(me, *pieces, into)


def tie(*arrays):
    return lax.optimization_barrier(arrays)


def swap(x, d):
    return lax.ppermute(x, "rep", [(i, i ^ d) for i in range(4)])


def fw(x):
    return lax.ppermute(x, "shard", [(RING[i], RING[(i + 1) % 8]) for i in range(8)])


def bw(x):
    return lax.ppermute(x, "shard", [(RING[(i + 1) % 8], RING[i]) for i in range(8)])


def relative(s, n):
    if n != 8:
        return jnp.arange(8, dtype=jnp.int32), jnp.arange(8, dtype=jnp.int32)
    table, inverse = [], []
    for shard in range(8):
        p = RING.index(shard)
        row = [RING[(p + d) % 8] for d in (0, -1, 1, -2, 2, -3, 3, 4)]
        table.append(row)
        inverse.append([row.index(i) for i in range(8)])
    return jnp.asarray(table, jnp.int32)[s], jnp.asarray(inverse, jnp.int32)[s]


def cut(rows):
    return -(-rows // 32) * 16


def ring_pieces(piece, pieces):
    half = cut(piece.shape[0])
    a = b = piece
    pieces.append(piece)
    for _ in range(3):
        a, b = yield fw(a), bw(b)
        pieces += [a, b]
    a, b = yield fw(a[:half]), bw(b[half:])
    pieces.append(jnp.concatenate([a, b], 0))
    yield


def add16(a, b):
    return (a.astype(F32) + b.astype(F32)).astype(BF)


def ring_sum():
    far = yield
    half = cut(far.shape[0])
    rf, rb, (own, f1, b1, f2, b2, f3, b3) = yield far[:half], far[half:]
    sf = jnp.concatenate([add16(b3[:half], rf), b3[half:]], 0)
    sb = jnp.concatenate([f3[:half], add16(f3[half:], rb)], 0)
    rf, rb = yield sf, sb
    rf, rb = yield add16(b2, rf), add16(f2, rb)
    rf, rb = yield add16(b1, rf), add16(f1, rb)
    yield (own.astype(F32) + rf.astype(F32) + rb.astype(F32)).astype(BF)


def launch(steps, arrived, *others):
    forward, backward, *others = tie(*steps.send(arrived), *others)
    return [fw(forward), bw(backward)], *others


def blocks_of(x):
    return [x[k * TOK : (k + 1) * TOK] for k in range(4)]


def sum_rep(parts):
    far = swap(parts[3], 1)
    chip = swap((parts[2].astype(F32) + far.astype(F32)).astype(BF), 2)
    return parts[0].astype(F32) + swap(parts[1], 1).astype(F32) + chip.astype(F32)


def shards(n, tokens, cotangent, lengths, order, mask, in_weight, out_weight, conv_weight, conv_bias, dt_bias,
           a_log, skip_gain, gain_outer, gain_inner):
    r, s = lax.axis_index("rep"), lax.axis_index("shard")
    ring = n == 8
    inner_width = TILES * LANES
    perm, place = relative(s, n)
    keep = mask.astype(F32)[:, None]
    catalog = jnp.arange(lengths.shape[0], dtype=jnp.int32)
    picked = jnp.sum(jnp.where(order[:, None] == catalog[None, :], lengths[None, :], 0), axis=1)
    bounds = jnp.stack([picked[0], picked[0] + picked[1]])[None, :]
    bounds = jnp.concatenate([bounds, swap(bounds, 1), swap(bounds, 2), swap(bounds, 3)], 0)

    turned = in_weight.T
    me = r[None]
    rest = pick_rest(me, turned)
    normed = norm_rows(perm, tokens, gain_outer[None, :])
    gout = (cotangent.astype(F32) * keep).astype(BF)

    def own_lanes(v, width):
        v = lax.dynamic_index_in_dim(v.reshape(v.shape[:-1] + (TILES, 4, width)), r, v.ndim, False)
        return v.reshape(v.shape[:-2] + (TILES * width,))

    heads = H // 4
    skip = jnp.broadcast_to(skip_gain[:, None], (H, P_SIZE)).reshape(1, DIN)
    rows8 = jnp.concatenate(
        [conv_weight, conv_bias[None], jnp.pad(skip, ((0, 0), (0, 2 * N))), jnp.zeros((2, CONVCH), F32)], 0
    )
    cw = jnp.concatenate([own_lanes(rows8[:, :DIN], LANES), rows8[:, DIN:]], 1)
    hp = jnp.stack([own_lanes(dt_bias, 2), own_lanes(-jnp.exp(a_log), 2)])
    hp = jnp.pad(hp, ((0, 6), (0, LANES - heads)))
    gain = own_lanes(gain_inner, LANES)[None, :]

    if ring:
        pieces = []
        steps = ring_pieces(rest, pieces)
        sent = next(steps)
        core, chip = swap(normed, 1), swap(normed, 2)
        two = pick_two(me, turned, out_weight)
        *sent, core, two = tie(*sent, core, two)
        sent = steps.send(sent)
        *sent, gout = tie(*sent, gout)
        sent = steps.send(sent)
        sent = steps.send(tie(*sent))
        near = jnp.concatenate(pieces[:7] + [jnp.zeros_like(rest)], 1)
        *sent, chip, two, near = tie(*sent, chip, two, near)
        steps.send(sent)
        rest_far = pieces[7]

        pieces = []
        steps = ring_pieces(two, pieces)
        sent = next(steps)
        far, gchip, gcore = swap(chip, 1), swap(gout, 2), swap(gout, 1)
        w_rest = lax.dynamic_update_slice(near, rest_far, (0, 7 * rest.shape[1]))
        all_normed = jnp.concatenate([normed, core, chip, far], 0)
        all_normed, w_rest = tie(all_normed, w_rest)
        proj = mm_nt(all_normed, w_rest).astype(BF)
        *sent, proj = tie(*sent, proj)
        sent = steps.send(sent)
        scan = scan_forward(bounds, proj, cw, hp, 0, 2)
        *sent, scan, gchip, gcore = tie(*sent, scan, gchip, gcore)
        sent = steps.send(sent)
        gfar = swap(gchip, 1)
        scan = scan_forward(bounds, proj, cw, hp, 2, 2, scan)
        *sent, scan, gfar = tie(*sent, scan, gfar)
        sent = steps.send(sent)
        all_gout = jnp.concatenate([gout, gcore, gchip, gfar], 0)
        *sent, all_gout = tie(*sent, all_gout)
        steps.send(sent)
        ginner, w_out, w_two = inner_gradient(perm, all_gout, pieces)
    else:
        everyone = lambda x: [x, swap(x, 1), swap(x, 2), swap(x, 3)]
        w_rest = lax.all_gather(rest, "shard", axis=1, tiled=True)
        w_two = lax.all_gather(pick_gate(me, turned), "shard", axis=1, tiled=True)
        w_out = lax.all_gather(out_weight.astype(BF), "shard", axis=0, tiled=True)
        w_out = lax.dynamic_index_in_dim(w_out.reshape(TILES, 4, LANES, D), r, 1, False).reshape(inner_width, D)
        all_normed = jnp.concatenate(everyone(normed), 0)
        all_gout = jnp.concatenate(everyone(gout), 0)
        proj = mm_nt(all_normed, w_rest).astype(BF)
        scan = scan_forward(bounds, proj, cw, hp, 0, 4)
        ginner = mm_nt(all_gout, w_out).astype(BF)

    gate, sums = gate_stats(all_normed, w_two, scan, ginner, gain)
    there = [swap(sums, d) for d in (1, 2, 3)]
    sums = jnp.stack([sums[k] + there[0][k ^ 1] + there[1][k ^ 2] + there[2][k ^ 3] for k in range(4)])
    inner, dgate, dscan, dgain = gate_both(sums, scan, gate, ginner, gain)

    def columns_of(x):
        return [x[:, k * 256 : (k + 1) * 256] for k in range(x.shape[1] // 256)]

    at_r = (jnp.arange(4) == r).astype(F32)
    sizes = [4 * CONVCH, CONVCH, H, H, H, D, DIN]

    def all_lanes(v, width):
        v = v.reshape(v.shape[:-1] + (TILES, 1, width)) * at_r[:, None]
        return v.reshape(v.shape[:-3] + (TILES * 4 * width,))

    def small_vector(dcw, dhp, dgo, dgain):
        wide = jnp.concatenate([all_lanes(dcw[:5, :inner_width], LANES), dcw[:5, inner_width:]], 1)
        dskip = jnp.sum(dcw[5, :inner_width].reshape(heads, P_SIZE), axis=1)
        dgo = dgo[0].reshape(8, D // 8)[place].reshape(D) / gain_outer
        parts = [
            wide.reshape(-1),
            all_lanes(dhp[0, :heads], 2),
            all_lanes(dhp[1, :heads], 2),
            all_lanes(dskip, 2),
            dgo,
            all_lanes(dgain[0], LANES),
        ]
        flat = jnp.concatenate(parts)
        return jnp.pad(flat, (0, -flat.shape[0] % 1024)).reshape(-1, LANES)

    width = in_weight.shape[1]
    final = functools.partial(normed_gradient, w_rest=w_rest, dgate=dgate, w_two=w_two, normed=all_normed)
    if ring:
        outs = columns_of(out_terms(perm, inner, all_gout))
        (dgate, _) = tie(dgate, outs[7])
        terms8 = columns_of(lax.dot_general(dgate, all_normed, TN, preferred_element_type=F32).astype(BF))
        terms8 = [jnp.concatenate(p, 0) for p in zip(terms8, outs)]
        steps = ring_sum()
        next(steps)
        sent, inner, dscan = launch(steps, terms8[7], inner, dscan)
        back = functools.partial(scan_backward, bounds, proj, cw, hp, scan)
        branch = mm(inner, w_out).astype(BF)
        *sent, branch = tie(*sent, branch)
        b0, b1, b2, b3 = blocks_of(branch)
        sent, dscan, b3 = launch(steps, (*sent, terms8[:7]), dscan, b3)
        far = swap(b3, 1)
        gproj, dcw, dhp = back(dscan, 2, 2)
        *sent, gproj, far = tie(*sent, gproj, far)
        sent, gproj, chip = launch(steps, sent, gproj, add16(b2, far))
        core, chip = swap(b1, 1), swap(chip, 2)
        late, dgo = final(gproj, first=2, count=2)
        *sent, gproj, core, late = tie(*sent, gproj, core, late)
        sent, gproj, late = launch(steps, sent, gproj, late)
        far = swap(late[TOK:], 1)
        gproj, d, e = back(dscan, 0, 1, gproj)
        dcw, dhp = dcw + d, dhp + e
        gproj, far = tie(gproj, far)
        gproj, total = tie(gproj, add16(late[:TOK], far))
        gproj, d, e = back(dscan, 1, 1, gproj)
        dcw, dhp = dcw + d, dhp + e
        *sent, gproj = tie(*sent, gproj)
        share, gproj = tie(steps.send(sent), gproj)
        upper = swap(total[: TOK // 2], 2)

        far, turned_proj = across_rows(gproj, all_normed, 7, 1, True)
        steps = ring_sum()
        next(steps)
        sent, turned_proj = launch(steps, far[0], turned_proj)
        gates = [share, swap(share, 1)]
        seven = across_rows(turned_proj, all_normed, 0, 7, False)
        *sent, seven, gproj, upper, lower, share, chip = tie(
            *sent, seven, gproj, upper, total[TOK // 2 :], share, chip
        )
        branch = (b0, core, chip)
        sent, gproj, lower = launch(steps, (*sent, list(seven)), gproj, lower)
        lower = swap(lower, 2)
        early, d = final(gproj, first=0, count=2)
        dgo = dgo + d
        *sent, early, lower, share = tie(*sent, early, lower, share)
        sent, early, share, dgo = launch(steps, sent, early, share, dgo)
        gates.append(swap(share, 2))
        core = swap(early[TOK:], 1)
        bits = [1 << k for k in range(n.bit_length() - 1)]
        flip = lambda v, d: v + lax.ppermute(v, "shard", [(i, i ^ d) for i in range(n)])
        layer_out = (keep * (tokens.astype(F32) + sum(b.astype(F32) for b in branch))).astype(BF)
        *sent, core, layer_out, dgo = tie(*sent, core, layer_out, dgo)
        sent, core, dgo = launch(steps, sent, core, dgo)
        small = small_vector(dcw, dhp, dgo, dgain)
        small = small + swap(small, 1)
        parts = [early[:TOK], core, jnp.concatenate([upper, lower], 0)]
        grad_tokens = last_rows(perm, tokens, cotangent, keep, gain_outer[None, :], parts)
        *sent, gates[2], grad_tokens, small = tie(*sent, gates[2], grad_tokens, small)
        share, small, gates[2] = tie(steps.send(sent), small, gates[2])
        rests = [share, swap(share, 1), swap(share, 2)]
        gates.append(swap(gates[2], 1))
        for d in bits:
            small = flip(small, d)
        grad_in, grad_out_weight = first_join(me, gates, width)
        rests[2], grad_in = tie(rests[2], grad_in)
        small = small + swap(small, 2)
        rests.append(swap(rests[2], 1))
    else:
        side = lambda x: jnp.concatenate(list(x), 1)
        rows_sum = lambda x, axis: lax.psum_scatter(
            x.astype(F32), "shard", scatter_dimension=axis, tiled=True
        ).astype(BF)
        branch = sum_rep(blocks_of(mm(inner, w_out).astype(BF)))
        gproj, dcw, dhp = scan_backward(bounds, proj, cw, hp, scan, dscan, 0, 4)
        layer_out = (keep * (tokens.astype(F32) + branch.astype(F32))).astype(BF)
        gnormed, dgo = final(gproj, first=0, count=4)
        total = sum_rep(blocks_of(gnormed)).astype(BF)
        grad_tokens = last_rows(
            perm, tokens, cotangent, keep, gain_outer[None, :], [total, jnp.zeros_like(total), jnp.zeros_like(total)]
        )
        grad_out = lax.dot_general(inner, all_gout, TN, preferred_element_type=F32)
        spread = grad_out.reshape(TILES, 1, LANES, D).astype(F32) * (jnp.arange(4)[None, :, None, None] == r)
        spread = lax.psum_scatter(spread.reshape(DIN, D), "shard", scatter_dimension=0, tiled=True)
        grad_out_weight = lax.psum(spread, "rep")
        gates = everyone(rows_sum(side(across_rows(dgate, all_normed, 0, 8, True)[0]), 1))
        rests = everyone(rows_sum(side(across_rows(gproj, all_normed, 0, 8, True)[0]), 1))
        grad_in, _ = first_join(me, gates, width)
        small = lax.psum(small_vector(dcw, dhp, dgo, dgain), ("rep", "shard"))
    grad_in_weight = last_join(me, rests, grad_in).T

    small = small.reshape(-1)
    ends = [sum(sizes[: i + 1]) for i in range(len(sizes))]
    g_cw, g_cb, g_db, g_al, g_sk, g_go, g_gi = [small[e - z : e] for e, z in zip(ends, sizes)]
    return (
        layer_out,
        grad_tokens,
        grad_in_weight,
        grad_out_weight,
        g_cw.reshape(4, CONVCH),
        g_cb,
        g_db,
        g_al,
        g_sk,
        g_go,
        g_gi,
    )


def solution(mesh):
    rows = P(("rep", "shard"), None)
    vector = P(("rep", "shard"))
    owned = P("shard", None)
    return jax.shard_map(
        functools.partial(shards, mesh.shape["shard"]),
        mesh=mesh,
        in_specs=(rows, rows, P(), vector, vector, owned, owned) + (P(),) * 7,
        out_specs=(rows, rows, owned, owned) + (P(),) * 7,
        check_vma=False,
    )
```

```python
import functools

import jax
import jax.numpy as jnp
from jax import lax
from jax.experimental import pallas as pl
from jax.experimental.pallas import tpu as pltpu
from jax.sharding import PartitionSpec as P

D = 2048
DIN = 4096
P_SIZE = 64
N = 128
Q = 256
H = 64
CONVCH = DIN + 2 * N
EPSILON = 1e-05
LOG2E = 1.4426950408889634
LANES = 128
TOK = 512
TILES = DIN // 128 // 4
HEADS = H // 4
REST = TILES * 128 + 2 * N + H // 4
HIGHEST = lax.Precision.HIGHEST
BF = jnp.bfloat16
F32 = jnp.float32
NT = (((1,), (1,)), ((), ()))
TN = (((0,), (0,)), ((), ()))
RING = (0, 2, 4, 6, 7, 5, 3, 1)


def mm(a, b):
    return jnp.dot(a, b, preferred_element_type=F32)


def mm_nt(a, b):
    return lax.dot_general(a, b, NT, preferred_element_type=F32)


def iota(shape, dim):
    return lax.broadcasted_iota(jnp.int32, shape, dim)


def start_of(rows, b1, b2):
    return jnp.where(rows >= b2, b2, jnp.where(rows >= b1, b1, 0))


def sigmoid(v):
    return 0.5 * jnp.tanh(0.5 * v) + 0.5


def conv_pre(x, taps, bias, lk):
    pre = bias + taps[3] * x
    for k in range(1, 4):
        pre = pre + taps[3 - k] * (pltpu.roll(x, k, 0) * lk[k - 1])
    return pre


def taps_of(cw_ref, lanes):
    return [cw_ref[k : k + 1, lanes] for k in range(4)], cw_ref[4:5, lanes]


def terms(v, count):
    out = []
    for _ in range(count):
        out.append(v.astype(BF).astype(F32))
        v = v - out[-1]
    return out


def side_by_side(parts):
    return sum(pltpu.roll(p, HEADS * i, 1) if i else p for i, p in enumerate(parts))


def prepare(b1, b2, bc_ref, dt_ref, cwb_ref, hp_ref, lk, score, bmat, cmat, btrans, ctrans,
            dts, sig, late, early, expand, transposed):
    rows = iota((TOK, LANES), 0)
    lane = iota((TOK, LANES), 1)
    pos = rows - start_of(rows, b1, b2)
    for k in range(1, 4):
        lk[k - 1] = (pos >= k).astype(F32)
    links = [lk[0], lk[1], lk[2]]
    for half, keep in ((0, bmat), (1, cmat)):
        lanes = slice(half * LANES, (half + 1) * LANES)
        taps, bias = taps_of(cwb_ref, lanes)
        pre = conv_pre(bc_ref[:, lanes].astype(F32), taps, bias, links)
        act = pre * sigmoid(pre)
        keep[...] = act.astype(BF)
        if half == 0:
            btrans[...] = act[:Q].T.astype(BF)
        elif ctrans is not None:
            ctrans[...] = act[Q:].T.astype(BF)
    for c in range(2):
        part = slice(c * Q, (c + 1) * Q)
        if transposed:
            s = mm_nt(bmat[part, :], cmat[part, :])
        else:
            s = mm_nt(cmat[part, :], bmat[part, :])
        score[c] = jnp.where(allowed(c, b1, b2, transposed), s, 0.0)
    real = lane < HEADS
    raw = jnp.where(real, dt_ref[...].astype(F32), 0.0) + hp_ref[0:1, :]
    step = jnp.where(real, jnp.maximum(raw, 0.0) + jnp.log1p(jnp.exp(-jnp.abs(raw))), 0.0)
    if dts is not None:
        dts[...] = step
        sig[...] = sigmoid(raw)
    decay = step * (hp_ref[1:2, :] * LOG2E)
    lower = (iota((Q, Q), 0) >= iota((Q, Q), 1)).astype(F32)
    sums = [
        jnp.dot(lower, decay[c * Q : (c + 1) * Q], precision=HIGHEST, preferred_element_type=F32) for c in range(2)
    ]
    last = start_of(Q - 1, b1, b2)
    out = jnp.where(rows[:Q] >= last, jnp.exp2(sums[0][Q - 1 : Q, :] - sums[0]), 0.0)
    into = jnp.where(start_of(rows[Q:], b1, b2) <= Q - 1, jnp.exp2(sums[1]), 0.0)
    middle = jnp.where(real, jnp.concatenate([out, into], 0), 0.0)
    expand[...] = side_by_side(terms(step, 2) + terms(middle, 2)).astype(BF)
    split = side_by_side(terms(jnp.concatenate(sums, 0), 3))
    used = lane % 64 < 3 * HEADS
    late[...] = jnp.where(used & (lane >= 64), 1.0, split).astype(BF)
    early[...] = jnp.where(used & (lane < 64), 1.0, pltpu.roll(-split, 64, 1)).astype(BF)


def both_heads(v, t):
    lane = iota(v.shape, 1) % HEADS
    zero = jnp.zeros_like(v)
    return jnp.concatenate([jnp.where(lane == 2 * t, v, zero), jnp.where(lane == 2 * t + 1, v, zero)], 0)


def spread_over(expand, t):
    row, col = iota((LANES, 2 * LANES), 0), iota((LANES, 2 * LANES), 1)
    head = 2 * t + (col % LANES) // P_SIZE
    pick = (row % HEADS == head) & (row // (2 * HEADS) == col // LANES)
    both = mm(expand[...], pick.astype(BF))
    return both[:, :LANES], both[:, LANES:]


def allowed(c, b1, b2, transposed):
    late = iota((Q, Q), 1 if transposed else 0) + c * Q
    early = iota((Q, Q), 0 if transposed else 1) + c * Q
    return (early <= late) & (early >= start_of(late, b1, b2))


def fwd_kernel(bnd, xs_ref, bc_ref, dt_ref, cwx_ref, cwb_ref, hp_ref, out_ref,
               lk, score, bmat, cmat, btrans, late, early, expand):
    b = pl.program_id(0)
    prepare(bnd[b, 0], bnd[b, 1], bc_ref, dt_ref, cwb_ref, hp_ref, lk, score, bmat, cmat,
            btrans, None, None, None, late, early, expand, False)
    for t in range(TILES):
        fwd_tile(t, slice(t * LANES, (t + 1) * LANES), xs_ref, cwx_ref, out_ref,
                 lk, score, cmat, btrans, late, early, expand)


def fwd_tile(t, at, xs_ref, cwx_ref, out_ref, lk, score, cmat, btrans, late, early, expand):
    taps, bias = taps_of(cwx_ref, at)
    pre = conv_pre(xs_ref[:, at].astype(F32), taps, bias, [lk[0], lk[1], lk[2]])
    x = pre * sigmoid(pre)
    first = iota((TOK, LANES), 1) < P_SIZE
    dtx, middle = spread_over(expand, t)
    xt = x * dtx
    xt16 = xt.astype(BF)
    half = Q // 2
    outs = []
    for c in range(2):
        o = c * Q
        for rows, width in ((slice(o, o + half), half), (slice(o + half, o + Q), Q)):
            last = rows.stop - o
            w = mm_nt(both_heads(late[rows, :], t), early[o : o + width, :])
            s = score[c, last - half : last, :width]
            w = jnp.exp2(jnp.minimum(w, 0.0)) * jnp.concatenate([s, s], 0)
            y = mm(w.astype(BF), xt16[o : o + width])
            outs.append(jnp.where(first[:half], y[:half], y[half:]))
    outs = [jnp.concatenate(outs[:2], 0), jnp.concatenate(outs[2:], 0)]
    state = mm(btrans[...], (middle[:Q] * xt[:Q]).astype(BF))
    outs[1] = outs[1] + mm(cmat[Q:, :], state.astype(BF)) * middle[Q:]
    skip = cwx_ref[5:6, at]
    out_ref[:, at] = jnp.concatenate(outs, 0) + skip * x


def conv_back(dact, pre, sg, xin, taps, links):
    dpre = dact * (sg * (1.0 + pre * (1.0 - sg)))
    g = taps[3] * dpre
    sums = [None] * 5
    sums[3] = jnp.sum(dpre * xin, axis=0, keepdims=True)
    sums[4] = jnp.sum(dpre, axis=0, keepdims=True)
    for k in range(1, 4):
        q = links[k - 1] * dpre
        g = g + taps[3 - k] * pltpu.roll(q, TOK - k, 0)
        sums[3 - k] = jnp.sum(q * pltpu.roll(xin, k, 0), axis=0, keepdims=True)
    return g, sums


def bwd_tile(t, at, xs_ref, cwx_ref, scan_ref, dscan_ref, out_ref, dcw_ref,
             lk, score, bmat, btrans, ctrans, late, early, expand, dscore, rsum, rsum3, dball, dcall):
    taps, bias = taps_of(cwx_ref, at)
    links = [lk[0], lk[1], lk[2]]
    xin = xs_ref[:, at].astype(F32)
    pre = conv_pre(xin, taps, bias, links)
    sg = sigmoid(pre)
    x = pre * sg
    first = iota((TOK, LANES), 1) < P_SIZE
    dtx, middle = spread_over(expand, t)
    xt = x * dtx
    xt16 = xt.astype(BF)
    xtf = xt16.astype(F32)
    skip = cwx_ref[5:6, at]
    dy16 = dscan_ref[:, at]
    dy = dy16.astype(F32)
    dyf = dy
    zero = jnp.zeros((Q // 2, LANES), BF)
    half = Q // 2
    parts = []
    for c in range(2):
        o = c * Q
        for rows, begin in ((slice(o, o + half), 0), (slice(o + half, o + Q), half)):
            at_row = slice(begin, begin + half)
            later = slice(o + begin, o + Q)
            w = jnp.exp2(jnp.minimum(mm_nt(both_heads(early[rows, :], t), late[later, :]), 0.0))
            xr = xt16[rows]
            xr = jnp.concatenate([jnp.where(first[:half], xr, zero), jnp.where(first[:half], zero, xr)], 0)
            wp = w * mm_nt(xr, dy16[later])
            dscore[c, at_row, begin:] += wp[:half] + wp[half:]
            s = score[c, at_row, begin:]
            y = mm((w * jnp.concatenate([s, s], 0)).astype(BF), dy16[later])
            parts.append(jnp.where(first[:half], y[:half], y[half:]))
    parts = [jnp.concatenate(parts[:2], 0), jnp.concatenate(parts[2:], 0)]
    tx, ex = middle[:Q], middle[Q:]
    txt16 = (tx * xt[:Q]).astype(BF)
    state = mm(btrans[...], txt16).astype(BF)
    dye = (ex * dy[Q:]).astype(BF)
    dstate = mm(ctrans[...], dye).astype(BF)
    dcall[...] += mm_nt(dye, state)
    dball[...] += mm_nt(txt16, dstate)
    across = tx * mm(bmat[:Q, :], dstate)
    within = jnp.concatenate(parts, 0)
    dxt = jnp.concatenate([parts[0] + across, parts[1]], 0)
    r1 = dyf * (scan_ref[:, at] - skip * x) - xtf * within
    r2 = x * dxt
    r3 = xtf[:Q] * across

    hi = r1.astype(BF)
    row, col = iota((2 * LANES, LANES), 0), iota((2 * LANES, LANES), 1)
    pick = (col == 2 * t + (row % LANES) // P_SIZE).astype(BF)
    rsum[...] += mm(jnp.concatenate([hi, (r1 - hi.astype(F32)).astype(BF)], 1), pick)
    row, col = iota((2 * LANES, 2 * LANES), 0), iota((2 * LANES, 2 * LANES), 1)
    pick = ((col % LANES == 2 * t + (row % LANES) // P_SIZE) & (row // LANES == col // LANES)).astype(BF)
    r3 = jnp.concatenate([r3, jnp.zeros_like(r3)], 0)
    rsum3[...] += mm(jnp.concatenate([r2.astype(BF), r3.astype(BF)], 1), pick)
    g, sums = conv_back(dxt * dtx + skip * dy, pre, sg, xin, taps, links)
    sums.append(jnp.sum(dy * x, axis=0, keepdims=True))
    sums.append(jnp.zeros((2, LANES), F32))
    out_ref[:, at] = g.astype(BF)
    dcw_ref[:, at] += jnp.concatenate(sums, 0)


def bwd_kernel(bnd, xs_ref, bc_ref, dt_ref, cwx_ref, cwb_ref, hp_ref, scan_ref, dscan_ref,
               out_ref, dcw_ref, dhp_ref,
               lk, score, bmat, cmat, btrans, late, early, expand, ctrans, dts, sig, dscore, rsum, rsum3, dball, dcall):
    b = pl.program_id(0)
    b1, b2 = bnd[b, 0], bnd[b, 1]

    @pl.when(b == 0)
    def _():
        dcw_ref[...] = jnp.zeros_like(dcw_ref)
        dhp_ref[...] = jnp.zeros_like(dhp_ref)

    prepare(b1, b2, bc_ref, dt_ref, cwb_ref, hp_ref, lk, score, bmat, cmat,
            btrans, ctrans, dts, sig, late, early, expand, True)
    for v in (dscore, rsum, rsum3, dball, dcall):
        v[...] = jnp.zeros_like(v)
    for t in range(TILES):
        bwd_tile(t, slice(t * LANES, (t + 1) * LANES), xs_ref, cwx_ref, scan_ref, dscan_ref, out_ref, dcw_ref,
                 lk, score, bmat, btrans, ctrans, late, early, expand, dscore, rsum, rsum3, dball, dcall)
    links = [lk[0], lk[1], lk[2]]

    db, dc = [], []
    for c in range(2):
        part = slice(c * Q, (c + 1) * Q)
        ds = jnp.where(allowed(c, b1, b2, True), dscore[c], 0.0)
        db.append(mm(ds.astype(BF), cmat[part, :]))
        dc.append(mm(ds.T.astype(BF), bmat[part, :]))
    db[0] = db[0] + dball[...]
    dc[1] = dc[1] + dcall[...]
    base = TILES * LANES
    for i, dact in enumerate((jnp.concatenate(db, 0), jnp.concatenate(dc, 0))):
        lanes = slice(i * LANES, (i + 1) * LANES)
        taps_b, bias_b = taps_of(cwb_ref, lanes)
        xin_b = bc_ref[:, lanes].astype(F32)
        pre_b = conv_pre(xin_b, taps_b, bias_b, links)
        g, sums = conv_back(dact, pre_b, sigmoid(pre_b), xin_b, taps_b, links)
        sums.append(jnp.zeros((3, LANES), F32))
        at = slice(base + i * LANES, base + (i + 1) * LANES)
        out_ref[:, at] = g.astype(BF)
        dcw_ref[:, at] += jnp.concatenate(sums, 0)
    upper = (iota((Q, Q), 0) <= iota((Q, Q), 1)).astype(F32)
    below = (iota((Q, Q), 0) > iota((Q, Q), 1)).astype(F32)
    high = functools.partial(jnp.dot, precision=HIGHEST, preferred_element_type=F32)
    rate = hp_ref[1:2, :]
    da = jnp.concatenate(
        [
            high(upper, rsum[:Q, :]) + high(below, rsum3[:Q, LANES:]),
            high(upper, rsum[Q:, :]),
        ],
        0,
    )
    step = dts[...]
    draw = (rsum3[:, :LANES] + da * rate) * sig[...]
    dhp_ref[0:1, :] += jnp.sum(draw, axis=0, keepdims=True)
    dhp_ref[1:2, :] += jnp.sum(da * (rate * step), axis=0, keepdims=True)
    out_ref[:, base + 2 * LANES :] = draw[:, :HEADS].astype(BF)


def params(*semantics, mib=48):
    return pltpu.CompilerParams(dimension_semantics=semantics, vmem_limit_bytes=mib * 1024 * 1024)


def cost(flops, moved):
    return pl.CostEstimate(flops=int(flops / 16), bytes_accessed=int(moved / 16), transcendentals=0)


def block_scratch(extra):
    column = pltpu.VMEM((TOK, LANES), F32)
    packed = pltpu.VMEM((TOK, LANES), BF)
    part = pltpu.VMEM((Q, LANES), F32)
    half = pltpu.VMEM((LANES, Q), BF)
    square = pltpu.VMEM((2, Q, Q), F32)
    base = [pltpu.VMEM((3, TOK, LANES), F32), square, packed, packed, half, packed, packed, packed]
    if not extra:
        return base
    return base + [half, column, column, square, column, pltpu.VMEM((TOK, 2 * LANES), F32), part, part]


def mixer_specs(first):
    return [
        pl.BlockSpec((TOK, TILES * LANES), lambda b, *_: (b + first, 0)),
        pl.BlockSpec((TOK, 2 * LANES), lambda b, *_: (b + first, TILES // 2)),
        pl.BlockSpec((TOK, LANES), lambda b, *_: (b + first, TILES + 2)),
        pl.BlockSpec((8, TILES * LANES), lambda b, *_: (0, 0)),
        pl.BlockSpec((8, 2 * LANES), lambda b, *_: (0, TILES // 2)),
        pl.BlockSpec((8, LANES), lambda b, *_: (0, 0)),
    ]


ANY = pl.BlockSpec(memory_space=pl.ANY)


def fwd_into(bnd, *refs):
    fwd_kernel(bnd, *refs[:6], *refs[7:])


def scan_forward(bounds, proj, cw, hp, first, count, into=None):
    return pl.pallas_call(
        fwd_kernel if into is None else fwd_into,
        out_shape=jax.ShapeDtypeStruct((proj.shape[0], TILES * LANES), F32),
        grid_spec=pltpu.PrefetchScalarGridSpec(
            num_scalar_prefetch=1,
            grid=(count,),
            in_specs=mixer_specs(first) + ([] if into is None else [ANY]),
            out_specs=pl.BlockSpec((TOK, TILES * LANES), lambda b, *_: (b + first, 0)),
            scratch_shapes=block_scratch(False),
        ),
        input_output_aliases={} if into is None else {7: 0},
        compiler_params=params("arbitrary"),
        cost_estimate=cost(count * 8e9, count * 4e6),
    )(bounds[first : first + count], proj, proj, proj, cw, cw, hp, *([] if into is None else [into]))


def bwd_into(bnd, *refs):
    bwd_kernel(bnd, *refs[:8], *refs[9:])


def scan_backward(bounds, proj, cw, hp, scan, dscan, first, count, into=None):
    tile = pl.BlockSpec((TOK, TILES * LANES), lambda b, *_: (b + first, 0))
    return pl.pallas_call(
        bwd_kernel if into is None else bwd_into,
        out_shape=(
            jax.ShapeDtypeStruct((proj.shape[0], REST), BF),
            jax.ShapeDtypeStruct((8, (TILES + 2) * LANES), F32),
            jax.ShapeDtypeStruct((8, LANES), F32),
        ),
        grid_spec=pltpu.PrefetchScalarGridSpec(
            num_scalar_prefetch=1,
            grid=(count,),
            in_specs=mixer_specs(first) + [tile, tile] + ([] if into is None else [ANY]),
            out_specs=(
                pl.BlockSpec((TOK, REST), lambda b, *_: (b + first, 0)),
                pl.BlockSpec((8, (TILES + 2) * LANES), lambda b, *_: (0, 0)),
                pl.BlockSpec((8, LANES), lambda b, *_: (0, 0)),
            ),
            scratch_shapes=block_scratch(True),
        ),
        input_output_aliases={} if into is None else {9: 0},
        compiler_params=params("arbitrary"),
        cost_estimate=cost(count * 16e9, count * 6e6),
    )(
        bounds[first : first + count],
        proj, proj, proj,
        cw,
        cw,
        hp,
        scan, dscan,
        *([] if into is None else [into]),
    )


def whole_once(a):
    return pl.BlockSpec(a.shape, lambda i, *_: (0, 0), pipeline_mode=pl.Buffered(1))


def ginner_kernel(perm, gout_ref, *refs):
    pieces, (out_ref, wide_ref, gate_ref) = refs[:-3], refs[-3:]
    inner = TILES * LANES

    @pl.when(pl.program_id(0) == 0)
    def _():
        for p, piece in enumerate(pieces):
            rows = pl.ds(pl.multiple_of(perm[p] * LANES, LANES), LANES)
            for k in range(8):
                wide_ref[rows, k * 256 : (k + 1) * 256] = piece[inner + k * LANES : inner + (k + 1) * LANES, :]
            gate_ref[:, p * 256 : (p + 1) * 256] = piece[:inner, :]

    out_ref[...] = mm_nt(gout_ref[...], wide_ref[...]).astype(BF)


def inner_gradient(perm, gout, pieces):
    rows, inner = gout.shape[0], TILES * LANES
    whole = pl.BlockSpec((inner, D), lambda i, *_: (0, 0))
    return pl.pallas_call(
        ginner_kernel,
        out_shape=(jax.ShapeDtypeStruct((rows, inner), BF), jax.ShapeDtypeStruct((inner, D), BF), jax.ShapeDtypeStruct((inner, D), BF)),
        grid_spec=pltpu.PrefetchScalarGridSpec(
            num_scalar_prefetch=1,
            grid=(rows // TOK,),
            in_specs=[pl.BlockSpec((TOK, D), lambda i, *_: (i, 0))] + [whole_once(a) for a in pieces],
            out_specs=(pl.BlockSpec((TOK, inner), lambda i, *_: (i, 0)), whole, whole),
        ),
        compiler_params=params("arbitrary"),
        cost_estimate=cost(2 * rows * inner * D, 2 * (rows * D + rows * inner + 4 * inner * D)),
    )(perm, gout, *pieces)


def out_kernel(perm, inner_ref, gout_ref, out_ref, turned, result):
    @pl.when(pl.program_id(0) == 0)
    def _():
        turned[...] = inner_ref[...].T

    result[...] = mm(turned[...], gout_ref[...])
    for p in range(8):
        rows = pl.ds(pl.multiple_of(perm[p] * LANES, LANES), LANES)
        out_ref[:, p * 256 : (p + 1) * 256] = result[rows, :].astype(BF)


def out_terms(perm, inner, gout):
    rows, wide = inner.shape
    return pl.pallas_call(
        out_kernel,
        out_shape=jax.ShapeDtypeStruct((wide, D), BF),
        grid_spec=pltpu.PrefetchScalarGridSpec(
            num_scalar_prefetch=1,
            grid=(8,),
            in_specs=[
                pl.BlockSpec((rows, wide), lambda k, *_: (0, 0)),
                pl.BlockSpec((rows, 256), lambda k, *_: (0, k)),
            ],
            out_specs=pl.BlockSpec((LANES, D), lambda k, *_: (k, 0)),
            scratch_shapes=[pltpu.VMEM((wide, rows), BF), pltpu.VMEM((wide, 256), F32)],
        ),
        compiler_params=params("arbitrary", mib=48),
        cost_estimate=cost(2 * rows * wide * D, 2 * (rows * wide + rows * D + wide * D)),
    )(perm, inner, gout)


def stat_kernel(norm_ref, w_ref, scan_ref, gin_ref, gain_ref, gate_ref, out_ref):
    gate_ref[...] = mm_nt(norm_ref[...], w_ref[...]).astype(BF)
    one = two = jnp.zeros((TOK, LANES), F32)
    for t in range(TILES):
        at = slice(t * LANES, (t + 1) * LANES)
        gate = gate_ref[:, at].astype(F32)
        gated = scan_ref[:, at] * (gate * sigmoid(gate))
        one = one + gated * gated
        two = two + gated * (gin_ref[:, at].astype(F32) * gain_ref[:, at])
    a = jnp.sum(one.T, axis=0, keepdims=True)
    c = jnp.sum(two.T, axis=0, keepdims=True)
    out_ref[0] = jnp.concatenate([a, c, jnp.zeros((6, TOK), F32)], 0)


def gate_stats(normed, w_gate, scan, ginner, gain):
    rows, inner = scan.shape
    tile = pl.BlockSpec((TOK, inner), lambda b: (b, 0))
    return pl.pallas_call(
        stat_kernel,
        out_shape=(jax.ShapeDtypeStruct((rows, inner), BF), jax.ShapeDtypeStruct((rows // TOK, 8, TOK), F32)),
        grid=(rows // TOK,),
        in_specs=[
            pl.BlockSpec((TOK, D), lambda b: (b, 0)),
            pl.BlockSpec((inner, D), lambda b: (0, 0)),
            tile,
            tile,
            pl.BlockSpec((1, inner), lambda b: (0, 0)),
        ],
        out_specs=(tile, pl.BlockSpec((1, 8, TOK), lambda b: (b, 0, 0))),
        compiler_params=params("arbitrary", mib=48),
        cost_estimate=cost(2 * rows * inner * D, rows * (D * 2 + inner * 8) + inner * D * 2),
    )(normed, w_gate, scan, ginner, gain)


def gate_kernel(sum_ref, scan_ref, gate_ref, gin_ref, gain_ref, inner_ref, dgate_ref, dscan_ref, dgain_ref):
    rows = scan_ref.shape[0]

    @pl.when((pl.program_id(0) == 0) & (pl.program_id(1) == 0))
    def _():
        dgain_ref[...] = jnp.zeros_like(dgain_ref)

    r = lax.rsqrt(sum_ref[0, 0:1, :] * (1.0 / DIN) + EPSILON)
    c = r * r * sum_ref[0, 1:2, :] * (1.0 / DIN)
    rinv = jnp.broadcast_to(r, (LANES, rows)).T
    coef = jnp.broadcast_to(c, (LANES, rows)).T
    for t in range(TILES):
        at = slice(t * LANES, (t + 1) * LANES)
        gate = gate_ref[:, at].astype(F32)
        sg = sigmoid(gate)
        act = gate * sg
        scan = scan_ref[:, at]
        gain = gain_ref[:, at]
        gated = scan * act
        scaled = gated * rinv
        gin = gin_ref[:, at].astype(F32)
        inner_ref[:, at] = (scaled * gain).astype(BF)
        dgated = rinv * (gin * gain - gated * coef)
        dscan_ref[:, at] = (dgated * act).astype(BF)
        dgate_ref[:, at] = (dgated * scan * (sg + act * (1.0 - sg))).astype(BF)
        dgain_ref[0:1, at] += jnp.sum(gin * scaled, axis=0, keepdims=True)


def gate_both(sums, scan, gate, ginner, gain):
    rows, inner = scan.shape
    tile = pl.BlockSpec((Q, inner), lambda b, h: (2 * b + h, 0))
    whole = jax.ShapeDtypeStruct((rows, inner), BF)
    return pl.pallas_call(
        gate_kernel,
        out_shape=(whole, whole, whole, jax.ShapeDtypeStruct((8, inner), F32)),
        grid=(rows // TOK, 2),
        in_specs=[
            pl.BlockSpec((1, 8, Q), lambda b, h: (b, 0, h)),
            tile,
            tile,
            tile,
            pl.BlockSpec((1, inner), lambda b, h: (0, 0)),
        ],
        out_specs=(tile, tile, tile, pl.BlockSpec((8, inner), lambda b, h: (0, 0))),
        compiler_params=params("arbitrary", "arbitrary", mib=48),
        cost_estimate=cost(0, rows * inner * 14),
    )(sums, scan, gate, ginner, gain)


def back_kernel(a_ref, wa_ref, b_ref, wb_ref, norm_ref, out_ref, dgo_ref):
    @pl.when(pl.program_id(0) == 0)
    def _():
        dgo_ref[...] = jnp.zeros_like(dgo_ref)

    for c in range(4):
        at = slice(c * 512, (c + 1) * 512)
        res = mm(a_ref[...], wa_ref[:, at]) + mm(b_ref[...], wb_ref[:, at])
        out_ref[:, at] = res.astype(BF)
        dgo_ref[0:1, at] += jnp.sum(res * norm_ref[:, at].astype(F32), axis=0, keepdims=True)


def normed_gradient(gproj, w_rest, dgate, w_two, normed, first, count):
    rows, inner = dgate.shape
    row = lambda width: pl.BlockSpec((TOK, width), lambda b: (b + first, 0))
    return pl.pallas_call(
        back_kernel,
        out_shape=(jax.ShapeDtypeStruct((count * TOK, D), BF), jax.ShapeDtypeStruct((8, D), F32)),
        grid=(count,),
        in_specs=[
            row(REST),
            pl.BlockSpec((REST, D), lambda b: (0, 0)),
            row(inner),
            pl.BlockSpec((inner, D), lambda b: (0, 0)),
            row(D),
        ],
        out_specs=(pl.BlockSpec((TOK, D), lambda b: (b, 0)), pl.BlockSpec((8, D), lambda b: (0, 0))),
        compiler_params=params("arbitrary", mib=48),
        cost_estimate=cost(2 * count * TOK * D * (REST + inner), 2 * (REST + inner) * D),
    )(gproj, w_rest, dgate, w_two, normed)


def across_kernel(a_ref, b_ref, out_ref, *turned):
    if len(turned) == 2:
        (kept, turned) = turned

        @pl.when(pl.program_id(0) == 0)
        def _():
            turned[...] = a_ref[...].T
            kept[...] = turned[...]
    else:
        turned = a_ref
    out_ref[0] = mm(turned[...], b_ref[...]).astype(out_ref.dtype)


def across_rows(a, b, first, count, turn):
    rows, n = b.shape
    m = a.shape[1] if turn else a.shape[0]
    whole = pl.BlockSpec(a.shape, lambda k: (0, 0))
    part = jax.ShapeDtypeStruct((count, m, 256), BF)
    spec = pl.BlockSpec((1, m, 256), lambda k: (k, 0, 0))
    return pl.pallas_call(
        across_kernel,
        out_shape=(part, jax.ShapeDtypeStruct((m, rows), BF)) if turn else part,
        grid=(count,),
        in_specs=[whole, pl.BlockSpec((rows, 256), lambda k: (0, k + first))],
        out_specs=(spec, pl.BlockSpec((m, rows), lambda k: (0, 0))) if turn else spec,
        scratch_shapes=[pltpu.VMEM((m, rows), BF)] if turn else [],
        compiler_params=params("arbitrary", mib=48),
        cost_estimate=cost(2 * rows * m * 256 * count, 2 * (rows * m + rows * 256 * count + m * 256 * count)),
    )(a, b)


def pick_rest_kernel(me, *refs):
    tiles, (shared, steps, out_ref) = refs[:TILES], refs[TILES:]
    for t, ref in enumerate(tiles):
        out_ref[t * LANES : (t + 1) * LANES, :] = ref[...].astype(BF)
    wide = TILES * LANES
    out_ref[wide : wide + 2 * N, :] = shared[...].astype(BF)
    mine, head = iota((HEADS, H), 0), iota((HEADS, H), 1)
    pick = (head == 8 * (mine // 2) + 2 * me[0] + mine % 2).astype(BF)
    out_ref[wide + 2 * N :, :] = mm(pick, steps[...].astype(BF)).astype(BF)


def tile_spec(lanes, t):
    return pl.BlockSpec((LANES, lanes), lambda i, me: (4 * t + me[0], 0))


def pick_rest(me, turned):
    lanes = turned.shape[1]
    fixed = lambda rows, at: pl.BlockSpec((rows, lanes), lambda i, me: (at // rows, 0))
    return pl.pallas_call(
        pick_rest_kernel,
        out_shape=jax.ShapeDtypeStruct((REST, lanes), BF),
        grid_spec=pltpu.PrefetchScalarGridSpec(
            num_scalar_prefetch=1,
            grid=(1,),
            in_specs=[tile_spec(lanes, TILES + t) for t in range(TILES)] + [fixed(2 * N, 2 * DIN), fixed(H, 2 * DIN + 2 * N)],
            out_specs=pl.BlockSpec((REST, lanes), lambda i, me: (0, 0)),
        ),
        compiler_params=params("arbitrary"),
        cost_estimate=cost(0, 6 * REST * lanes),
    )(me, *[turned] * (TILES + 2))


def pick_two_kernel(me, *refs):
    tiles, (rows, out_ref) = refs[:TILES], refs[TILES:]
    for t, ref in enumerate(tiles):
        out_ref[t * LANES : (t + 1) * LANES, :] = ref[...].astype(BF)
    wide = TILES * LANES
    for k in range(8):
        out_ref[wide + k * LANES : wide + (k + 1) * LANES, :] = rows[:, k * 256 : (k + 1) * 256].astype(BF)


def pick_two(me, turned, out_weight):
    lanes = turned.shape[1]
    return pl.pallas_call(
        pick_two_kernel,
        out_shape=jax.ShapeDtypeStruct((2 * TILES * LANES, lanes), BF),
        grid_spec=pltpu.PrefetchScalarGridSpec(
            num_scalar_prefetch=1,
            grid=(1,),
            in_specs=[tile_spec(lanes, t) for t in range(TILES)] + [pl.BlockSpec((LANES, D), lambda i, me: (me[0], 0))],
            out_specs=pl.BlockSpec((2 * TILES * LANES, lanes), lambda i, me: (0, 0)),
        ),
        compiler_params=params("arbitrary"),
        cost_estimate=cost(0, 12 * TILES * LANES * lanes),
    )(me, *[turned] * TILES, out_weight)


def pick_gate_kernel(me, *refs):
    for t, ref in enumerate(refs[:-1]):
        refs[-1][t * LANES : (t + 1) * LANES, :] = ref[...].astype(BF)


def pick_gate(me, turned):
    lanes = turned.shape[1]
    return pl.pallas_call(
        pick_gate_kernel,
        out_shape=jax.ShapeDtypeStruct((TILES * LANES, lanes), BF),
        grid_spec=pltpu.PrefetchScalarGridSpec(
            num_scalar_prefetch=1,
            grid=(1,),
            in_specs=[tile_spec(lanes, t) for t in range(TILES)],
            out_specs=pl.BlockSpec((TILES * LANES, lanes), lambda i, me: (0, 0)),
        ),
        compiler_params=params("arbitrary"),
        cost_estimate=cost(0, 6 * TILES * LANES * lanes),
    )(me, *[turned] * TILES)


STEP = 128


def norm_kernel(perm, tok_ref, gain_ref, out_ref):
    x = tok_ref[...].astype(F32)
    inv = lax.rsqrt(jnp.mean(x * x, axis=1, keepdims=True) + EPSILON)
    wide = D // 8
    for k in range(8):
        here = pl.ds(pl.multiple_of(perm[k] * wide, wide), wide)
        out_ref[:, k * wide : (k + 1) * wide] = (
            tok_ref[:, here].astype(F32) * inv * gain_ref[:, here]
        ).astype(BF)


def norm_rows(perm, tokens, gain):
    rows = tokens.shape[0]
    row = pl.BlockSpec((STEP, D), lambda i, *_: (i, 0))
    return pl.pallas_call(
        norm_kernel,
        out_shape=jax.ShapeDtypeStruct((rows, D), BF),
        grid_spec=pltpu.PrefetchScalarGridSpec(
            num_scalar_prefetch=1,
            grid=(rows // STEP,),
            in_specs=[row, pl.BlockSpec((1, D), lambda i, *_: (0, 0))],
            out_specs=row,
        ),
        compiler_params=params("arbitrary"),
        cost_estimate=pl.CostEstimate(flops=0, bytes_accessed=rows * D * 4, transcendentals=0),
    )(perm, tokens, gain)


def last_kernel(perm, tok_ref, cot_ref, keep_ref, gain_ref, one_ref, two_ref, three_ref, out_ref, grad):
    wide = D // 8
    for k in range(8):
        here = pl.ds(pl.multiple_of(perm[k] * wide, wide), wide)
        at = slice(k * wide, (k + 1) * wide)
        grad[:, here] = (
            one_ref[:, at].astype(F32) + two_ref[:, at].astype(F32) + three_ref[:, at].astype(F32)
        ) * gain_ref[:, here]
    x = tok_ref[...].astype(F32)
    inv = lax.rsqrt(jnp.mean(x * x, axis=1, keepdims=True) + EPSILON)
    g = grad[...]
    dot = jnp.mean(g * x, axis=1, keepdims=True)
    out_ref[...] = inv * (g - x * (inv * inv * dot)) + keep_ref[...] * cot_ref[...].astype(F32)


def last_rows(perm, tokens, cotangent, keep, gain, parts):
    rows = tokens.shape[0]
    row = pl.BlockSpec((STEP, D), lambda i, *_: (i, 0))
    return pl.pallas_call(
        last_kernel,
        out_shape=jax.ShapeDtypeStruct((rows, D), F32),
        grid_spec=pltpu.PrefetchScalarGridSpec(
            num_scalar_prefetch=1,
            grid=(rows // STEP,),
            in_specs=[
                row,
                row,
                pl.BlockSpec((STEP, 1), lambda i, *_: (i, 0)),
                pl.BlockSpec((1, D), lambda i, *_: (0, 0)),
                row,
                row,
                row,
            ],
            out_specs=row,
            scratch_shapes=[pltpu.VMEM((STEP, D), F32)],
        ),
        compiler_params=params("arbitrary"),
        cost_estimate=pl.CostEstimate(flops=0, bytes_accessed=rows * D * 14, transcendentals=0),
    )(perm, tokens, cotangent, keep, gain, *parts)


def first_join_kernel(me, *refs):
    pieces, (out_ref, grad_ref, stage, sem) = refs[:4], refs[4:]
    inner = TILES * LANES
    for k in range(4):
        q = jnp.bitwise_xor(me[0], k)
        for t in range(TILES):
            rows = pl.ds(pl.multiple_of((4 * t + q) * LANES, LANES), LANES)
            stage[rows, :] = pieces[k][t * LANES : (t + 1) * LANES, :].astype(F32)
    copy = pltpu.make_async_copy(stage, out_ref.at[pl.ds(0, 4 * inner)], sem)
    copy.start()
    for k in range(4):
        q = jnp.bitwise_xor(me[0], k)
        rows = pl.ds(pl.multiple_of(q * LANES, LANES), LANES)
        for c in range((pieces[k].shape[0] - inner) // LANES):
            grad_ref[rows, c * 256 : (c + 1) * 256] = pieces[k][
                inner + c * LANES : inner + (c + 1) * LANES, :
            ].astype(F32)
    copy.wait()


def first_join(me, pieces, width):
    lanes = pieces[0].shape[1]
    whole = pl.BlockSpec(pieces[0].shape, lambda i, *_: (0, 0))
    return pl.pallas_call(
        first_join_kernel,
        out_shape=(
            jax.ShapeDtypeStruct((width, lanes), F32),
            jax.ShapeDtypeStruct((4 * LANES, D), F32),
        ),
        grid_spec=pltpu.PrefetchScalarGridSpec(
            num_scalar_prefetch=1,
            grid=(1,),
            in_specs=[whole] * 4,
            out_specs=(ANY, pl.BlockSpec((4 * LANES, D), lambda i, *_: (0, 0))),
            scratch_shapes=[pltpu.VMEM((4 * TILES * LANES, lanes), F32), pltpu.SemaphoreType.DMA],
        ),
        compiler_params=params("arbitrary", mib=48),
        cost_estimate=cost(0, 320e6),
    )(me, *pieces)


def last_join_kernel(me, one, two, three, four, into, out_ref, stage, sem):
    pieces = (one, two, three, four)
    inner = TILES * LANES
    few = H // 4
    for k in range(4):
        q = jnp.bitwise_xor(me[0], k)
        for t in range(TILES):
            rows = pl.ds(pl.multiple_of((4 * t + q) * LANES, LANES), LANES)
            stage[rows, :] = pieces[k][t * LANES : (t + 1) * LANES, :].astype(F32)
    stage[4 * inner : 4 * inner + 2 * N, :] = sum(p[inner : inner + 2 * N, :].astype(F32) for p in pieces)
    steps = None
    for k in range(4):
        q = jnp.bitwise_xor(me[0], k)
        head, mine = iota((H, few), 0), iota((H, few), 1)
        spread = (head == 8 * (mine // 2) + 2 * q + mine % 2).astype(BF)
        term = mm(spread, pieces[k][inner + 2 * N :, :])
        steps = term if steps is None else steps + term
    stage[4 * inner + 2 * N :, :] = steps
    copy = pltpu.make_async_copy(stage, out_ref.at[pl.ds(4 * inner, stage.shape[0])], sem)
    copy.start()
    copy.wait()


def last_join(me, pieces, into):
    lanes = pieces[0].shape[1]
    whole = pl.BlockSpec(pieces[0].shape, lambda i, *_: (0, 0))
    return pl.pallas_call(
        last_join_kernel,
        out_shape=jax.ShapeDtypeStruct(into.shape, F32),
        grid_spec=pltpu.PrefetchScalarGridSpec(
            num_scalar_prefetch=1,
            grid=(1,),
            in_specs=[whole] * 4 + [ANY],
            out_specs=ANY,
            scratch_shapes=[pltpu.VMEM((into.shape[0] - 4 * TILES * LANES, lanes), F32), pltpu.SemaphoreType.DMA],
        ),
        input_output_aliases={5: 0},
        compiler_params=params("arbitrary"),
        cost_estimate=cost(0, 8e6),
    )(me, *pieces, into)


def tie(*arrays):
    return lax.optimization_barrier(arrays)


def swap(x, d):
    return lax.ppermute(x, "rep", [(i, i ^ d) for i in range(4)])


def fw(x):
    return lax.ppermute(x, "shard", [(RING[i], RING[(i + 1) % 8]) for i in range(8)])


def bw(x):
    return lax.ppermute(x, "shard", [(RING[(i + 1) % 8], RING[i]) for i in range(8)])


def relative(s, n):
    if n != 8:
        return jnp.arange(8, dtype=jnp.int32), jnp.arange(8, dtype=jnp.int32)
    table, inverse = [], []
    for shard in range(8):
        p = RING.index(shard)
        row = [RING[(p + d) % 8] for d in (0, -1, 1, -2, 2, -3, 3, 4)]
        table.append(row)
        inverse.append([row.index(i) for i in range(8)])
    return jnp.asarray(table, jnp.int32)[s], jnp.asarray(inverse, jnp.int32)[s]


def cut(rows):
    return -(-rows // 32) * 16


def ring_pieces(piece, pieces):
    half = cut(piece.shape[0])
    a = b = piece
    pieces.append(piece)
    for _ in range(3):
        a, b = yield fw(a), bw(b)
        pieces += [a, b]
    a, b = yield fw(a[:half]), bw(b[half:])
    pieces.append(jnp.concatenate([a, b], 0))
    yield


def add16(a, b):
    return (a.astype(F32) + b.astype(F32)).astype(BF)


def ring_sum():
    far = yield
    half = cut(far.shape[0])
    rf, rb, (own, f1, b1, f2, b2, f3, b3) = yield far[:half], far[half:]
    sf = jnp.concatenate([add16(b3[:half], rf), b3[half:]], 0)
    sb = jnp.concatenate([f3[:half], add16(f3[half:], rb)], 0)
    rf, rb = yield sf, sb
    rf, rb = yield add16(b2, rf), add16(f2, rb)
    rf, rb = yield add16(b1, rf), add16(f1, rb)
    yield (own.astype(F32) + rf.astype(F32) + rb.astype(F32)).astype(BF)


def launch(steps, arrived, *others):
    forward, backward, *others = tie(*steps.send(arrived), *others)
    return [fw(forward), bw(backward)], *others


def blocks_of(x):
    return [x[k * TOK : (k + 1) * TOK] for k in range(4)]


def sum_rep(parts):
    far = swap(parts[3], 1)
    chip = swap((parts[2].astype(F32) + far.astype(F32)).astype(BF), 2)
    return parts[0].astype(F32) + swap(parts[1], 1).astype(F32) + chip.astype(F32)


def shards(n, tokens, cotangent, lengths, order, mask, in_weight, out_weight, conv_weight, conv_bias, dt_bias,
           a_log, skip_gain, gain_outer, gain_inner):
    r, s = lax.axis_index("rep"), lax.axis_index("shard")
    ring = n == 8
    inner_width = TILES * LANES
    perm, place = relative(s, n)
    keep = mask.astype(F32)[:, None]
    catalog = jnp.arange(lengths.shape[0], dtype=jnp.int32)
    picked = jnp.sum(jnp.where(order[:, None] == catalog[None, :], lengths[None, :], 0), axis=1)
    bounds = jnp.stack([picked[0], picked[0] + picked[1]])[None, :]
    bounds = jnp.concatenate([bounds, swap(bounds, 1), swap(bounds, 2), swap(bounds, 3)], 0)

    turned = in_weight.T
    me = r[None]
    rest = pick_rest(me, turned)
    normed = norm_rows(perm, tokens, gain_outer[None, :])
    gout = (cotangent.astype(F32) * keep).astype(BF)

    def own_lanes(v, width):
        v = lax.dynamic_index_in_dim(v.reshape(v.shape[:-1] + (TILES, 4, width)), r, v.ndim, False)
        return v.reshape(v.shape[:-2] + (TILES * width,))

    heads = H // 4
    skip = jnp.broadcast_to(skip_gain[:, None], (H, P_SIZE)).reshape(1, DIN)
    rows8 = jnp.concatenate(
        [conv_weight, conv_bias[None], jnp.pad(skip, ((0, 0), (0, 2 * N))), jnp.zeros((2, CONVCH), F32)], 0
    )
    cw = jnp.concatenate([own_lanes(rows8[:, :DIN], LANES), rows8[:, DIN:]], 1)
    hp = jnp.stack([own_lanes(dt_bias, 2), own_lanes(-jnp.exp(a_log), 2)])
    hp = jnp.pad(hp, ((0, 6), (0, LANES - heads)))
    gain = own_lanes(gain_inner, LANES)[None, :]

    if ring:
        pieces = []
        steps = ring_pieces(rest, pieces)
        sent = next(steps)
        core, chip = swap(normed, 1), swap(normed, 2)
        two = pick_two(me, turned, out_weight)
        *sent, core, two = tie(*sent, core, two)
        sent = steps.send(sent)
        *sent, gout = tie(*sent, gout)
        sent = steps.send(sent)
        sent = steps.send(tie(*sent))
        near = jnp.concatenate(pieces[:7] + [jnp.zeros_like(rest)], 1)
        *sent, chip, two, near = tie(*sent, chip, two, near)
        steps.send(sent)
        rest_far = pieces[7]

        pieces = []
        steps = ring_pieces(two, pieces)
        sent = next(steps)
        far, gchip, gcore = swap(chip, 1), swap(gout, 2), swap(gout, 1)
        w_rest = lax.dynamic_update_slice(near, rest_far, (0, 7 * rest.shape[1]))
        all_normed = jnp.concatenate([normed, core, chip, far], 0)
        all_normed, w_rest = tie(all_normed, w_rest)
        proj = mm_nt(all_normed, w_rest).astype(BF)
        *sent, proj = tie(*sent, proj)
        sent = steps.send(sent)
        scan = scan_forward(bounds, proj, cw, hp, 0, 2)
        *sent, scan, gchip, gcore = tie(*sent, scan, gchip, gcore)
        sent = steps.send(sent)
        gfar = swap(gchip, 1)
        scan = scan_forward(bounds, proj, cw, hp, 2, 2, scan)
        *sent, scan, gfar = tie(*sent, scan, gfar)
        sent = steps.send(sent)
        all_gout = jnp.concatenate([gout, gcore, gchip, gfar], 0)
        *sent, all_gout = tie(*sent, all_gout)
        steps.send(sent)
        ginner, w_out, w_two = inner_gradient(perm, all_gout, pieces)
    else:
        everyone = lambda x: [x, swap(x, 1), swap(x, 2), swap(x, 3)]
        w_rest = lax.all_gather(rest, "shard", axis=1, tiled=True)
        w_two = lax.all_gather(pick_gate(me, turned), "shard", axis=1, tiled=True)
        w_out = lax.all_gather(out_weight.astype(BF), "shard", axis=0, tiled=True)
        w_out = lax.dynamic_index_in_dim(w_out.reshape(TILES, 4, LANES, D), r, 1, False).reshape(inner_width, D)
        all_normed = jnp.concatenate(everyone(normed), 0)
        all_gout = jnp.concatenate(everyone(gout), 0)
        proj = mm_nt(all_normed, w_rest).astype(BF)
        scan = scan_forward(bounds, proj, cw, hp, 0, 4)
        ginner = mm_nt(all_gout, w_out).astype(BF)

    gate, sums = gate_stats(all_normed, w_two, scan, ginner, gain)
    there = [swap(sums, d) for d in (1, 2, 3)]
    sums = jnp.stack([sums[k] + there[0][k ^ 1] + there[1][k ^ 2] + there[2][k ^ 3] for k in range(4)])
    inner, dgate, dscan, dgain = gate_both(sums, scan, gate, ginner, gain)

    def columns_of(x):
        return [x[:, k * 256 : (k + 1) * 256] for k in range(x.shape[1] // 256)]

    at_r = (jnp.arange(4) == r).astype(F32)
    sizes = [4 * CONVCH, CONVCH, H, H, H, D, DIN]

    def all_lanes(v, width):
        v = v.reshape(v.shape[:-1] + (TILES, 1, width)) * at_r[:, None]
        return v.reshape(v.shape[:-3] + (TILES * 4 * width,))

    def small_vector(dcw, dhp, dgo, dgain):
        wide = jnp.concatenate([all_lanes(dcw[:5, :inner_width], LANES), dcw[:5, inner_width:]], 1)
        dskip = jnp.sum(dcw[5, :inner_width].reshape(heads, P_SIZE), axis=1)
        dgo = dgo[0].reshape(8, D // 8)[place].reshape(D) / gain_outer
        parts = [
            wide.reshape(-1),
            all_lanes(dhp[0, :heads], 2),
            all_lanes(dhp[1, :heads], 2),
            all_lanes(dskip, 2),
            dgo,
            all_lanes(dgain[0], LANES),
        ]
        flat = jnp.concatenate(parts)
        return jnp.pad(flat, (0, -flat.shape[0] % 1024)).reshape(-1, LANES)

    width = in_weight.shape[1]
    final = functools.partial(normed_gradient, w_rest=w_rest, dgate=dgate, w_two=w_two, normed=all_normed)
    if ring:
        outs = columns_of(out_terms(perm, inner, all_gout))
        (dgate, _) = tie(dgate, outs[7])
        terms8 = columns_of(lax.dot_general(dgate, all_normed, TN, preferred_element_type=F32).astype(BF))
        terms8 = [jnp.concatenate(p, 0) for p in zip(terms8, outs)]
        steps = ring_sum()
        next(steps)
        sent, inner, dscan = launch(steps, terms8[7], inner, dscan)
        back = functools.partial(scan_backward, bounds, proj, cw, hp, scan)
        branch = mm(inner, w_out).astype(BF)
        *sent, branch = tie(*sent, branch)
        b0, b1, b2, b3 = blocks_of(branch)
        sent, dscan, b3 = launch(steps, (*sent, terms8[:7]), dscan, b3)
        far = swap(b3, 1)
        gproj, dcw, dhp = back(dscan, 2, 2)
        *sent, gproj, far = tie(*sent, gproj, far)
        sent, gproj, chip = launch(steps, sent, gproj, add16(b2, far))
        core, chip = swap(b1, 1), swap(chip, 2)
        late, dgo = final(gproj, first=2, count=2)
        *sent, gproj, core, late = tie(*sent, gproj, core, late)
        sent, gproj, late = launch(steps, sent, gproj, late)
        far = swap(late[TOK:], 1)
        gproj, d, e = back(dscan, 0, 1, gproj)
        dcw, dhp = dcw + d, dhp + e
        gproj, far = tie(gproj, far)
        gproj, total = tie(gproj, add16(late[:TOK], far))
        gproj, d, e = back(dscan, 1, 1, gproj)
        dcw, dhp = dcw + d, dhp + e
        *sent, gproj = tie(*sent, gproj)
        share, gproj = tie(steps.send(sent), gproj)
        upper = swap(total[: TOK // 2], 2)

        far, turned_proj = across_rows(gproj, all_normed, 7, 1, True)
        steps = ring_sum()
        next(steps)
        sent, turned_proj = launch(steps, far[0], turned_proj)
        gates = [share, swap(share, 1)]
        seven = across_rows(turned_proj, all_normed, 0, 7, False)
        *sent, seven, gproj, upper, lower, share, chip = tie(
            *sent, seven, gproj, upper, total[TOK // 2 :], share, chip
        )
        branch = (b0, core, chip)
        sent, gproj, lower = launch(steps, (*sent, list(seven)), gproj, lower)
        lower = swap(lower, 2)
        early, d = final(gproj, first=0, count=2)
        dgo = dgo + d
        *sent, early, lower, share = tie(*sent, early, lower, share)
        sent, early, share, dgo = launch(steps, sent, early, share, dgo)
        gates.append(swap(share, 2))
        core = swap(early[TOK:], 1)
        bits = [1 << k for k in range(n.bit_length() - 1)]
        flip = lambda v, d: v + lax.ppermute(v, "shard", [(i, i ^ d) for i in range(n)])
        layer_out = (keep * (tokens.astype(F32) + sum(b.astype(F32) for b in branch))).astype(BF)
        *sent, core, layer_out, dgo = tie(*sent, core, layer_out, dgo)
        sent, core, dgo = launch(steps, sent, core, dgo)
        small = small_vector(dcw, dhp, dgo, dgain)
        small = small + swap(small, 1)
        small = small + swap(small, 2)
        parts = [early[:TOK], core, jnp.concatenate([upper, lower], 0)]
        grad_tokens = last_rows(perm, tokens, cotangent, keep, gain_outer[None, :], parts)
        *sent, gates[2], grad_tokens, small = tie(*sent, gates[2], grad_tokens, small)
        share, small, gates[2] = tie(steps.send(sent), small, gates[2])
        rests = [share, swap(share, 1), swap(share, 2)]
        gates.append(swap(gates[2], 1))
        for d in bits:
            small = flip(small, d)
        grad_in, grad_out_weight = first_join(me, gates, width)
        rests[2], grad_in = tie(rests[2], grad_in)
        rests.append(swap(rests[2], 1))
    else:
        side = lambda x: jnp.concatenate(list(x), 1)
        rows_sum = lambda x, axis: lax.psum_scatter(
            x.astype(F32), "shard", scatter_dimension=axis, tiled=True
        ).astype(BF)
        branch = sum_rep(blocks_of(mm(inner, w_out).astype(BF)))
        gproj, dcw, dhp = scan_backward(bounds, proj, cw, hp, scan, dscan, 0, 4)
        layer_out = (keep * (tokens.astype(F32) + branch.astype(F32))).astype(BF)
        gnormed, dgo = final(gproj, first=0, count=4)
        total = sum_rep(blocks_of(gnormed)).astype(BF)
        grad_tokens = last_rows(
            perm, tokens, cotangent, keep, gain_outer[None, :], [total, jnp.zeros_like(total), jnp.zeros_like(total)]
        )
        grad_out = lax.dot_general(inner, all_gout, TN, preferred_element_type=F32)
        spread = grad_out.reshape(TILES, 1, LANES, D).astype(F32) * (jnp.arange(4)[None, :, None, None] == r)
        spread = lax.psum_scatter(spread.reshape(DIN, D), "shard", scatter_dimension=0, tiled=True)
        grad_out_weight = lax.psum(spread, "rep")
        gates = everyone(rows_sum(side(across_rows(dgate, all_normed, 0, 8, True)[0]), 1))
        rests = everyone(rows_sum(side(across_rows(gproj, all_normed, 0, 8, True)[0]), 1))
        grad_in, _ = first_join(me, gates, width)
        small = lax.psum(small_vector(dcw, dhp, dgo, dgain), ("rep", "shard"))
    grad_in_weight = last_join(me, rests, grad_in).T

    small = small.reshape(-1)
    ends = [sum(sizes[: i + 1]) for i in range(len(sizes))]
    g_cw, g_cb, g_db, g_al, g_sk, g_go, g_gi = [small[e - z : e] for e, z in zip(ends, sizes)]
    return (
        layer_out,
        grad_tokens,
        grad_in_weight,
        grad_out_weight,
        g_cw.reshape(4, CONVCH),
        g_cb,
        g_db,
        g_al,
        g_sk,
        g_go,
        g_gi,
    )


def solution(mesh):
    rows = P(("rep", "shard"), None)
    vector = P(("rep", "shard"))
    owned = P("shard", None)
    return jax.shard_map(
        functools.partial(shards, mesh.shape["shard"]),
        mesh=mesh,
        in_specs=(rows, rows, P(), vector, vector, owned, owned) + (P(),) * 7,
        out_specs=(rows, rows, owned, owned) + (P(),) * 7,
        check_vma=False,
    )
```
